1024 devices in a mesh: dp: 128 (over x, z_hi, y), mp: 8 (over z_lo, core).
Axes of the slice: x: 8, y: 8, z: 8 (z_hi: 2, z_lo: 4; z = z_hi * 4 + z_lo), core: 2. Of those that a mesh axis runs over, the one named last changes fastest.
Arguments:
- picture_tower_activations: bfloat16 [131072, 1152], P(('dp', 'mp')), may hold values from -6 to 6
- caption_tower_activations: bfloat16 [131072, 1152], P(('dp', 'mp')), may hold values from -6 to 6
- picture_mapping_kernel: bfloat16 [1152, 1152], replicated, may hold values from -0.1875 to 0.1875
- caption_mapping_kernel: bfloat16 [1152, 1152], replicated, may hold values from -0.1875 to 0.1875
- sigmoid_sharpness: float32 [1], replicated, may hold values from 5 to 20
- sigmoid_shift_term: float32 [1], replicated, may hold values from -4 to -1
Outputs:
- image_head_grad: float32 [128, 1152, 1152], P('dp', 'mp')
- text_head_grad: float32 [128, 1152, 1152], P('dp', 'mp')
The draws below stay inside these ranges and needn't reach their ends.
All inputs are finite; a program needn't handle non-finite values.
Results may differ from the reference program's by a relative error of at most 0.017.
Values may be sent and summed in bfloat16 or wider, within the bound.
No kernel may reach another device: no remote copies, remote signals or barrier semaphores. Data moves between devices by JAX's collectives and lax.ppermute only.
A program may use at most 64 MiB of HBM per device.

```python
import math
import jax
import jax.numpy as jnp
from jax import lax

D = 1152
ROWS = 128
SHIFTS = 3
BATCH = 131072
N_DP = 128
N_MP = 8


def block_levels(rng, dims, split, smallest, largest):
    def one(position, shards_of):
        steps = jax.random.uniform(jax.random.fold_in(jax.random.fold_in(rng, 6), position), (shards_of,), jnp.float32, smallest / len(split), largest / len(split))
        return jnp.repeat(jnp.exp(steps), dims[position] // shards_of).reshape((-1,) + (1,) * (len(dims) - position - 1))

    gain = one(*split[0])
    for cut in split[1:]:
        gain = gain * one(*cut)
    return gain


def noise(rng, shape, width, bound, split=(), kind=jnp.bfloat16):
    array = jax.random.normal(rng, shape, jnp.float32) * width
    if len(split) > 0:
        array = block_levels(rng, shape, split, -0.22, 0.18) * array
    return jnp.clip(array, min=-bound, max=bound).astype(kind)


def setup_inputs(seed: int = 0) -> dict:
    key_of = jax.random.split(jax.random.key(seed), 7)
    picture_tower_activations = noise(key_of[0], (BATCH, D), 1.0, 6.0, ((0, 1024),))
    caption_tower_activations = noise(key_of[1], (BATCH, D), 1.0, 6.0, ((0, 1024),))
    picture_mapping_kernel = noise(key_of[2], (D, D), D ** -0.5, 0.1875)
    caption_mapping_kernel = noise(key_of[3], (D, D), D ** -0.5, 0.1875)
    sigmoid_sharpness = jnp.clip(jnp.exp(jax.random.uniform(key_of[4], (1,), jnp.float32, math.log(5.0), math.log(20.0))), 5.0, 20.0)
    sigmoid_shift_term = jnp.clip(jax.random.uniform(key_of[5], (1,), jnp.float32, -4.0, -1.0), -4.0, -1.0)
    return dict(picture_tower_activations=picture_tower_activations, caption_tower_activations=caption_tower_activations, picture_mapping_kernel=picture_mapping_kernel, caption_mapping_kernel=caption_mapping_kernel, sigmoid_sharpness=sigmoid_sharpness, sigmoid_shift_term=sigmoid_shift_term)


epsilon = 1e-06

def project_rows(features, projection):
    x_values = jnp.dot(features, projection, preferred_element_type=jnp.float32)
    norm_rows = jnp.sqrt(lax.optimization_barrier(jnp.sum(x_values * x_values, axis=-1, keepdims=True)) + epsilon)
    return (x_values, norm_rows)

def rounded(values):
    return lax.optimization_barrier(values.astype(jnp.bfloat16)).astype(jnp.float32)

def paired_blocks(image_embedded, text_embedded, multiplier_coefficient, block_offset, positive_pairs):
    logit_matrix = multiplier_coefficient * jnp.dot(image_embedded, text_embedded.T, preferred_element_type=jnp.float32) + block_offset
    prob_values = jax.nn.sigmoid(logit_matrix)
    if positive_pairs:
        prob_values = prob_values - jnp.eye(image_embedded.shape[0], dtype=jnp.float32)
    head_weights = (prob_values / image_embedded.shape[0]).astype(jnp.bfloat16)
    image_projection = multiplier_coefficient * jnp.dot(head_weights, text_embedded, preferred_element_type=jnp.float32)
    text_projection = multiplier_coefficient * jnp.dot(head_weights.T, image_embedded, preferred_element_type=jnp.float32)
    return (image_projection, text_projection)

def reference(picture_tower_activations, caption_tower_activations, picture_mapping_kernel, caption_mapping_kernel, sigmoid_sharpness, sigmoid_shift_term):
    multiplier_coefficient = sigmoid_sharpness[0]
    block_offset = sigmoid_shift_term[0]
    block_count = N_DP * N_MP
    grid_shape = (N_DP, N_MP, ROWS, D)
    image_blocks = picture_tower_activations.reshape(block_count, ROWS, D)
    text_blocks = caption_tower_activations.reshape(block_count, ROWS, D)

    def unit_maker(projection):

        def unit_block(features):
            x_values, norm_rows = project_rows(features, projection)
            return (x_values / norm_rows).astype(jnp.bfloat16)
        return unit_block
    image_embedded = lax.map(unit_maker(picture_mapping_kernel), image_blocks)
    text_embedded = lax.map(unit_maker(caption_mapping_kernel), text_blocks)
    image_embedding_grad = jnp.zeros((block_count, ROWS, D), jnp.float32)
    text_embedding_grad = jnp.zeros((block_count, ROWS, D), jnp.float32)
    for shift_step in range(SHIFTS + 1):
        received_block = jnp.roll(text_embedded.reshape(grid_shape), shift_step, axis=0).reshape(block_count, ROWS, D)
        positive_pairs = shift_step == 0
        image_projection, text_projection = lax.map(lambda block_list: paired_blocks(block_list[0], block_list[1], multiplier_coefficient, block_offset, positive_pairs), (image_embedded, received_block))
        if shift_step > 0:
            image_projection = rounded(image_projection)
            text_projection = rounded(text_projection)
        image_embedding_grad = image_embedding_grad + image_projection
        text_embedding_grad = text_embedding_grad + jnp.roll(text_projection.reshape(grid_shape), -shift_step, axis=0).reshape(block_count, ROWS, D)

    def head_grad(all_features, all_dz, projection):

        def block_term(block_list):
            features, dz_block = block_list
            x_values, norm_rows = project_rows(features, projection)
            unit_rows = x_values / norm_rows
            dx_block = ((dz_block - unit_rows * lax.optimization_barrier(jnp.sum(unit_rows * dz_block, axis=-1, keepdims=True))) / norm_rows).astype(jnp.bfloat16)
            return rounded(jnp.dot(features.T, dx_block, preferred_element_type=jnp.float32))

        def group_sum(group_blocks):

            def accumulate(running, block_list):
                return (running + block_term(block_list), None)
            running, unused = lax.scan(accumulate, jnp.zeros((D, D), jnp.float32), group_blocks)
            return running
        return lax.map(group_sum, (all_features.reshape(grid_shape), all_dz.reshape(grid_shape)))
    image_grad = head_grad(picture_tower_activations, image_embedding_grad, picture_mapping_kernel)
    text_grad = head_grad(caption_tower_activations, text_embedding_grad, caption_mapping_kernel)
    return (image_grad, text_grad)
```

```python
import functools

import jax
import jax.numpy as jnp
from jax import lax
from jax.experimental import pallas as pl
from jax.experimental.pallas import tpu as pltpu
from jax.sharding import Mesh, PartitionSpec as P

NAMES = ("x", "zh", "y", "zl", "c")
NX, NZH, NY, NZL, NC = SIZES = (8, 2, 8, 4, 2)
ROWS = 128
D = 1152
CHIP = 288
CORE = 144
LEFT = 640
EPS = 1e-06
BF = jnp.bfloat16
F32 = jnp.float32
VMEM = pl.BlockSpec(memory_space=pltpu.VMEM)
SMEM = pl.BlockSpec(memory_space=pltpu.SMEM)
ANY = pl.BlockSpec(memory_space=pl.ANY)
PARAMS = pltpu.CompilerParams(vmem_limit_bytes=32 * 1024 * 1024)


def index_of(x, zh, y, zl, c):
    return (((x * NZH + zh) * NY + y) * NZL + zl) * NC + c


def pairs_of(rule):
    found = []
    for x in range(NX):
        for zh in range(NZH):
            for y in range(NY):
                for zl in range(NZL):
                    for c in range(NC):
                        target = rule(x, zh, y, zl, c)
                        if target is not None:
                            found.append((index_of(x, zh, y, zl, c), index_of(*target)))
    return found


def send(value, rule):
    return lax.ppermute(value, NAMES, pairs_of(rule))


def other_core(x, zh, y, zl, c):
    return (x, zh, y, zl, 1 - c)


def first_hop(x, zh, y, zl, c):
    if c == 1:
        return (x, zh, y + 1, zl, 0) if y < 7 else None
    return (x, zh, y - 1, zl, 1) if y > 0 else None


def second_hop(x, zh, y, zl, c):
    if not 1 <= y <= 6:
        return None
    return (x, zh, y + 1 if c == 0 else y - 1, zl, c)


def third_hop(x, zh, y, zl, c):
    if c == 0:
        return (x, zh, y + 1, zl, 0) if y < 7 else None
    return (x, zh, y - 1, zl, 1) if y > 0 else None


def crossing(x, zh, y, zl, c):
    if c == 1 and y >= 5:
        column = {7: 1, 6: 0, 5: 2}[y]
        return (x, 1, column, zl, 0) if zh == 0 else ((x + 1) % NX, 0, column, zl, 0)
    if c == 0 and y <= 2:
        column = {0: 6, 1: 7, 2: 5}[y]
        return (x, 0, column, zl, 1) if zh == 1 else ((x - 1) % NX, 1, column, zl, 1)
    return None


def from_second(x, zh, y, zl, c):
    if c == 0 and y == 1:
        return (x, zh, 0, zl, 0)
    if c == 1 and y == 6:
        return (x, zh, 7, zl, 1)
    return None


def from_third(x, zh, y, zl, c):
    if c == 0 and y == 2:
        return (x, zh, 0, zl, 0)
    if c == 1 and y == 5:
        return (x, zh, 7, zl, 1)
    return None


def inward(x, zh, y, zl, c):
    return {0: (x, zh, y, 1, c), 3: (x, zh, y, 2, c)}.get(zl)


def middle(x, zh, y, zl, c):
    return {1: (x, zh, y, 2, c), 2: (x, zh, y, 1, c)}.get(zl)


def outward(x, zh, y, zl, c):
    return {1: (x, zh, y, 0, c), 2: (x, zh, y, 3, c)}.get(zl)


def outward_cross(x, zh, y, zl, c):
    return {1: (x, zh, y, 0, 1 - c), 2: (x, zh, y, 3, 1 - c)}.get(zl)


def normalised(x):
    total = jnp.sum(x * x, axis=-1, keepdims=True)
    rn = 1.0 / jnp.sqrt(total + EPS)
    u = x * rn
    return u, jnp.broadcast_to(rn, (ROWS, 128))


def project_own_kernel(
    flags, pictures, captions, wp, wc, w_ref, z_ref, u_ref, rn_ref, f_ref, sems
):
    c = flags[0]
    parts = 3
    width = D // parts

    def fetch(feats, head):
        pltpu.make_async_copy(feats, f_ref, sems.at[parts]).start()
        for j in range(parts):
            cols = pl.ds(j * width, width)
            pltpu.make_async_copy(head.at[:, cols], w_ref.at[:, cols], sems.at[j]).start()

    @pl.when(c == 0)
    def _():
        fetch(pictures, wp)

    @pl.when(c == 1)
    def _():
        fetch(captions, wc)

    pltpu.make_async_copy(pictures, f_ref, sems.at[parts]).wait()
    for j in range(parts):
        cols = pl.ds(j * width, width)
        pltpu.make_async_copy(wp.at[:, cols], w_ref.at[:, cols], sems.at[j]).wait()
        u_ref[:, cols] = jnp.dot(f_ref[...], w_ref[:, cols], preferred_element_type=F32)
    u, rn_ref[...] = normalised(u_ref[...])
    u_ref[...] = u
    z_ref[...] = u.astype(BF)


def project_own(flags, pictures, captions, wp, wc):
    return pl.pallas_call(
        project_own_kernel,
        name="project_own",
        out_shape=(
            jax.ShapeDtypeStruct((D, D), BF),
            jax.ShapeDtypeStruct((ROWS, D), BF),
            jax.ShapeDtypeStruct((ROWS, D), F32),
            jax.ShapeDtypeStruct((ROWS, 128), F32),
        ),
        in_specs=[SMEM, ANY, ANY, ANY, ANY],
        out_specs=(VMEM,) * 4,
        scratch_shapes=[pltpu.VMEM((ROWS, D), BF), pltpu.SemaphoreType.DMA((4,))],
        compiler_params=PARAMS,
        cost_estimate=pl.CostEstimate(
            flops=2 * ROWS * D * D, bytes_accessed=4 * D * D + 8 * ROWS * D, transcendentals=0
        ),
    )(flags, pictures, captions, wp, wc)


def project_other_kernel(recv, w_ref, z_own, z_ref, u_ref, rn_ref):
    z_ref[:ROWS] = z_own[...]
    u, rn_ref[...] = normalised(
        jnp.dot(recv[...], w_ref[...], preferred_element_type=F32)
    )
    u_ref[...] = u
    z_ref[ROWS:] = u.astype(BF)


def project_other(recv, w, z_own):
    return pl.pallas_call(
        project_other_kernel,
        name="project_other",
        out_shape=(
            jax.ShapeDtypeStruct((2 * ROWS, D), BF),
            jax.ShapeDtypeStruct((ROWS, D), F32),
            jax.ShapeDtypeStruct((ROWS, 128), F32),
        ),
        in_specs=[VMEM] * 3,
        out_specs=(VMEM,) * 3,
        compiler_params=PARAMS,
        cost_estimate=pl.CostEstimate(
            flops=2 * ROWS * D * D, bytes_accessed=2 * D * D + 8 * ROWS * D, transcendentals=0
        ),
    )(recv, w, z_own)


def turn_kernel(flags, pictures, captions, recv, after, ft_ref, turned, f_ref, sem):
    del after
    mirror = flags[3]

    @pl.when(flags[0] == 0)
    def _():
        pltpu.make_async_copy(pictures, f_ref, sem).start()

    @pl.when(flags[0] == 1)
    def _():
        pltpu.make_async_copy(captions, f_ref, sem).start()

    turned[:, ROWS:] = recv[...].T
    pltpu.make_async_copy(pictures, f_ref, sem).wait()
    turned[:, :ROWS] = f_ref[...].T
    for j in range(4):
        start = pl.multiple_of(jnp.where(mirror == 1, 3 - j, j) * CHIP, CHIP)
        ft_ref[j * CHIP : (j + 1) * CHIP] = turned[pl.ds(start, CHIP)]


def turn(flags, pictures, captions, recv, after):
    return pl.pallas_call(
        turn_kernel,
        name="turn",
        out_shape=jax.ShapeDtypeStruct((D, 2 * ROWS), BF),
        in_specs=[SMEM, ANY, ANY, VMEM, ANY],
        out_specs=VMEM,
        scratch_shapes=[
            pltpu.VMEM((D, 2 * ROWS), BF),
            pltpu.VMEM((ROWS, D), BF),
            pltpu.SemaphoreType.DMA(()),
        ],
        compiler_params=PARAMS,
        cost_estimate=pl.CostEstimate(
            flops=0, bytes_accessed=8 * ROWS * D, transcendentals=0
        ),
    )(flags, pictures, captions, recv, after)


def pairs_kernel(
    flags, scale, z_ref, u_own, u_other, rn_own, rn_other,
    here, one, two, three, cross, second, third, early_end, early_mid,
    dx_ref, others, sems,
):
    del early_end, early_mid

    def fetch(source, s):
        for b in range(2):
            pltpu.make_async_copy(
                source.at[pl.ds((1 - b) * ROWS, ROWS)],
                others.at[b, pl.ds(s * ROWS, ROWS)],
                sems.at[2 * s + b],
            ).start()

    fetch(here, 0)

    @pl.when(flags[1] == 0)
    def _():
        fetch(one, 1)

    @pl.when(flags[1] == 1)
    def _():
        fetch(second, 1)

    @pl.when(flags[2] == 0)
    def _():
        fetch(two, 2)

    @pl.when(flags[2] == 1)
    def _():
        fetch(cross, 2)

    @pl.when(flags[1] == 0)
    def _():
        fetch(three, 3)

    @pl.when(flags[1] == 1)
    def _():
        fetch(third, 3)

    t = scale[0]
    bias = scale[1]
    for s in range(4):
        for b in range(2):
            pltpu.make_async_copy(
                here.at[pl.ds(0, ROWS)],
                others.at[b, pl.ds(s * ROWS, ROWS)],
                sems.at[2 * s + b],
            ).wait()
    row = lax.broadcasted_iota(jnp.int32, (ROWS, 4 * ROWS), 0)
    col = lax.broadcasted_iota(jnp.int32, (ROWS, 4 * ROWS), 1)
    for b in range(2):
        mine = z_ref[b * ROWS : (b + 1) * ROWS]
        logits = t * lax.dot_general(
            mine, others[b], (((1,), (1,)), ((), ())), preferred_element_type=F32
        ) + bias
        prob = jax.nn.sigmoid(logits) - jnp.where(row == col, 1.0, 0.0)
        weight = (prob * (1.0 / ROWS)).astype(BF)
        dz = t * jnp.dot(weight, others[b], preferred_element_type=F32)
        u = (u_own, u_other)[b][...]
        rn = (rn_own, rn_other)[b][:, :1]
        inner = jnp.sum(u * dz, axis=-1, keepdims=True)
        dx_ref[b * ROWS : (b + 1) * ROWS] = ((dz - u * inner) * rn).astype(BF)


def pairs(flags, scale, z, *rest):
    rows = 2 * ROWS
    return pl.pallas_call(
        pairs_kernel,
        name="pairs",
        out_shape=jax.ShapeDtypeStruct((rows, D), BF),
        in_specs=[SMEM, SMEM] + [VMEM] * 5 + [ANY] * 9,
        out_specs=VMEM,
        scratch_shapes=[
            pltpu.VMEM((2, 4 * ROWS, D), BF),
            pltpu.SemaphoreType.DMA((8,)),
        ],
        compiler_params=PARAMS,
        cost_estimate=pl.CostEstimate(
            flops=16 * rows * ROWS * D, bytes_accessed=14 * rows * D, transcendentals=rows * 512
        ),
    )(flags, scale, z, *rest)


def near_kernel(ft, dx, feats_end, dx_end, feats_mid, dx_mid, inner_ref, outer_ref):
    dx_own = dx[...]
    dx_other = dx_mid[...]
    inner_ref[...] = (
        jnp.dot(ft[CHIP : 2 * CHIP], dx_own, preferred_element_type=F32)
        + jnp.dot(feats_end[:CHIP], dx_end[...], preferred_element_type=F32)
        + jnp.dot(feats_mid[:CHIP], dx_other, preferred_element_type=F32)
    )
    outer_ref[...] = jnp.dot(ft[:CHIP], dx_own, preferred_element_type=F32) + jnp.dot(
        feats_mid[CHIP:], dx_other, preferred_element_type=F32
    )


def near(ft, dx, feats_end, dx_end, feats_mid, dx_mid):
    return pl.pallas_call(
        near_kernel,
        name="near",
        out_shape=(
            jax.ShapeDtypeStruct((CHIP, D), F32),
            jax.ShapeDtypeStruct((CHIP, D), F32),
        ),
        in_specs=[VMEM] * 6,
        out_specs=(VMEM, VMEM),
        compiler_params=PARAMS,
        cost_estimate=pl.CostEstimate(
            flops=20 * CHIP * ROWS * D, bytes_accessed=14 * CHIP * D, transcendentals=0
        ),
    )(ft, dx, feats_end, dx_end, feats_mid, dx_mid)


def far_kernel(first, flags, inner_ref, outer_ref, feats, dx, *refs):
    keep, swap, same, crossed, total, part = refs[-6:]
    c = flags[0]
    cols = slice(0, LEFT) if first else slice(LEFT, D)
    dx_far = dx[...]
    part[...] = outer_ref[:, cols] + jnp.dot(
        feats[CHIP:], dx_far, preferred_element_type=F32
    )
    total[...] = inner_ref[:, cols] + jnp.dot(
        feats[:CHIP], dx_far, preferred_element_type=F32
    )
    mine = pl.ds(pl.multiple_of(c * CORE, CORE), CORE)
    theirs = pl.ds(pl.multiple_of((1 - c) * CORE, CORE), CORE)
    same[...] = part[mine].astype(BF)
    crossed[...] = part[theirs].astype(BF)
    if not first:
        keep[:, :LEFT] = refs[0][...]
        swap[:, :LEFT] = refs[1][...]
    into = slice(0, LEFT) if first else slice(LEFT, D)

    @pl.when(flags[4] == 1)
    def _():
        keep[:, into] = total[mine]
        swap[:, into] = total[theirs].astype(BF)

    @pl.when(flags[4] == 0)
    def _():
        keep[:, into] = part[mine]
        swap[:, into] = part[theirs].astype(BF)


def far(flags, inner, outer, feats, dx, *earlier):
    first = not earlier
    cols = LEFT if first else D - LEFT
    kept = LEFT if first else D
    return pl.pallas_call(
        functools.partial(far_kernel, first),
        name="far_left" if first else "far_right",
        out_shape=(
            jax.ShapeDtypeStruct((CORE, kept), F32),
            jax.ShapeDtypeStruct((CORE, kept), BF),
            jax.ShapeDtypeStruct((CORE, cols), BF),
            jax.ShapeDtypeStruct((CORE, cols), BF),
        ),
        in_specs=[SMEM] + [VMEM] * (4 + len(earlier)),
        out_specs=(VMEM,) * 4,
        scratch_shapes=[pltpu.VMEM((CHIP, cols), F32), pltpu.VMEM((CHIP, cols), F32)],
        compiler_params=PARAMS,
        cost_estimate=pl.CostEstimate(
            flops=8 * CHIP * ROWS * cols, bytes_accessed=14 * CHIP * cols, transcendentals=0
        ),
    )(flags, inner, outer, feats, dx, *earlier)


def finish_kernel(
    flags, keep, swap, same_left, crossed_left, same_right, crossed_right, image_ref, text_ref
):
    def put(own_ref, other_ref):
        for cols, same, crossed in (
            (slice(0, LEFT), same_left, crossed_left),
            (slice(LEFT, D), same_right, crossed_right),
        ):
            own_ref[0, :, cols] = keep[:, cols] + same[...].astype(F32)
            other_ref[0, :, cols] = swap[:, cols].astype(F32) + crossed[...].astype(F32)

    @pl.when(flags[0] == 0)
    def _():
        put(image_ref, text_ref)

    @pl.when(flags[0] == 1)
    def _():
        put(text_ref, image_ref)


def finish(flags, *parts):
    shape = jax.ShapeDtypeStruct((1, CORE, D), F32)
    return pl.pallas_call(
        finish_kernel,
        name="finish",
        out_shape=(shape, shape),
        in_specs=[SMEM] + [VMEM] * 6,
        out_specs=(VMEM, VMEM),
        compiler_params=PARAMS,
        cost_estimate=pl.CostEstimate(
            flops=4 * CORE * D, bytes_accessed=18 * CORE * D, transcendentals=0
        ),
    )(flags, *parts)


def on_device(pictures, captions, picture_head, caption_head, sharpness, shift_term):
    c = lax.axis_index("c")
    y = lax.axis_index("y")
    zl = lax.axis_index("zl")
    yy = jnp.where(c == 0, y, 7 - y)
    flags = jnp.stack(
        [c, yy == 0, yy <= 1, zl >= 2, (zl == 1) | (zl == 2)]
    ).astype(jnp.int32)
    scale = jnp.concatenate([sharpness, shift_term])

    received = send(jnp.where(c == 0, captions, pictures), other_core)
    head, z_own, u_own, rn_own = project_own(
        flags, pictures, captions, picture_head, caption_head
    )
    z, u_other, rn_other = project_other(received, head, z_own)

    cross = send(z, crossing)
    one = send(z, first_hop)
    here = send(z, other_core)
    two = send(one, second_hop)
    three = send(jnp.where(yy <= 1, cross, two), third_hop)
    second = send(cross, from_second)
    third = send(cross, from_third)
    ft = turn(flags, pictures, captions, received, two)
    ft_end = send(ft[CHIP:], inward)
    ft_mid = send(ft[2 * CHIP :], middle)
    ft_far = send(ft_end[CHIP:], middle)
    dx = pairs(
        flags, scale, z, u_own, u_other, rn_own, rn_other,
        here, one, two, three, cross, second, third, ft_end, ft_mid,
    )

    dx_end = send(dx, inward)
    dx_mid = send(dx, middle)
    far_left = send(dx_end[:, :LEFT], middle)
    far_right = send(dx_end[:, LEFT:], middle)
    inner, outer = near(ft, dx, ft_end, dx_end, ft_mid, dx_mid)
    keep, swap, same_left, crossed_left = far(flags, inner, outer, ft_far, far_left)
    crossed_left = send(crossed_left, outward_cross)
    same_left = send(same_left, outward)
    keep, swap, same_right, crossed_right = far(
        flags, inner, outer, ft_far, far_right, keep, swap
    )
    crossed_right = send(crossed_right, outward_cross)
    same_right = send(same_right, outward)
    swap = send(swap, other_core)
    return finish(flags, keep, swap, same_left, crossed_left, same_right, crossed_right)


def solution(mesh):
    physical = Mesh(mesh.devices.reshape(SIZES), NAMES)
    rows = P(NAMES, None)
    grad = P(("x", "zh", "y"), ("zl", "c"), None)
    return jax.shard_map(
        on_device,
        mesh=physical,
        in_specs=(rows, rows, P(), P(), P(), P()),
        out_specs=(grad, grad),
        check_vma=False,
    )
```

```python
import jax
import jax.numpy as jnp
from jax import lax
from jax.experimental import pallas as pl
from jax.experimental.pallas import tpu as pltpu
from jax.sharding import Mesh, PartitionSpec as P

NAMES = ("x", "zh", "y", "zl", "c")
NX, NZH, NY, NZL, NC = SIZES = (8, 2, 8, 4, 2)
ROWS = 128
D = 1152
CHIP = 288
CORE = 144
EPS = 1e-06
BF = jnp.bfloat16
F32 = jnp.float32
PROJECT_LIMIT = 58
VMEM = pl.BlockSpec(memory_space=pltpu.VMEM)
SMEM = pl.BlockSpec(memory_space=pltpu.SMEM)
ANY = pl.BlockSpec(memory_space=pl.ANY)
HBM = pl.BlockSpec(memory_space=pltpu.HBM)
PARAMS = pltpu.CompilerParams(vmem_limit_bytes=32 * 1024 * 1024)


def index_of(x, zh, y, zl, c):
    return (((x * NZH + zh) * NY + y) * NZL + zl) * NC + c


def pairs_of(rule):
    found = []
    for x in range(NX):
        for zh in range(NZH):
            for y in range(NY):
                for zl in range(NZL):
                    for c in range(NC):
                        target = rule(x, zh, y, zl, c)
                        if target is not None:
                            found.append((index_of(x, zh, y, zl, c), index_of(*target)))
    return found


def send(value, rule):
    return lax.ppermute(value, NAMES, pairs_of(rule))


def other_core(x, zh, y, zl, c):
    return (x, zh, y, zl, 1 - c)


def first_hop(x, zh, y, zl, c):
    if c == 1:
        return (x, zh, y + 1, zl, 0) if y < 7 else None
    return (x, zh, y - 1, zl, 1) if y > 0 else None


def second_hop(x, zh, y, zl, c):
    if not 1 <= y <= 6:
        return None
    return (x, zh, y + 1 if c == 0 else y - 1, zl, c)


def third_hop(x, zh, y, zl, c):
    if c == 0:
        return (x, zh, y + 1, zl, 0) if y < 7 else None
    return (x, zh, y - 1, zl, 1) if y > 0 else None


def above(x, zh, column):
    return (x, 1, column) if zh == 0 else ((x + 1) % NX, 0, column)


def below(x, zh, column):
    return (x, 0, column) if zh == 1 else ((x - 1) % NX, 1, column)


def first_crossing(x, zh, y, zl, c):
    if c == 1 and y == 7:
        return (*above(x, zh, 1), zl, 0)
    if c == 0 and y == 0:
        return (*below(x, zh, 6), zl, 1)
    return None


def later_crossing(x, zh, y, zl, c):
    if c == 0 and y == 7:
        return (*above(x, zh, 0), zl, 0)
    if c == 1 and y == 0:
        return (*below(x, zh, 7), zl, 1)
    return None


def from_second(x, zh, y, zl, c):
    if c == 0 and y == 1:
        return (x, zh, 0, zl, 0)
    if c == 1 and y == 6:
        return (x, zh, 7, zl, 1)
    return None


def inward(x, zh, y, zl, c):
    return {0: (x, zh, y, 1, c), 3: (x, zh, y, 2, c)}.get(zl)


def middle(x, zh, y, zl, c):
    return {1: (x, zh, y, 2, c), 2: (x, zh, y, 1, c)}.get(zl)


def outward(x, zh, y, zl, c):
    return {1: (x, zh, y, 0, c), 2: (x, zh, y, 3, c)}.get(zl)


def outward_cross(x, zh, y, zl, c):
    return {1: (x, zh, y, 0, 1 - c), 2: (x, zh, y, 3, 1 - c)}.get(zl)


def project_kernel(
    flags, pictures, captions, recv, wp, wc, z_ref, u_ref, rn_ref, f_ref, w_ref, sems
):
    c = flags[0]
    parts = 3
    width = D // parts

    def fetch(feats, head):
        pltpu.make_async_copy(feats, f_ref.at[pl.ds(0, ROWS)], sems.at[parts]).start()
        for j in range(parts):
            cols = pl.ds(j * width, width)
            pltpu.make_async_copy(head.at[:, cols], w_ref.at[j], sems.at[j]).start()

    @pl.when(c == 0)
    def _():
        fetch(pictures, wp)

    @pl.when(c == 1)
    def _():
        fetch(captions, wc)

    f_ref[ROWS:] = recv[...]
    pltpu.make_async_copy(pictures, f_ref.at[pl.ds(0, ROWS)], sems.at[parts]).wait()
    total = jnp.zeros((2 * ROWS, 1), F32)
    for j in range(parts):
        cols = pl.ds(j * width, width)
        pltpu.make_async_copy(wp.at[:, cols], w_ref.at[j], sems.at[j]).wait()
        x = jnp.dot(f_ref[...], w_ref[j], preferred_element_type=F32)
        u_ref[:, cols] = x
        total = total + jnp.sum(x * x, axis=-1, keepdims=True)
    rn = 1.0 / jnp.sqrt(total + EPS)
    rn_ref[...] = jnp.broadcast_to(rn, (2 * ROWS, 128))
    u = u_ref[...] * rn
    u_ref[...] = u
    z_ref[...] = u.astype(BF)


def project(flags, pictures, captions, recv, wp, wc):
    rows = 2 * ROWS
    return pl.pallas_call(
        project_kernel,
        name="project",
        out_shape=(
            jax.ShapeDtypeStruct((rows, D), BF),
            jax.ShapeDtypeStruct((rows, D), F32),
            jax.ShapeDtypeStruct((rows, 128), F32),
        ),
        in_specs=[SMEM, HBM, HBM, VMEM, HBM, HBM],
        out_specs=(VMEM,) * 3,
        scratch_shapes=[
            pltpu.VMEM((rows, D), BF),
            pltpu.VMEM((3, D, D // 3), BF),
            pltpu.SemaphoreType.DMA((4,)),
        ],
        compiler_params=pltpu.CompilerParams(vmem_limit_bytes=PROJECT_LIMIT * 1024 * 1024),
        cost_estimate=pl.CostEstimate(
            flops=2 * rows * D * D, bytes_accessed=2 * D * D + 8 * rows * D, transcendentals=0
        ),
    )(flags, pictures, captions, recv, wp, wc)


def turn_kernel(flags, pictures, captions, recv, ft_ref, turned, f_ref, sem):
    mirror = flags[3]

    @pl.when(flags[0] == 0)
    def _():
        pltpu.make_async_copy(pictures, f_ref, sem).start()

    @pl.when(flags[0] == 1)
    def _():
        pltpu.make_async_copy(captions, f_ref, sem).start()

    turned[:, ROWS:] = recv[...].T
    pltpu.make_async_copy(pictures, f_ref, sem).wait()
    turned[:, :ROWS] = f_ref[...].T
    for j in range(4):
        start = pl.multiple_of(jnp.where(mirror == 1, 3 - j, j) * CHIP, CHIP)
        ft_ref[j * CHIP : (j + 1) * CHIP] = turned[pl.ds(start, CHIP)]


def turn(flags, pictures, captions, recv):
    return pl.pallas_call(
        turn_kernel,
        name="turn",
        out_shape=jax.ShapeDtypeStruct((D, 2 * ROWS), BF),
        in_specs=[SMEM, HBM, HBM, VMEM],
        out_specs=VMEM,
        scratch_shapes=[
            pltpu.VMEM((D, 2 * ROWS), BF),
            pltpu.VMEM((ROWS, D), BF),
            pltpu.SemaphoreType.DMA(()),
        ],
        compiler_params=PARAMS,
        cost_estimate=pl.CostEstimate(
            flops=0, bytes_accessed=8 * ROWS * D, transcendentals=0
        ),
    )(flags, pictures, captions, recv)


def choose_kernel(flags, two, cross_one, cross_two, out_ref, sem):
    place = flags[1]

    @pl.when(place == 0)
    def _():
        pltpu.make_async_copy(cross_two, out_ref, sem).start()

    @pl.when(place == 1)
    def _():
        pltpu.make_async_copy(cross_one, out_ref, sem).start()

    @pl.when(place > 1)
    def _():
        pltpu.make_async_copy(two, out_ref, sem).start()

    pltpu.make_async_copy(two, out_ref, sem).wait()


def choose(flags, two, cross_one, cross_two):
    return pl.pallas_call(
        choose_kernel,
        name="choose",
        out_shape=jax.ShapeDtypeStruct((2 * ROWS, D), BF),
        in_specs=[SMEM] + [ANY] * 3,
        out_specs=VMEM,
        scratch_shapes=[pltpu.SemaphoreType.DMA(())],
        compiler_params=PARAMS,
        cost_estimate=pl.CostEstimate(
            flops=0, bytes_accessed=8 * ROWS * D, transcendentals=0
        ),
    )(flags, two, cross_one, cross_two)


def pairs_kernel(
    flags, scale, z_ref, u_ref, rn_ref,
    here, one, two, three, cross_one, cross_two, cross_three, second, early_mid, early_far,
    dx_ref, others, sems,
):
    del early_mid, early_far
    place = flags[1]

    def fetch(source, s):
        for b in range(2):
            pltpu.make_async_copy(
                source.at[pl.ds((1 - b) * ROWS, ROWS)],
                others.at[b, pl.ds(s * ROWS, ROWS)],
                sems.at[2 * s + b],
            ).start()

    fetch(here, 0)

    @pl.when(place > 0)
    def _():
        fetch(one, 1)
        fetch(three, 3)

    @pl.when(place == 0)
    def _():
        fetch(second, 1)
        fetch(cross_two, 2)
        fetch(cross_three, 3)

    @pl.when(place == 1)
    def _():
        fetch(cross_one, 2)

    @pl.when(place > 1)
    def _():
        fetch(two, 2)

    t = scale[0]
    bias = scale[1]
    for s in range(4):
        for b in range(2):
            pltpu.make_async_copy(
                here.at[pl.ds(0, ROWS)],
                others.at[b, pl.ds(s * ROWS, ROWS)],
                sems.at[2 * s + b],
            ).wait()
    row = lax.broadcasted_iota(jnp.int32, (ROWS, 4 * ROWS), 0)
    col = lax.broadcasted_iota(jnp.int32, (ROWS, 4 * ROWS), 1)
    for b in range(2):
        mine = z_ref[b * ROWS : (b + 1) * ROWS]
        logits = t * lax.dot_general(
            mine, others[b], (((1,), (1,)), ((), ())), preferred_element_type=F32
        ) + bias
        prob = jax.nn.sigmoid(logits) - jnp.where(row == col, 1.0, 0.0)
        weight = (prob * (1.0 / ROWS)).astype(BF)
        dz = t * jnp.dot(weight, others[b], preferred_element_type=F32)
        u = u_ref[b * ROWS : (b + 1) * ROWS]
        rn = rn_ref[b * ROWS : (b + 1) * ROWS, :1]
        inner = jnp.sum(u * dz, axis=-1, keepdims=True)
        dx_ref[b * ROWS : (b + 1) * ROWS] = ((dz - u * inner) * rn).astype(BF)


def pairs(flags, scale, z, *rest):
    rows = 2 * ROWS
    return pl.pallas_call(
        pairs_kernel,
        name="pairs",
        out_shape=jax.ShapeDtypeStruct((rows, D), BF),
        in_specs=[SMEM, SMEM] + [VMEM] * 3 + [ANY] * 10,
        out_specs=VMEM,
        scratch_shapes=[
            pltpu.VMEM((2, 4 * ROWS, D), BF),
            pltpu.SemaphoreType.DMA((8,)),
        ],
        compiler_params=PARAMS,
        cost_estimate=pl.CostEstimate(
            flops=16 * rows * ROWS * D, bytes_accessed=14 * rows * D, transcendentals=rows * 512
        ),
    )(flags, scale, z, *rest)


def near_kernel(ft, dx, feats_end, dx_end, feats_mid, dx_mid, inner_ref, outer_ref):
    dx_own = dx[...]
    dx_other = dx_mid[...]
    inner_ref[...] = (
        jnp.dot(ft[CHIP : 2 * CHIP], dx_own, preferred_element_type=F32)
        + jnp.dot(feats_end[:CHIP], dx_end[...], preferred_element_type=F32)
        + jnp.dot(feats_mid[:CHIP], dx_other, preferred_element_type=F32)
    )
    outer_ref[...] = jnp.dot(ft[:CHIP], dx_own, preferred_element_type=F32) + jnp.dot(
        feats_mid[CHIP:], dx_other, preferred_element_type=F32
    )


def near(ft, dx, feats_end, dx_end, feats_mid, dx_mid):
    return pl.pallas_call(
        near_kernel,
        name="near",
        out_shape=(
            jax.ShapeDtypeStruct((CHIP, D), F32),
            jax.ShapeDtypeStruct((CHIP, D), F32),
        ),
        in_specs=[VMEM] * 6,
        out_specs=(VMEM,) * 2,
        compiler_params=PARAMS,
        cost_estimate=pl.CostEstimate(
            flops=20 * CHIP * ROWS * D, bytes_accessed=14 * CHIP * D, transcendentals=0
        ),
    )(ft, dx, feats_end, dx_end, feats_mid, dx_mid)


def far_kernel(flags, outer_ref, feats, dx, same, crossed, part):
    c = flags[0]
    part[...] = outer_ref[...] + jnp.dot(
        feats[CHIP:], dx[...], preferred_element_type=F32
    )
    mine = pl.ds(pl.multiple_of(c * CORE, CORE), CORE)
    theirs = pl.ds(pl.multiple_of((1 - c) * CORE, CORE), CORE)
    same[...] = part[mine].astype(BF)
    crossed[...] = part[theirs].astype(BF)


def far(flags, outer, feats, dx):
    return pl.pallas_call(
        far_kernel,
        name="far",
        out_shape=(
            jax.ShapeDtypeStruct((CORE, D), BF),
            jax.ShapeDtypeStruct((CORE, D), BF),
            jax.ShapeDtypeStruct((CHIP, D), F32),
        ),
        in_specs=[SMEM] + [VMEM] * 3,
        out_specs=(VMEM,) * 3,
        compiler_params=PARAMS,
        cost_estimate=pl.CostEstimate(
            flops=4 * CHIP * ROWS * D, bytes_accessed=14 * CHIP * D, transcendentals=0
        ),
    )(flags, outer, feats, dx)


def rest_kernel(flags, inner_ref, feats, dx, part, keep, swap, total):
    c = flags[0]
    mine = pl.ds(pl.multiple_of(c * CORE, CORE), CORE)
    theirs = pl.ds(pl.multiple_of((1 - c) * CORE, CORE), CORE)

    @pl.when(flags[4] == 1)
    def _():
        total[...] = inner_ref[...] + jnp.dot(
            feats[:CHIP], dx[...], preferred_element_type=F32
        )
        keep[...] = total[mine]
        swap[...] = total[theirs].astype(BF)

    @pl.when(flags[4] == 0)
    def _():
        keep[...] = part[mine]
        swap[...] = part[theirs].astype(BF)


def rest(flags, *parts):
    return pl.pallas_call(
        rest_kernel,
        name="rest",
        out_shape=(
            jax.ShapeDtypeStruct((CORE, D), F32),
            jax.ShapeDtypeStruct((CORE, D), BF),
        ),
        in_specs=[SMEM] + [VMEM] * 4,
        out_specs=(VMEM, VMEM),
        scratch_shapes=[pltpu.VMEM((CHIP, D), F32)],
        compiler_params=PARAMS,
        cost_estimate=pl.CostEstimate(
            flops=4 * CHIP * ROWS * D, bytes_accessed=14 * CHIP * D, transcendentals=0
        ),
    )(flags, *parts)


def finish_kernel(flags, same, crossed, swap, keep, image_ref, text_ref):
    own = keep[...] + same[...].astype(F32)
    other = swap[...].astype(F32) + crossed[...].astype(F32)

    @pl.when(flags[0] == 0)
    def _():
        image_ref[0] = own
        text_ref[0] = other

    @pl.when(flags[0] == 1)
    def _():
        image_ref[0] = other
        text_ref[0] = own


def finish(flags, *parts):
    shape = jax.ShapeDtypeStruct((1, CORE, D), F32)
    return pl.pallas_call(
        finish_kernel,
        name="finish",
        out_shape=(shape, shape),
        in_specs=[SMEM] + [VMEM] * 4,
        out_specs=(VMEM, VMEM),
        compiler_params=PARAMS,
        cost_estimate=pl.CostEstimate(
            flops=4 * CORE * D, bytes_accessed=18 * CORE * D, transcendentals=0
        ),
    )(flags, *parts)


def on_device(pictures, captions, picture_head, caption_head, sharpness, shift_term):
    c = lax.axis_index("c")
    y = lax.axis_index("y")
    zl = lax.axis_index("zl")
    yy = jnp.where(c == 0, y, 7 - y)
    flags = jnp.stack([c, yy, zl, zl >= 2, (zl == 1) | (zl == 2)]).astype(jnp.int32)
    scale = jnp.concatenate([sharpness, shift_term])

    received = send(jnp.where(c == 0, captions, pictures), other_core)
    z, u, rn = project(flags, pictures, captions, received, picture_head, caption_head)

    one = send(z, first_hop)
    cross_one = send(z, first_crossing)
    here = send(z, other_core)
    ft = turn(flags, pictures, captions, received)
    one, ft = lax.optimization_barrier((one, ft))
    two = send(one, second_hop)
    ft_end = send(ft[CHIP:], inward)
    ft_mid = send(ft[2 * CHIP :], middle)
    cross_two = send(one, later_crossing)
    cross_three = send(two, later_crossing)
    second = send(cross_one, from_second)
    three = send(choose(flags, two, cross_one, cross_two), third_hop)
    ft_far = send(ft_end[CHIP:], middle)
    dx = pairs(
        flags, scale, z, u, rn,
        here, one, two, three, cross_one, cross_two, cross_three, second, ft_mid, ft_far,
    )

    dx_end = send(dx, inward)
    dx_mid = send(dx, middle)
    dx_far = send(dx_end, middle)
    inner, outer = near(ft, dx, ft_end, dx_end, ft_mid, dx_mid)
    same, crossed, part = far(flags, outer, ft_far, dx_far)
    same = send(same, outward)
    crossed = send(crossed, outward_cross)
    keep, swap = rest(flags, inner, ft_far, dx_far, part)
    swap = send(swap, other_core)
    return finish(flags, same, crossed, swap, keep)


def solution(mesh):
    physical = Mesh(mesh.devices.reshape(SIZES), NAMES)
    rows = P(NAMES, None)
    grad = P(("x", "zh", "y"), ("zl", "c"), None)
    return jax.shard_map(
        on_device,
        mesh=physical,
        in_specs=(rows, rows, P(), P(), P(), P()),
        out_specs=(grad, grad),
        check_vma=False,
    )
```

```python
import functools

import jax
import jax.numpy as jnp
from jax import lax
from jax.experimental import pallas as pl
from jax.experimental.pallas import tpu as pltpu
from jax.sharding import Mesh, PartitionSpec as P

NAMES = ("x", "zh", "y", "zl", "c")
NX, NZH, NY, NZL, NC = SIZES = (8, 2, 8, 4, 2)
ROWS = 128
D = 1152
CHIP = 288
CORE = 144
LEFT = 512
HALVES = (slice(0, LEFT), slice(LEFT, D))
EPS = 1e-06
BF = jnp.bfloat16
F32 = jnp.float32
PROJECT_LIMIT = 51
VMEM = pl.BlockSpec(memory_space=pltpu.VMEM)
SMEM = pl.BlockSpec(memory_space=pltpu.SMEM)
ANY = pl.BlockSpec(memory_space=pl.ANY)
HBM = pl.BlockSpec(memory_space=pltpu.HBM)
PARAMS = pltpu.CompilerParams(vmem_limit_bytes=32 * 1024 * 1024)


def index_of(x, zh, y, zl, c):
    return (((x * NZH + zh) * NY + y) * NZL + zl) * NC + c


def pairs_of(rule):
    found = []
    for x in range(NX):
        for zh in range(NZH):
            for y in range(NY):
                for zl in range(NZL):
                    for c in range(NC):
                        target = rule(x, zh, y, zl, c)
                        if target is not None:
                            found.append((index_of(x, zh, y, zl, c), index_of(*target)))
    return found


def send(value, rule):
    return lax.ppermute(value, NAMES, pairs_of(rule))


def other_core(x, zh, y, zl, c):
    return (x, zh, y, zl, 1 - c)


def first_hop(x, zh, y, zl, c):
    if c == 1:
        return (x, zh, y + 1, zl, 0) if y < 7 else None
    return (x, zh, y - 1, zl, 1) if y > 0 else None


def second_hop(x, zh, y, zl, c):
    if not 1 <= y <= 6:
        return None
    return (x, zh, y + 1 if c == 0 else y - 1, zl, c)


def third_hop(x, zh, y, zl, c):
    if c == 0:
        return (x, zh, y + 1, zl, 0) if y < 7 else None
    return (x, zh, y - 1, zl, 1) if y > 0 else None


def above(x, zh, column):
    return (x, 1, column) if zh == 0 else ((x + 1) % NX, 0, column)


def below(x, zh, column):
    return (x, 0, column) if zh == 1 else ((x - 1) % NX, 1, column)


def first_crossing(x, zh, y, zl, c):
    if c == 1 and y >= 6:
        return (*above(x, zh, y - 6), zl, 0)
    if c == 0 and y <= 1:
        return (*below(x, zh, y + 6), zl, 1)
    return None


def second_crossing(x, zh, y, zl, c):
    if c == 0 and y == 6:
        return (*above(x, zh, 0), zl, 0)
    if c == 1 and y == 1:
        return (*below(x, zh, 7), zl, 1)
    return None


def from_second(x, zh, y, zl, c):
    if c == 0 and y == 1:
        return (x, zh, 0, zl, 0)
    if c == 1 and y == 6:
        return (x, zh, 7, zl, 1)
    return None


def inward(x, zh, y, zl, c):
    return {0: (x, zh, y, 1, c), 3: (x, zh, y, 2, c)}.get(zl)


def middle(x, zh, y, zl, c):
    return {1: (x, zh, y, 2, c), 2: (x, zh, y, 1, c)}.get(zl)


def outward(x, zh, y, zl, c):
    return {1: (x, zh, y, 0, c), 2: (x, zh, y, 3, c)}.get(zl)


def outward_cross(x, zh, y, zl, c):
    return {1: (x, zh, y, 0, 1 - c), 2: (x, zh, y, 3, 1 - c)}.get(zl)


def project_kernel(
    flags, own, recv, wp, wc, z_ref, u_ref, rn_ref, f_ref, w_ref, sems
):
    c = flags[0]
    parts = 3
    width = D // parts

    def fetch(head):
        for j in range(parts):
            cols = pl.ds(j * width, width)
            pltpu.make_async_copy(head.at[:, cols], w_ref.at[j], sems.at[j]).start()

    @pl.when(c == 0)
    def _():
        fetch(wp)

    @pl.when(c == 1)
    def _():
        fetch(wc)

    f_ref[:ROWS] = own[...]
    f_ref[ROWS:] = recv[...]
    total = jnp.zeros((2 * ROWS, 1), F32)
    for j in range(parts):
        cols = pl.ds(j * width, width)
        pltpu.make_async_copy(wp.at[:, cols], w_ref.at[j], sems.at[j]).wait()
        x = jnp.dot(f_ref[...], w_ref[j], preferred_element_type=F32)
        u_ref[:, cols] = x
        total = total + jnp.sum(x * x, axis=-1, keepdims=True)
    rn = 1.0 / jnp.sqrt(total + EPS)
    rn_ref[...] = jnp.broadcast_to(rn, (2 * ROWS, 128))
    u = u_ref[...] * rn
    u_ref[...] = u
    z_ref[...] = u.astype(BF)


def project(flags, own, recv, wp, wc):
    rows = 2 * ROWS
    return pl.pallas_call(
        project_kernel,
        name="project",
        out_shape=(
            jax.ShapeDtypeStruct((rows, D), BF),
            jax.ShapeDtypeStruct((rows, D), F32),
            jax.ShapeDtypeStruct((rows, 128), F32),
        ),
        in_specs=[SMEM, VMEM, VMEM, HBM, HBM],
        out_specs=(VMEM,) * 3,
        scratch_shapes=[
            pltpu.VMEM((rows, D), BF),
            pltpu.VMEM((3, D, D // 3), BF),
            pltpu.SemaphoreType.DMA((3,)),
        ],
        compiler_params=pltpu.CompilerParams(vmem_limit_bytes=PROJECT_LIMIT * 1024 * 1024),
        cost_estimate=pl.CostEstimate(
            flops=2 * rows * D * D, bytes_accessed=2 * D * D + 8 * rows * D, transcendentals=0
        ),
    )(flags, own, recv, wp, wc)


def turn_kernel(flags, own, recv, ft_ref, turned):
    mirror = flags[3]
    turned[:, :ROWS] = own[...].T
    turned[:, ROWS:] = recv[...].T
    for j in range(4):
        start = pl.multiple_of(jnp.where(mirror == 1, 3 - j, j) * CHIP, CHIP)
        ft_ref[j * CHIP : (j + 1) * CHIP] = turned[pl.ds(start, CHIP)]


def turn(flags, own, recv):
    return pl.pallas_call(
        turn_kernel,
        name="turn",
        out_shape=jax.ShapeDtypeStruct((D, 2 * ROWS), BF),
        in_specs=[SMEM, VMEM, VMEM],
        out_specs=VMEM,
        scratch_shapes=[pltpu.VMEM((D, 2 * ROWS), BF)],
        compiler_params=PARAMS,
        cost_estimate=pl.CostEstimate(
            flops=0, bytes_accessed=8 * ROWS * D, transcendentals=0
        ),
    )(flags, own, recv)


def choose_kernel(flags, two, cross_one, out_ref, sem):
    place = flags[1]

    @pl.when(place <= 1)
    def _():
        pltpu.make_async_copy(cross_one, out_ref, sem).start()

    @pl.when(place > 1)
    def _():
        pltpu.make_async_copy(two, out_ref, sem).start()

    pltpu.make_async_copy(two, out_ref, sem).wait()


def choose(flags, two, cross_one):
    return pl.pallas_call(
        choose_kernel,
        name="choose",
        out_shape=jax.ShapeDtypeStruct((2 * ROWS, D), BF),
        in_specs=[SMEM] + [ANY] * 2,
        out_specs=VMEM,
        scratch_shapes=[pltpu.SemaphoreType.DMA(())],
        compiler_params=PARAMS,
        cost_estimate=pl.CostEstimate(
            flops=0, bytes_accessed=8 * ROWS * D, transcendentals=0
        ),
    )(flags, two, cross_one)


def pairs_kernel(
    flags, scale, z_ref, u_ref, rn_ref,
    here, one, two, three, cross_one, cross_two, second, early_mid, early_far,
    dx_left, dx_right, others, sems,
):
    del early_mid, early_far
    place = flags[1]

    def fetch(source, s):
        for b in range(2):
            pltpu.make_async_copy(
                source.at[pl.ds((1 - b) * ROWS, ROWS)],
                others.at[b, pl.ds(s * ROWS, ROWS)],
                sems.at[2 * s + b],
            ).start()

    fetch(here, 0)

    @pl.when(place > 0)
    def _():
        fetch(one, 1)
        fetch(three, 3)

    @pl.when(place == 0)
    def _():
        fetch(second, 1)
        fetch(cross_two, 3)

    @pl.when(place <= 1)
    def _():
        fetch(cross_one, 2)

    @pl.when(place > 1)
    def _():
        fetch(two, 2)

    t = scale[0]
    bias = scale[1]
    for s in range(4):
        for b in range(2):
            pltpu.make_async_copy(
                here.at[pl.ds(0, ROWS)],
                others.at[b, pl.ds(s * ROWS, ROWS)],
                sems.at[2 * s + b],
            ).wait()
    row = lax.broadcasted_iota(jnp.int32, (ROWS, 4 * ROWS), 0)
    col = lax.broadcasted_iota(jnp.int32, (ROWS, 4 * ROWS), 1)
    for b in range(2):
        mine = z_ref[b * ROWS : (b + 1) * ROWS]
        logits = t * lax.dot_general(
            mine, others[b], (((1,), (1,)), ((), ())), preferred_element_type=F32
        ) + bias
        prob = jax.nn.sigmoid(logits) - jnp.where(row == col, 1.0, 0.0)
        weight = (prob * (1.0 / ROWS)).astype(BF)
        dz = t * jnp.dot(weight, others[b], preferred_element_type=F32)
        u = u_ref[b * ROWS : (b + 1) * ROWS]
        rn = rn_ref[b * ROWS : (b + 1) * ROWS, :1]
        inner = jnp.sum(u * dz, axis=-1, keepdims=True)
        dx = ((dz - u * inner) * rn).astype(BF)
        for cols, dx_ref in zip(HALVES, (dx_left, dx_right)):
            dx_ref[b * ROWS : (b + 1) * ROWS] = dx[:, cols]


def pairs(flags, scale, z, *rest):
    rows = 2 * ROWS
    return pl.pallas_call(
        pairs_kernel,
        name="pairs",
        out_shape=(
            jax.ShapeDtypeStruct((rows, LEFT), BF),
            jax.ShapeDtypeStruct((rows, D - LEFT), BF),
        ),
        in_specs=[SMEM, SMEM] + [VMEM] * 3 + [ANY] * 9,
        out_specs=(VMEM, VMEM),
        scratch_shapes=[
            pltpu.VMEM((2, 4 * ROWS, D), BF),
            pltpu.SemaphoreType.DMA((8,)),
        ],
        compiler_params=PARAMS,
        cost_estimate=pl.CostEstimate(
            flops=16 * rows * ROWS * D, bytes_accessed=14 * rows * D, transcendentals=rows * 512
        ),
    )(flags, scale, z, *rest)


def near_kernel(ft, feats_end, feats_mid, *refs):
    inner_ref, outer_ref = refs[6:]
    for cols, dx, dx_end, dx_mid in zip(HALVES, refs[:2], refs[2:4], refs[4:6]):
        dx_own = dx[...]
        dx_other = dx_mid[...]
        inner_ref[:, cols] = (
            jnp.dot(ft[CHIP : 2 * CHIP], dx_own, preferred_element_type=F32)
            + jnp.dot(feats_end[:CHIP], dx_end[...], preferred_element_type=F32)
            + jnp.dot(feats_mid[:CHIP], dx_other, preferred_element_type=F32)
        )
        outer_ref[:, cols] = jnp.dot(
            ft[:CHIP], dx_own, preferred_element_type=F32
        ) + jnp.dot(feats_mid[CHIP:], dx_other, preferred_element_type=F32)


def near(ft, feats_end, feats_mid, *dxs):
    return pl.pallas_call(
        near_kernel,
        name="near",
        out_shape=(
            jax.ShapeDtypeStruct((CHIP, D), F32),
            jax.ShapeDtypeStruct((CHIP, D), F32),
        ),
        in_specs=[VMEM] * 9,
        out_specs=(VMEM, VMEM),
        compiler_params=PARAMS,
        cost_estimate=pl.CostEstimate(
            flops=20 * CHIP * ROWS * D, bytes_accessed=14 * CHIP * D, transcendentals=0
        ),
    )(ft, feats_end, feats_mid, *dxs)


def far_kernel(half, flags, outer_ref, feats, dx, *refs):
    same, crossed, part = refs[-3:]
    c = flags[0]
    part[...] = outer_ref[:, HALVES[half]] + jnp.dot(
        feats[CHIP:], dx[...], preferred_element_type=F32
    )
    mine = pl.ds(pl.multiple_of(c * CORE, CORE), CORE)
    theirs = pl.ds(pl.multiple_of((1 - c) * CORE, CORE), CORE)
    same[...] = part[mine].astype(BF)
    crossed[...] = part[theirs].astype(BF)


def far(half, flags, outer, feats, dx, *after):
    cols = dx.shape[1]
    return pl.pallas_call(
        functools.partial(far_kernel, half),
        name="far",
        out_shape=(
            jax.ShapeDtypeStruct((CORE, cols), BF),
            jax.ShapeDtypeStruct((CORE, cols), BF),
            jax.ShapeDtypeStruct((CHIP, cols), F32),
        ),
        in_specs=[SMEM] + [VMEM] * 3 + [ANY] * len(after),
        out_specs=(VMEM,) * 3,
        compiler_params=PARAMS,
        cost_estimate=pl.CostEstimate(
            flops=4 * CHIP * ROWS * cols, bytes_accessed=14 * CHIP * cols, transcendentals=0
        ),
    )(flags, outer, feats, dx, *after)


def rest_kernel(
    flags, inner_ref, feats, dx_left, dx_right, part_left, part_right,
    keep, swap_left, swap_right, total,
):
    c = flags[0]
    mine = pl.ds(pl.multiple_of(c * CORE, CORE), CORE)
    theirs = pl.ds(pl.multiple_of((1 - c) * CORE, CORE), CORE)

    @pl.when(flags[4] == 1)
    def _():
        for cols, dx in zip(HALVES, (dx_left, dx_right)):
            total[:, cols] = inner_ref[:, cols] + jnp.dot(
                feats[:CHIP], dx[...], preferred_element_type=F32
            )
        keep[...] = total[mine]
        swap_left[...] = total[theirs, :LEFT].astype(BF)
        swap_right[...] = total[theirs, LEFT:].astype(BF)

    @pl.when(flags[4] == 0)
    def _():
        for cols, part, swap in zip(
            HALVES, (part_left, part_right), (swap_left, swap_right)
        ):
            keep[:, cols] = part[mine]
            swap[...] = part[theirs].astype(BF)


def rest(flags, *parts):
    return pl.pallas_call(
        rest_kernel,
        name="rest",
        out_shape=(
            jax.ShapeDtypeStruct((CORE, D), F32),
            jax.ShapeDtypeStruct((CORE, LEFT), BF),
            jax.ShapeDtypeStruct((CORE, D - LEFT), BF),
        ),
        in_specs=[SMEM] + [VMEM] * 6,
        out_specs=(VMEM,) * 3,
        scratch_shapes=[pltpu.VMEM((CHIP, D), F32)],
        compiler_params=PARAMS,
        cost_estimate=pl.CostEstimate(
            flops=4 * CHIP * ROWS * D, bytes_accessed=14 * CHIP * D, transcendentals=0
        ),
    )(flags, *parts)


def finish_kernel(
    flags, same_left, crossed_left, same_right, crossed_right, swap_left, swap_right, keep,
    image_ref, text_ref,
):
    def put(own_ref, other_ref):
        for cols, same, crossed, swap in (
            (HALVES[0], same_left, crossed_left, swap_left),
            (HALVES[1], same_right, crossed_right, swap_right),
        ):
            own_ref[0, :, cols] = keep[:, cols] + same[...].astype(F32)
            other_ref[0, :, cols] = swap[...].astype(F32) + crossed[...].astype(F32)

    @pl.when(flags[0] == 0)
    def _():
        put(image_ref, text_ref)

    @pl.when(flags[0] == 1)
    def _():
        put(text_ref, image_ref)


def finish(flags, *parts):
    shape = jax.ShapeDtypeStruct((1, CORE, D), F32)
    return pl.pallas_call(
        finish_kernel,
        name="finish",
        out_shape=(shape, shape),
        in_specs=[SMEM] + [VMEM] * 7,
        out_specs=(VMEM, VMEM),
        compiler_params=PARAMS,
        cost_estimate=pl.CostEstimate(
            flops=4 * CORE * D, bytes_accessed=18 * CORE * D, transcendentals=0
        ),
    )(flags, *parts)


def on_device(pictures, captions, picture_head, caption_head, sharpness, shift_term):
    c = lax.axis_index("c")
    y = lax.axis_index("y")
    zl = lax.axis_index("zl")
    yy = jnp.where(c == 0, y, 7 - y)
    flags = jnp.stack([c, yy, zl, zl >= 2, (zl == 1) | (zl == 2)]).astype(jnp.int32)
    scale = jnp.concatenate([sharpness, shift_term])

    received = send(jnp.where(c == 0, captions, pictures), other_core)
    own = jnp.where(c == 0, pictures, captions)
    z, u, rn = project(flags, own, received, picture_head, caption_head)

    one = send(z, first_hop)
    cross_one = send(z, first_crossing)
    ft = turn(flags, own, received)
    one, ft = lax.optimization_barrier((one, ft))
    ft_end = send(ft[CHIP:], inward)
    ft_mid = send(ft[2 * CHIP :], middle)
    ft_far = send(ft_end[CHIP:], middle)
    two = send(one, second_hop)
    cross_two = send(one, second_crossing)
    second = send(cross_one, from_second)
    chosen, z_late = lax.optimization_barrier((choose(flags, two, cross_one), z))
    three = send(chosen, third_hop)
    here = send(z_late, other_core)
    dxs = pairs(
        flags, scale, z, u, rn, here, one, two, three, cross_one, cross_two, second, ft_mid, ft_far
    )

    ends = [send(dx, inward) for dx in dxs]
    mids = [send(dx, middle) for dx in dxs]
    inner, outer = near(ft, ft_end, ft_mid, *dxs, *ends, *mids)
    right, inner = lax.optimization_barrier((ends[1], inner))
    fars = [send(ends[0], middle), send(right, middle)]
    same_left, crossed_left, part_left = far(0, flags, outer, ft_far, fars[0])
    same_left = send(same_left, outward)
    crossed_left = send(crossed_left, outward_cross)
    same_right, crossed_right, part_right = far(1, flags, outer, ft_far, fars[1], part_left)
    same_right = send(same_right, outward)
    crossed_right = send(crossed_right, outward_cross)
    keep, *swaps = rest(flags, inner, ft_far, *fars, part_left, part_right)
    swaps, same_left, crossed_left = lax.optimization_barrier(
        (swaps, same_left, crossed_left)
    )
    swaps = [send(swap, other_core) for swap in swaps]
    return finish(
        flags, same_left, crossed_left, same_right, crossed_right, *swaps, keep
    )


def solution(mesh):
    physical = Mesh(mesh.devices.reshape(SIZES), NAMES)
    rows = P(NAMES, None)
    grad = P(("x", "zh", "y"), ("zl", "c"), None)
    return jax.shard_map(
        on_device,
        mesh=physical,
        in_specs=(rows, rows, P(), P(), P(), P()),
        out_specs=(grad, grad),
        check_vma=False,
    )
```

```python
import functools

import jax
import jax.numpy as jnp
from jax import lax
from jax.experimental import pallas as pl
from jax.experimental.pallas import tpu as pltpu
from jax.sharding import Mesh, PartitionSpec as P

NAMES = ("x", "zh", "y", "zl", "c")
NX, NZH, NY, NZL, NC = SIZES = (8, 2, 8, 4, 2)
ROWS = 128
D = 1152
CHIP = 288
CORE = 144
LEFT = 512
HALVES = (slice(0, LEFT), slice(LEFT, D))
EPS = 1e-06
BF = jnp.bfloat16
F32 = jnp.float32
PROJECT_LIMIT = 51
VMEM = pl.BlockSpec(memory_space=pltpu.VMEM)
SMEM = pl.BlockSpec(memory_space=pltpu.SMEM)
ANY = pl.BlockSpec(memory_space=pl.ANY)
HBM = pl.BlockSpec(memory_space=pltpu.HBM)
PARAMS = pltpu.CompilerParams(vmem_limit_bytes=32 * 1024 * 1024)


def index_of(x, zh, y, zl, c):
    return (((x * NZH + zh) * NY + y) * NZL + zl) * NC + c


def pairs_of(rule):
    found = []
    for x in range(NX):
        for zh in range(NZH):
            for y in range(NY):
                for zl in range(NZL):
                    for c in range(NC):
                        target = rule(x, zh, y, zl, c)
                        if target is not None:
                            found.append((index_of(x, zh, y, zl, c), index_of(*target)))
    return found


def send(value, rule):
    return lax.ppermute(value, NAMES, pairs_of(rule))


def other_core(x, zh, y, zl, c):
    return (x, zh, y, zl, 1 - c)


def first_hop(x, zh, y, zl, c):
    if c == 1:
        return (x, zh, y + 1, zl, 0) if y < 7 else None
    return (x, zh, y - 1, zl, 1) if y > 0 else None


def second_hop(x, zh, y, zl, c):
    if not 1 <= y <= 6:
        return None
    return (x, zh, y + 1 if c == 0 else y - 1, zl, c)


def third_hop(x, zh, y, zl, c):
    if c == 0:
        return (x, zh, y + 1, zl, 0) if y < 7 else None
    return (x, zh, y - 1, zl, 1) if y > 0 else None


def above(x, zh, column):
    return (x, 1, column) if zh == 0 else ((x + 1) % NX, 0, column)


def below(x, zh, column):
    return (x, 0, column) if zh == 1 else ((x - 1) % NX, 1, column)


def first_crossing(x, zh, y, zl, c):
    if c == 1 and y in (5, 7):
        return (*above(x, zh, 1 if y == 7 else 5), zl, 0)
    if c == 0 and y in (0, 2):
        return (*below(x, zh, 6 if y == 0 else 2), zl, 1)
    return None


def second_crossing(x, zh, y, zl, c):
    if c == 0 and y == 7:
        return (*above(x, zh, 0), zl, 0)
    if c == 1 and y == 0:
        return (*below(x, zh, 7), zl, 1)
    return None


def from_near(x, zh, y, zl, c):
    if c == 0 and y == 1:
        return (x, zh, 0, zl, 0)
    if c == 1 and y == 6:
        return (x, zh, 7, zl, 1)
    return None


def from_afar(x, zh, y, zl, c):
    if c == 0 and y == 5:
        return (x, zh, 0, zl, 0)
    if c == 1 and y == 2:
        return (x, zh, 7, zl, 1)
    return None


def inward(x, zh, y, zl, c):
    return {0: (x, zh, y, 1, c), 3: (x, zh, y, 2, c)}.get(zl)


def middle(x, zh, y, zl, c):
    return {1: (x, zh, y, 2, c), 2: (x, zh, y, 1, c)}.get(zl)


def outward(x, zh, y, zl, c):
    return {1: (x, zh, y, 0, c), 2: (x, zh, y, 3, c)}.get(zl)


def outward_cross(x, zh, y, zl, c):
    return {1: (x, zh, y, 0, 1 - c), 2: (x, zh, y, 3, 1 - c)}.get(zl)


def project_kernel(
    flags, own, recv, wp, wc, z_ref, u_ref, rn_ref, f_ref, w_ref, sems
):
    c = flags[0]
    parts = 3
    width = D // parts

    def fetch(head):
        for j in range(parts):
            cols = pl.ds(j * width, width)
            pltpu.make_async_copy(head.at[:, cols], w_ref.at[j], sems.at[j]).start()

    @pl.when(c == 0)
    def _():
        fetch(wp)

    @pl.when(c == 1)
    def _():
        fetch(wc)

    f_ref[:ROWS] = own[...]
    f_ref[ROWS:] = recv[...]
    total = jnp.zeros((2 * ROWS, 1), F32)
    for j in range(parts):
        cols = pl.ds(j * width, width)
        pltpu.make_async_copy(wp.at[:, cols], w_ref.at[j], sems.at[j]).wait()
        x = jnp.dot(f_ref[...], w_ref[j], preferred_element_type=F32)
        u_ref[:, cols] = x
        total = total + jnp.sum(x * x, axis=-1, keepdims=True)
    rn = 1.0 / jnp.sqrt(total + EPS)
    rn_ref[...] = jnp.broadcast_to(rn, (2 * ROWS, 128))
    u = u_ref[...] * rn
    u_ref[...] = u
    z_ref[...] = u.astype(BF)


def project(flags, own, recv, wp, wc):
    rows = 2 * ROWS
    return pl.pallas_call(
        project_kernel,
        name="project",
        out_shape=(
            jax.ShapeDtypeStruct((rows, D), BF),
            jax.ShapeDtypeStruct((rows, D), F32),
            jax.ShapeDtypeStruct((rows, 128), F32),
        ),
        in_specs=[SMEM, VMEM, VMEM, HBM, HBM],
        out_specs=(VMEM,) * 3,
        scratch_shapes=[
            pltpu.VMEM((rows, D), BF),
            pltpu.VMEM((3, D, D // 3), BF),
            pltpu.SemaphoreType.DMA((3,)),
        ],
        compiler_params=pltpu.CompilerParams(vmem_limit_bytes=PROJECT_LIMIT * 1024 * 1024),
        cost_estimate=pl.CostEstimate(
            flops=2 * rows * D * D, bytes_accessed=2 * D * D + 8 * rows * D, transcendentals=0
        ),
    )(flags, own, recv, wp, wc)


def turn_kernel(flags, own, recv, ft_ref, turned):
    mirror = flags[3]
    turned[:, :ROWS] = own[...].T
    turned[:, ROWS:] = recv[...].T
    for j in range(4):
        start = pl.multiple_of(jnp.where(mirror == 1, 3 - j, j) * CHIP, CHIP)
        ft_ref[j * CHIP : (j + 1) * CHIP] = turned[pl.ds(start, CHIP)]


def turn(flags, own, recv):
    return pl.pallas_call(
        turn_kernel,
        name="turn",
        out_shape=jax.ShapeDtypeStruct((D, 2 * ROWS), BF),
        in_specs=[SMEM, VMEM, VMEM],
        out_specs=VMEM,
        scratch_shapes=[pltpu.VMEM((D, 2 * ROWS), BF)],
        compiler_params=PARAMS,
        cost_estimate=pl.CostEstimate(
            flops=0, bytes_accessed=8 * ROWS * D, transcendentals=0
        ),
    )(flags, own, recv)


def choose_kernel(flags, two, cross_one, cross_two, out_ref, sem):
    place = flags[1]

    @pl.when(place == 0)
    def _():
        pltpu.make_async_copy(cross_two, out_ref, sem).start()

    @pl.when(place == 1)
    def _():
        pltpu.make_async_copy(cross_one, out_ref, sem).start()

    @pl.when(place > 1)
    def _():
        pltpu.make_async_copy(two, out_ref, sem).start()

    pltpu.make_async_copy(two, out_ref, sem).wait()


def choose(flags, two, cross_one, cross_two):
    return pl.pallas_call(
        choose_kernel,
        name="choose",
        out_shape=jax.ShapeDtypeStruct((2 * ROWS, D), BF),
        in_specs=[SMEM] + [ANY] * 3,
        out_specs=VMEM,
        scratch_shapes=[pltpu.SemaphoreType.DMA(())],
        compiler_params=PARAMS,
        cost_estimate=pl.CostEstimate(
            flops=0, bytes_accessed=8 * ROWS * D, transcendentals=0
        ),
    )(flags, two, cross_one, cross_two)


def pairs_kernel(
    flags, scale, z_ref, u_ref, rn_ref,
    here, one, two, three, cross_one, cross_two, near_one, afar_one, early_mid, early_far,
    dx_left, dx_right, others, sems,
):
    del early_mid, early_far
    place = flags[1]

    def fetch(source, s):
        for b in range(2):
            pltpu.make_async_copy(
                source.at[pl.ds((1 - b) * ROWS, ROWS)],
                others.at[b, pl.ds(s * ROWS, ROWS)],
                sems.at[2 * s + b],
            ).start()

    fetch(here, 0)

    @pl.when(place > 0)
    def _():
        fetch(one, 1)
        fetch(three, 3)

    @pl.when(place == 0)
    def _():
        fetch(near_one, 1)
        fetch(cross_two, 2)
        fetch(afar_one, 3)

    @pl.when(place == 1)
    def _():
        fetch(cross_one, 2)

    @pl.when(place > 1)
    def _():
        fetch(two, 2)

    t = scale[0]
    bias = scale[1]
    for s in range(4):
        for b in range(2):
            pltpu.make_async_copy(
                here.at[pl.ds(0, ROWS)],
                others.at[b, pl.ds(s * ROWS, ROWS)],
                sems.at[2 * s + b],
            ).wait()
    row = lax.broadcasted_iota(jnp.int32, (ROWS, 4 * ROWS), 0)
    col = lax.broadcasted_iota(jnp.int32, (ROWS, 4 * ROWS), 1)
    for b in range(2):
        mine = z_ref[b * ROWS : (b + 1) * ROWS]
        logits = t * lax.dot_general(
            mine, others[b], (((1,), (1,)), ((), ())), preferred_element_type=F32
        ) + bias
        prob = jax.nn.sigmoid(logits) - jnp.where(row == col, 1.0, 0.0)
        weight = (prob * (1.0 / ROWS)).astype(BF)
        dz = t * jnp.dot(weight, others[b], preferred_element_type=F32)
        u = u_ref[b * ROWS : (b + 1) * ROWS]
        rn = rn_ref[b * ROWS : (b + 1) * ROWS, :1]
        inner = jnp.sum(u * dz, axis=-1, keepdims=True)
        dx = ((dz - u * inner) * rn).astype(BF)
        for cols, dx_ref in zip(HALVES, (dx_left, dx_right)):
            dx_ref[b * ROWS : (b + 1) * ROWS] = dx[:, cols]


def pairs(flags, scale, z, *rest):
    rows = 2 * ROWS
    return pl.pallas_call(
        pairs_kernel,
        name="pairs",
        out_shape=(
            jax.ShapeDtypeStruct((rows, LEFT), BF),
            jax.ShapeDtypeStruct((rows, D - LEFT), BF),
        ),
        in_specs=[SMEM, SMEM] + [VMEM] * 3 + [ANY] * 10,
        out_specs=(VMEM, VMEM),
        scratch_shapes=[
            pltpu.VMEM((2, 4 * ROWS, D), BF),
            pltpu.SemaphoreType.DMA((8,)),
        ],
        compiler_params=PARAMS,
        cost_estimate=pl.CostEstimate(
            flops=16 * rows * ROWS * D, bytes_accessed=14 * rows * D, transcendentals=rows * 512
        ),
    )(flags, scale, z, *rest)


def near_kernel(ft, feats_end, feats_mid, *refs):
    inner_ref, outer_ref = refs[6:]
    for cols, dx, dx_end, dx_mid in zip(HALVES, refs[:2], refs[2:4], refs[4:6]):
        dx_own = dx[...]
        dx_other = dx_mid[...]
        inner_ref[:, cols] = (
            jnp.dot(ft[CHIP : 2 * CHIP], dx_own, preferred_element_type=F32)
            + jnp.dot(feats_end[:CHIP], dx_end[...], preferred_element_type=F32)
            + jnp.dot(feats_mid[:CHIP], dx_other, preferred_element_type=F32)
        )
        outer_ref[:, cols] = jnp.dot(
            ft[:CHIP], dx_own, preferred_element_type=F32
        ) + jnp.dot(feats_mid[CHIP:], dx_other, preferred_element_type=F32)


def near(ft, feats_end, feats_mid, *dxs):
    return pl.pallas_call(
        near_kernel,
        name="near",
        out_shape=(
            jax.ShapeDtypeStruct((CHIP, D), F32),
            jax.ShapeDtypeStruct((CHIP, D), F32),
        ),
        in_specs=[VMEM] * 9,
        out_specs=(VMEM, VMEM),
        compiler_params=PARAMS,
        cost_estimate=pl.CostEstimate(
            flops=20 * CHIP * ROWS * D, bytes_accessed=14 * CHIP * D, transcendentals=0
        ),
    )(ft, feats_end, feats_mid, *dxs)


def far_kernel(half, flags, outer_ref, feats, dx, *refs):
    same, crossed, part = refs[-3:]
    c = flags[0]
    part[...] = outer_ref[:, HALVES[half]] + jnp.dot(
        feats[CHIP:], dx[...], preferred_element_type=F32
    )
    mine = pl.ds(pl.multiple_of(c * CORE, CORE), CORE)
    theirs = pl.ds(pl.multiple_of((1 - c) * CORE, CORE), CORE)
    same[...] = part[mine].astype(BF)
    crossed[...] = part[theirs].astype(BF)


def far(half, flags, outer, feats, dx, *after):
    cols = dx.shape[1]
    return pl.pallas_call(
        functools.partial(far_kernel, half),
        name="far",
        out_shape=(
            jax.ShapeDtypeStruct((CORE, cols), BF),
            jax.ShapeDtypeStruct((CORE, cols), BF),
            jax.ShapeDtypeStruct((CHIP, cols), F32),
        ),
        in_specs=[SMEM] + [VMEM] * 3 + [ANY] * len(after),
        out_specs=(VMEM,) * 3,
        compiler_params=PARAMS,
        cost_estimate=pl.CostEstimate(
            flops=4 * CHIP * ROWS * cols, bytes_accessed=14 * CHIP * cols, transcendentals=0
        ),
    )(flags, outer, feats, dx, *after)


def rest_kernel(
    flags, inner_ref, feats, dx_left, dx_right, part_left, part_right,
    keep, swap_left, swap_right, total,
):
    c = flags[0]
    mine = pl.ds(pl.multiple_of(c * CORE, CORE), CORE)
    theirs = pl.ds(pl.multiple_of((1 - c) * CORE, CORE), CORE)

    @pl.when(flags[4] == 1)
    def _():
        for cols, dx in zip(HALVES, (dx_left, dx_right)):
            total[:, cols] = inner_ref[:, cols] + jnp.dot(
                feats[:CHIP], dx[...], preferred_element_type=F32
            )
        keep[...] = total[mine]
        swap_left[...] = total[theirs, :LEFT].astype(BF)
        swap_right[...] = total[theirs, LEFT:].astype(BF)

    @pl.when(flags[4] == 0)
    def _():
        for cols, part, swap in zip(
            HALVES, (part_left, part_right), (swap_left, swap_right)
        ):
            keep[:, cols] = part[mine]
            swap[...] = part[theirs].astype(BF)


def rest(flags, *parts):
    return pl.pallas_call(
        rest_kernel,
        name="rest",
        out_shape=(
            jax.ShapeDtypeStruct((CORE, D), F32),
            jax.ShapeDtypeStruct((CORE, LEFT), BF),
            jax.ShapeDtypeStruct((CORE, D - LEFT), BF),
        ),
        in_specs=[SMEM] + [VMEM] * 6,
        out_specs=(VMEM,) * 3,
        scratch_shapes=[pltpu.VMEM((CHIP, D), F32)],
        compiler_params=PARAMS,
        cost_estimate=pl.CostEstimate(
            flops=4 * CHIP * ROWS * D, bytes_accessed=14 * CHIP * D, transcendentals=0
        ),
    )(flags, *parts)


def finish_kernel(
    flags, same_left, crossed_left, same_right, crossed_right, swap_left, swap_right, keep,
    image_ref, text_ref,
):
    def put(own_ref, other_ref):
        for cols, same, crossed, swap in (
            (HALVES[0], same_left, crossed_left, swap_left),
            (HALVES[1], same_right, crossed_right, swap_right),
        ):
            own_ref[0, :, cols] = keep[:, cols] + same[...].astype(F32)
            other_ref[0, :, cols] = swap[...].astype(F32) + crossed[...].astype(F32)

    @pl.when(flags[0] == 0)
    def _():
        put(image_ref, text_ref)

    @pl.when(flags[0] == 1)
    def _():
        put(text_ref, image_ref)


def finish(flags, *parts):
    shape = jax.ShapeDtypeStruct((1, CORE, D), F32)
    return pl.pallas_call(
        finish_kernel,
        name="finish",
        out_shape=(shape, shape),
        in_specs=[SMEM] + [VMEM] * 7,
        out_specs=(VMEM, VMEM),
        compiler_params=PARAMS,
        cost_estimate=pl.CostEstimate(
            flops=4 * CORE * D, bytes_accessed=18 * CORE * D, transcendentals=0
        ),
    )(flags, *parts)


def on_device(pictures, captions, picture_head, caption_head, sharpness, shift_term):
    c = lax.axis_index("c")
    y = lax.axis_index("y")
    zl = lax.axis_index("zl")
    yy = jnp.where(c == 0, y, 7 - y)
    flags = jnp.stack([c, yy, zl, zl >= 2, (zl == 1) | (zl == 2)]).astype(jnp.int32)
    scale = jnp.concatenate([sharpness, shift_term])

    received = send(jnp.where(c == 0, captions, pictures), other_core)
    own = jnp.where(c == 0, pictures, captions)
    z, u, rn = project(flags, own, received, picture_head, caption_head)

    one = send(z, first_hop)
    cross_one = send(z, first_crossing)
    ft = turn(flags, own, received)
    one, ft = lax.optimization_barrier((one, ft))
    two = send(one, second_hop)
    cross_two = send(one, second_crossing)
    ft_end = send(ft[CHIP:], inward)
    ft_mid = send(ft[2 * CHIP :], middle)
    near_one = send(cross_one, from_near)
    afar_one = send(cross_one, from_afar)
    ft_far = send(ft_end[CHIP:], middle)
    three = send(choose(flags, two, cross_one, cross_two), third_hop)
    here = send(z, other_core)
    dxs = pairs(
        flags, scale, z, u, rn, here, one, two, three,
        cross_one, cross_two, near_one, afar_one, ft_mid, ft_far,
    )

    ends = [send(dx, inward) for dx in dxs]
    mids = [send(dx, middle) for dx in dxs]
    inner, outer = near(ft, ft_end, ft_mid, *dxs, *ends, *mids)
    right, inner = lax.optimization_barrier((ends[1], inner))
    fars = [send(ends[0], middle), send(right, middle)]
    same_left, crossed_left, part_left = far(0, flags, outer, ft_far, fars[0])
    same_left = send(same_left, outward)
    crossed_left = send(crossed_left, outward_cross)
    same_right, crossed_right, part_right = far(1, flags, outer, ft_far, fars[1], part_left)
    same_right = send(same_right, outward)
    crossed_right = send(crossed_right, outward_cross)
    keep, *swaps = rest(flags, inner, ft_far, *fars, part_left, part_right)
    swaps, same_left, crossed_left = lax.optimization_barrier(
        (swaps, same_left, crossed_left)
    )
    swaps = [send(swap, other_core) for swap in swaps]
    return finish(
        flags, same_left, crossed_left, same_right, crossed_right, *swaps, keep
    )


def solution(mesh):
    physical = Mesh(mesh.devices.reshape(SIZES), NAMES)
    rows = P(NAMES, None)
    grad = P(("x", "zh", "y"), ("zl", "c"), None)
    return jax.shard_map(
        on_device,
        mesh=physical,
        in_specs=(rows, rows, P(), P(), P(), P()),
        out_specs=(grad, grad),
        check_vma=False,
    )
```

```python
import functools

import jax
import jax.numpy as jnp
from jax import lax
from jax.experimental import pallas as pl
from jax.experimental.pallas import tpu as pltpu
from jax.sharding import Mesh, PartitionSpec as P

NAMES = ("x", "zh", "y", "zl", "c")
NX, NZH, NY, NZL, NC = SIZES = (8, 2, 8, 4, 2)
ROWS = 128
D = 1152
CHIP = 288
CORE = 144
LEFT = 512
HALVES = (slice(0, LEFT), slice(LEFT, D))
EPS = 1e-06
BF = jnp.bfloat16
F32 = jnp.float32
PROJECT_LIMIT = 51
VMEM = pl.BlockSpec(memory_space=pltpu.VMEM)
SMEM = pl.BlockSpec(memory_space=pltpu.SMEM)
ANY = pl.BlockSpec(memory_space=pl.ANY)
HBM = pl.BlockSpec(memory_space=pltpu.HBM)
PARAMS = pltpu.CompilerParams(vmem_limit_bytes=32 * 1024 * 1024)


def index_of(x, zh, y, zl, c):
    return (((x * NZH + zh) * NY + y) * NZL + zl) * NC + c


def pairs_of(rule):
    found = []
    for x in range(NX):
        for zh in range(NZH):
            for y in range(NY):
                for zl in range(NZL):
                    for c in range(NC):
                        target = rule(x, zh, y, zl, c)
                        if target is not None:
                            found.append((index_of(x, zh, y, zl, c), index_of(*target)))
    return found


def send(value, rule):
    return lax.ppermute(value, NAMES, pairs_of(rule))


def other_core(x, zh, y, zl, c):
    return (x, zh, y, zl, 1 - c)


def first_hop(x, zh, y, zl, c):
    if c == 1:
        return (x, zh, y + 1, zl, 0) if y < 7 else None
    return (x, zh, y - 1, zl, 1) if y > 0 else None


def second_hop(x, zh, y, zl, c):
    if not 1 <= y <= 6:
        return None
    return (x, zh, y + 1 if c == 0 else y - 1, zl, c)


def third_hop(x, zh, y, zl, c):
    if c == 0:
        return (x, zh, y + 1, zl, 0) if y < 7 else None
    return (x, zh, y - 1, zl, 1) if y > 0 else None


def above(x, zh, column):
    return (x, 1, column) if zh == 0 else ((x + 1) % NX, 0, column)


def below(x, zh, column):
    return (x, 0, column) if zh == 1 else ((x - 1) % NX, 1, column)


def first_crossing(x, zh, y, zl, c):
    if c == 1 and y in (5, 7):
        return (*above(x, zh, 1 if y == 7 else 5), zl, 0)
    if c == 0 and y in (0, 2):
        return (*below(x, zh, 6 if y == 0 else 2), zl, 1)
    return None


def second_crossing(x, zh, y, zl, c):
    if c == 0 and y == 7:
        return (*above(x, zh, 0), zl, 0)
    if c == 1 and y == 0:
        return (*below(x, zh, 7), zl, 1)
    return None


def from_near(x, zh, y, zl, c):
    if c == 0 and y == 1:
        return (x, zh, 0, zl, 0)
    if c == 1 and y == 6:
        return (x, zh, 7, zl, 1)
    return None


def from_afar(x, zh, y, zl, c):
    if c == 0 and y == 5:
        return (x, zh, 0, zl, 0)
    if c == 1 and y == 2:
        return (x, zh, 7, zl, 1)
    return None


def inward(x, zh, y, zl, c):
    return {0: (x, zh, y, 1, c), 3: (x, zh, y, 2, c)}.get(zl)


def middle(x, zh, y, zl, c):
    return {1: (x, zh, y, 2, c), 2: (x, zh, y, 1, c)}.get(zl)


def inward_far(x, zh, y, zl, c):
    return {0: (x, zh, y, 2, c), 3: (x, zh, y, 1, c)}.get(zl)


def outward(x, zh, y, zl, c):
    return {1: (x, zh, y, 0, c), 2: (x, zh, y, 3, c)}.get(zl)


def outward_cross(x, zh, y, zl, c):
    return {1: (x, zh, y, 0, 1 - c), 2: (x, zh, y, 3, 1 - c)}.get(zl)


def project_kernel(
    flags, own, recv, wp, wc, z_ref, u_ref, rn_ref, f_ref, w_ref, sems
):
    c = flags[0]
    parts = 3
    width = D // parts

    def fetch(head):
        for j in range(parts):
            cols = pl.ds(j * width, width)
            pltpu.make_async_copy(head.at[:, cols], w_ref.at[j], sems.at[j]).start()

    @pl.when(c == 0)
    def _():
        fetch(wp)

    @pl.when(c == 1)
    def _():
        fetch(wc)

    f_ref[:ROWS] = own[...]
    f_ref[ROWS:] = recv[...]
    total = jnp.zeros((2 * ROWS, 1), F32)
    for j in range(parts):
        cols = pl.ds(j * width, width)
        pltpu.make_async_copy(wp.at[:, cols], w_ref.at[j], sems.at[j]).wait()
        x = jnp.dot(f_ref[...], w_ref[j], preferred_element_type=F32)
        u_ref[:, cols] = x
        total = total + jnp.sum(x * x, axis=-1, keepdims=True)
    rn = 1.0 / jnp.sqrt(total + EPS)
    rn_ref[...] = jnp.broadcast_to(rn, (2 * ROWS, 128))
    u = u_ref[...] * rn
    u_ref[...] = u
    z_ref[...] = u.astype(BF)


def project(flags, own, recv, wp, wc):
    rows = 2 * ROWS
    return pl.pallas_call(
        project_kernel,
        name="project",
        out_shape=(
            jax.ShapeDtypeStruct((rows, D), BF),
            jax.ShapeDtypeStruct((rows, D), F32),
            jax.ShapeDtypeStruct((rows, 128), F32),
        ),
        in_specs=[SMEM, VMEM, VMEM, HBM, HBM],
        out_specs=(VMEM,) * 3,
        scratch_shapes=[
            pltpu.VMEM((rows, D), BF),
            pltpu.VMEM((3, D, D // 3), BF),
            pltpu.SemaphoreType.DMA((3,)),
        ],
        compiler_params=pltpu.CompilerParams(vmem_limit_bytes=PROJECT_LIMIT * 1024 * 1024),
        cost_estimate=pl.CostEstimate(
            flops=2 * rows * D * D, bytes_accessed=2 * D * D + 8 * rows * D, transcendentals=0
        ),
    )(flags, own, recv, wp, wc)


def turn_kernel(flags, own, recv, ft_ref, turned):
    mirror = flags[3]
    turned[:, :ROWS] = own[...].T
    turned[:, ROWS:] = recv[...].T
    for j in range(4):
        start = pl.multiple_of(jnp.where(mirror == 1, 3 - j, j) * CHIP, CHIP)
        ft_ref[j * CHIP : (j + 1) * CHIP] = turned[pl.ds(start, CHIP)]


def turn(flags, own, recv):
    return pl.pallas_call(
        turn_kernel,
        name="turn",
        out_shape=jax.ShapeDtypeStruct((D, 2 * ROWS), BF),
        in_specs=[SMEM, VMEM, VMEM],
        out_specs=VMEM,
        scratch_shapes=[pltpu.VMEM((D, 2 * ROWS), BF)],
        compiler_params=PARAMS,
        cost_estimate=pl.CostEstimate(
            flops=0, bytes_accessed=8 * ROWS * D, transcendentals=0
        ),
    )(flags, own, recv)


def choose_kernel(flags, two, cross_one, cross_two, out_ref, sem):
    place = flags[1]

    @pl.when(place == 0)
    def _():
        pltpu.make_async_copy(cross_two, out_ref, sem).start()

    @pl.when(place == 1)
    def _():
        pltpu.make_async_copy(cross_one, out_ref, sem).start()

    @pl.when(place > 1)
    def _():
        pltpu.make_async_copy(two, out_ref, sem).start()

    pltpu.make_async_copy(two, out_ref, sem).wait()


def choose(flags, two, cross_one, cross_two):
    return pl.pallas_call(
        choose_kernel,
        name="choose",
        out_shape=jax.ShapeDtypeStruct((2 * ROWS, D), BF),
        in_specs=[SMEM] + [ANY] * 3,
        out_specs=VMEM,
        scratch_shapes=[pltpu.SemaphoreType.DMA(())],
        compiler_params=PARAMS,
        cost_estimate=pl.CostEstimate(
            flops=0, bytes_accessed=8 * ROWS * D, transcendentals=0
        ),
    )(flags, two, cross_one, cross_two)


def pairs_kernel(
    flags, scale, z_ref, u_ref, rn_ref,
    here, one, two, three, cross_one, cross_two, near_one, afar_one, early_mid, early_far,
    dx_left, dx_right, others, sems,
):
    del early_mid, early_far
    place = flags[1]

    def fetch(source, s):
        for b in range(2):
            pltpu.make_async_copy(
                source.at[pl.ds((1 - b) * ROWS, ROWS)],
                others.at[b, pl.ds(s * ROWS, ROWS)],
                sems.at[2 * s + b],
            ).start()

    fetch(here, 0)

    @pl.when(place > 0)
    def _():
        fetch(one, 1)
        fetch(three, 3)

    @pl.when(place == 0)
    def _():
        fetch(near_one, 1)
        fetch(cross_two, 2)
        fetch(afar_one, 3)

    @pl.when(place == 1)
    def _():
        fetch(cross_one, 2)

    @pl.when(place > 1)
    def _():
        fetch(two, 2)

    t = scale[0]
    bias = scale[1]
    for s in range(4):
        for b in range(2):
            pltpu.make_async_copy(
                here.at[pl.ds(0, ROWS)],
                others.at[b, pl.ds(s * ROWS, ROWS)],
                sems.at[2 * s + b],
            ).wait()
    row = lax.broadcasted_iota(jnp.int32, (ROWS, 4 * ROWS), 0)
    col = lax.broadcasted_iota(jnp.int32, (ROWS, 4 * ROWS), 1)
    for b in range(2):
        mine = z_ref[b * ROWS : (b + 1) * ROWS]
        logits = t * lax.dot_general(
            mine, others[b], (((1,), (1,)), ((), ())), preferred_element_type=F32
        ) + bias
        prob = jax.nn.sigmoid(logits) - jnp.where(row == col, 1.0, 0.0)
        weight = (prob * (1.0 / ROWS)).astype(BF)
        dz = t * jnp.dot(weight, others[b], preferred_element_type=F32)
        u = u_ref[b * ROWS : (b + 1) * ROWS]
        rn = rn_ref[b * ROWS : (b + 1) * ROWS, :1]
        inner = jnp.sum(u * dz, axis=-1, keepdims=True)
        dx = ((dz - u * inner) * rn).astype(BF)
        for cols, dx_ref in zip(HALVES, (dx_left, dx_right)):
            dx_ref[b * ROWS : (b + 1) * ROWS] = dx[:, cols]


def pairs(flags, scale, z, *rest):
    rows = 2 * ROWS
    return pl.pallas_call(
        pairs_kernel,
        name="pairs",
        out_shape=(
            jax.ShapeDtypeStruct((rows, LEFT), BF),
            jax.ShapeDtypeStruct((rows, D - LEFT), BF),
        ),
        in_specs=[SMEM, SMEM] + [VMEM] * 3 + [ANY] * 10,
        out_specs=(VMEM, VMEM),
        scratch_shapes=[
            pltpu.VMEM((2, 4 * ROWS, D), BF),
            pltpu.SemaphoreType.DMA((8,)),
        ],
        compiler_params=PARAMS,
        cost_estimate=pl.CostEstimate(
            flops=16 * rows * ROWS * D, bytes_accessed=14 * rows * D, transcendentals=rows * 512
        ),
    )(flags, scale, z, *rest)


def near_kernel(ft, feats_end, feats_mid, *refs):
    inner_ref, outer_ref = refs[6:]
    for cols, dx, dx_end, dx_mid in zip(HALVES, refs[:2], refs[2:4], refs[4:6]):
        dx_own = dx[...]
        dx_other = dx_mid[...]
        inner_ref[:, cols] = (
            jnp.dot(ft[CHIP : 2 * CHIP], dx_own, preferred_element_type=F32)
            + jnp.dot(feats_end[:CHIP], dx_end[...], preferred_element_type=F32)
            + jnp.dot(feats_mid[:CHIP], dx_other, preferred_element_type=F32)
        )
        outer_ref[:, cols] = jnp.dot(
            ft[:CHIP], dx_own, preferred_element_type=F32
        ) + jnp.dot(feats_mid[CHIP:], dx_other, preferred_element_type=F32)


def near(ft, feats_end, feats_mid, *dxs):
    return pl.pallas_call(
        near_kernel,
        name="near",
        out_shape=(
            jax.ShapeDtypeStruct((CHIP, D), F32),
            jax.ShapeDtypeStruct((CHIP, D), F32),
        ),
        in_specs=[VMEM] * 9,
        out_specs=(VMEM, VMEM),
        compiler_params=PARAMS,
        cost_estimate=pl.CostEstimate(
            flops=20 * CHIP * ROWS * D, bytes_accessed=14 * CHIP * D, transcendentals=0
        ),
    )(ft, feats_end, feats_mid, *dxs)


def far_kernel(half, flags, outer_ref, feats, dx, *refs):
    same, crossed, part = refs[-3:]
    c = flags[0]
    part[...] = outer_ref[:, HALVES[half]] + jnp.dot(
        feats[CHIP:], dx[...], preferred_element_type=F32
    )
    mine = pl.ds(pl.multiple_of(c * CORE, CORE), CORE)
    theirs = pl.ds(pl.multiple_of((1 - c) * CORE, CORE), CORE)
    same[...] = part[mine].astype(BF)
    crossed[...] = part[theirs].astype(BF)


def far(half, flags, outer, feats, dx, *after):
    cols = dx.shape[1]
    return pl.pallas_call(
        functools.partial(far_kernel, half),
        name="far",
        out_shape=(
            jax.ShapeDtypeStruct((CORE, cols), BF),
            jax.ShapeDtypeStruct((CORE, cols), BF),
            jax.ShapeDtypeStruct((CHIP, cols), F32),
        ),
        in_specs=[SMEM] + [VMEM] * 3 + [ANY] * len(after),
        out_specs=(VMEM,) * 3,
        compiler_params=PARAMS,
        cost_estimate=pl.CostEstimate(
            flops=4 * CHIP * ROWS * cols, bytes_accessed=14 * CHIP * cols, transcendentals=0
        ),
    )(flags, outer, feats, dx, *after)


def rest_kernel(
    flags, inner_ref, feats, dx_left, dx_right, part_left, part_right,
    keep, swap_left, swap_right, total,
):
    c = flags[0]
    mine = pl.ds(pl.multiple_of(c * CORE, CORE), CORE)
    theirs = pl.ds(pl.multiple_of((1 - c) * CORE, CORE), CORE)

    @pl.when(flags[4] == 1)
    def _():
        for cols, dx in zip(HALVES, (dx_left, dx_right)):
            total[:, cols] = inner_ref[:, cols] + jnp.dot(
                feats[:CHIP], dx[...], preferred_element_type=F32
            )
        keep[...] = total[mine]
        swap_left[...] = total[theirs, :LEFT].astype(BF)
        swap_right[...] = total[theirs, LEFT:].astype(BF)

    @pl.when(flags[4] == 0)
    def _():
        for cols, part, swap in zip(
            HALVES, (part_left, part_right), (swap_left, swap_right)
        ):
            keep[:, cols] = part[mine]
            swap[...] = part[theirs].astype(BF)


def rest(flags, *parts):
    return pl.pallas_call(
        rest_kernel,
        name="rest",
        out_shape=(
            jax.ShapeDtypeStruct((CORE, D), F32),
            jax.ShapeDtypeStruct((CORE, LEFT), BF),
            jax.ShapeDtypeStruct((CORE, D - LEFT), BF),
        ),
        in_specs=[SMEM] + [VMEM] * 6,
        out_specs=(VMEM,) * 3,
        scratch_shapes=[pltpu.VMEM((CHIP, D), F32)],
        compiler_params=PARAMS,
        cost_estimate=pl.CostEstimate(
            flops=4 * CHIP * ROWS * D, bytes_accessed=14 * CHIP * D, transcendentals=0
        ),
    )(flags, *parts)


def finish_kernel(
    flags, same_left, crossed_left, same_right, crossed_right, swap_left, swap_right, keep,
    image_ref, text_ref,
):
    def put(own_ref, other_ref):
        for cols, same, crossed, swap in (
            (HALVES[0], same_left, crossed_left, swap_left),
            (HALVES[1], same_right, crossed_right, swap_right),
        ):
            own_ref[0, :, cols] = keep[:, cols] + same[...].astype(F32)
            other_ref[0, :, cols] = swap[...].astype(F32) + crossed[...].astype(F32)

    @pl.when(flags[0] == 0)
    def _():
        put(image_ref, text_ref)

    @pl.when(flags[0] == 1)
    def _():
        put(text_ref, image_ref)


def finish(flags, *parts):
    shape = jax.ShapeDtypeStruct((1, CORE, D), F32)
    return pl.pallas_call(
        finish_kernel,
        name="finish",
        out_shape=(shape, shape),
        in_specs=[SMEM] + [VMEM] * 7,
        out_specs=(VMEM, VMEM),
        compiler_params=PARAMS,
        cost_estimate=pl.CostEstimate(
            flops=4 * CORE * D, bytes_accessed=18 * CORE * D, transcendentals=0
        ),
    )(flags, *parts)


def on_device(pictures, captions, picture_head, caption_head, sharpness, shift_term):
    c = lax.axis_index("c")
    y = lax.axis_index("y")
    zl = lax.axis_index("zl")
    yy = jnp.where(c == 0, y, 7 - y)
    flags = jnp.stack([c, yy, zl, zl >= 2, (zl == 1) | (zl == 2)]).astype(jnp.int32)
    scale = jnp.concatenate([sharpness, shift_term])

    received = send(jnp.where(c == 0, captions, pictures), other_core)
    own = jnp.where(c == 0, pictures, captions)
    z, u, rn = project(flags, own, received, picture_head, caption_head)

    one = send(z, first_hop)
    cross_one = send(z, first_crossing)
    ft = turn(flags, own, received)
    ft_end = send(ft[CHIP : 2 * CHIP], inward)
    ft_mid = send(ft[2 * CHIP :], middle)
    ft_far = send(ft[2 * CHIP :], inward_far)
    one, ft_end = lax.optimization_barrier((one, ft_end))
    two = send(one, second_hop)
    cross_two = send(one, second_crossing)
    near_one = send(cross_one, from_near)
    afar_one = send(cross_one, from_afar)
    two, ft_mid = lax.optimization_barrier((two, ft_mid))
    three = send(choose(flags, two, cross_one, cross_two), third_hop)
    here = send(z, other_core)
    dxs = pairs(
        flags, scale, z, u, rn, here, one, two, three,
        cross_one, cross_two, near_one, afar_one, ft_mid, ft_far,
    )

    ends = [send(dx, inward) for dx in dxs]
    mids = [send(dx, middle) for dx in dxs]
    inner, outer = near(ft, ft_end, ft_mid, *dxs, *ends, *mids)
    right, inner = lax.optimization_barrier((ends[1], inner))
    fars = [send(ends[0], middle), send(right, middle)]
    same_left, crossed_left, part_left = far(0, flags, outer, ft_far, fars[0])
    same_left = send(same_left, outward)
    crossed_left = send(crossed_left, outward_cross)
    same_right, crossed_right, part_right = far(1, flags, outer, ft_far, fars[1], part_left)
    same_right = send(same_right, outward)
    crossed_right = send(crossed_right, outward_cross)
    keep, *swaps = rest(flags, inner, ft_far, *fars, part_left, part_right)
    swaps, same_left, crossed_left = lax.optimization_barrier(
        (swaps, same_left, crossed_left)
    )
    swaps = [send(swap, other_core) for swap in swaps]
    return finish(
        flags, same_left, crossed_left, same_right, crossed_right, *swaps, keep
    )


def solution(mesh):
    physical = Mesh(mesh.devices.reshape(SIZES), NAMES)
    rows = P(NAMES, None)
    grad = P(("x", "zh", "y"), ("zl", "c"), None)
    return jax.shard_map(
        on_device,
        mesh=physical,
        in_specs=(rows, rows, P(), P(), P(), P()),
        out_specs=(grad, grad),
        check_vma=False,
    )
```

```python
import functools

import jax
import jax.numpy as jnp
from jax import lax
from jax.experimental import pallas as pl
from jax.experimental.pallas import tpu as pltpu
from jax.sharding import Mesh, PartitionSpec as P

NAMES = ("x", "zh", "y", "zl", "c")
NX, NZH, NY, NZL, NC = SIZES = (8, 2, 8, 4, 2)
ROWS = 128
D = 1152
CHIP = 288
CORE = 144
LEFT = 512
HALVES = (slice(0, LEFT), slice(LEFT, D))
EPS = 1e-06
BF = jnp.bfloat16
F32 = jnp.float32
PROJECT_LIMIT = 49
VMEM = pl.BlockSpec(memory_space=pltpu.VMEM)
SMEM = pl.BlockSpec(memory_space=pltpu.SMEM)
ANY = pl.BlockSpec(memory_space=pl.ANY)
HBM = pl.BlockSpec(memory_space=pltpu.HBM)
PARAMS = pltpu.CompilerParams(vmem_limit_bytes=32 * 1024 * 1024)


def index_of(x, zh, y, zl, c):
    return (((x * NZH + zh) * NY + y) * NZL + zl) * NC + c


def pairs_of(rule):
    found = []
    for x in range(NX):
        for zh in range(NZH):
            for y in range(NY):
                for zl in range(NZL):
                    for c in range(NC):
                        target = rule(x, zh, y, zl, c)
                        if target is not None:
                            found.append((index_of(x, zh, y, zl, c), index_of(*target)))
    return found


def send(value, rule):
    return lax.ppermute(value, NAMES, pairs_of(rule))


def other_core(x, zh, y, zl, c):
    return (x, zh, y, zl, 1 - c)


def first_hop(x, zh, y, zl, c):
    if c == 1:
        return (x, zh, y + 1, zl, 0) if y < 7 else None
    return (x, zh, y - 1, zl, 1) if y > 0 else None


def second_hop(x, zh, y, zl, c):
    if not 1 <= y <= 6:
        return None
    return (x, zh, y + 1 if c == 0 else y - 1, zl, c)


def third_hop(x, zh, y, zl, c):
    if c == 0:
        return (x, zh, y + 1, zl, 0) if y < 7 else None
    return (x, zh, y - 1, zl, 1) if y > 0 else None


def above(x, zh, column):
    return (x, 1, column) if zh == 0 else ((x + 1) % NX, 0, column)


def below(x, zh, column):
    return (x, 0, column) if zh == 1 else ((x - 1) % NX, 1, column)


def crossing(x, zh, y, zl, c):
    if c == 1 and y >= 5:
        return (*above(x, zh, {7: 1, 6: 0, 5: 5}[y]), zl, 0)
    if c == 0 and y <= 2:
        return (*below(x, zh, {0: 6, 1: 7, 2: 2}[y]), zl, 1)
    return None


def from_near(x, zh, y, zl, c):
    if c == 0 and y == 1:
        return (x, zh, 0, zl, 0)
    if c == 1 and y == 6:
        return (x, zh, 7, zl, 1)
    return None


def from_afar(x, zh, y, zl, c):
    if c == 0 and y == 5:
        return (x, zh, 0, zl, 0)
    if c == 1 and y == 2:
        return (x, zh, 7, zl, 1)
    return None


def inward(x, zh, y, zl, c):
    return {0: (x, zh, y, 1, c), 3: (x, zh, y, 2, c)}.get(zl)


def middle(x, zh, y, zl, c):
    return {1: (x, zh, y, 2, c), 2: (x, zh, y, 1, c)}.get(zl)


def inward_far(x, zh, y, zl, c):
    return {0: (x, zh, y, 2, c), 3: (x, zh, y, 1, c)}.get(zl)


def outward(x, zh, y, zl, c):
    return {1: (x, zh, y, 0, c), 2: (x, zh, y, 3, c)}.get(zl)


def outward_cross(x, zh, y, zl, c):
    return {1: (x, zh, y, 0, 1 - c), 2: (x, zh, y, 3, 1 - c)}.get(zl)


def normalised(x):
    total = jnp.sum(x * x, axis=-1, keepdims=True)
    rn = 1.0 / jnp.sqrt(total + EPS)
    return x * rn, jnp.broadcast_to(rn, (ROWS, 128))


def project_own_kernel(flags, own, wp, wc, w_ref, z_ref, u_ref, rn_ref, sems):
    c = flags[0]
    parts = 3
    width = D // parts

    def fetch(head):
        for j in range(parts):
            cols = pl.ds(j * width, width)
            pltpu.make_async_copy(head.at[:, cols], w_ref.at[:, cols], sems.at[j]).start()

    @pl.when(c == 0)
    def _():
        fetch(wp)

    @pl.when(c == 1)
    def _():
        fetch(wc)

    for j in range(parts):
        cols = pl.ds(j * width, width)
        pltpu.make_async_copy(wp.at[:, cols], w_ref.at[:, cols], sems.at[j]).wait()
        u_ref[:, cols] = jnp.dot(own[...], w_ref[:, cols], preferred_element_type=F32)
    u, rn_ref[...] = normalised(u_ref[...])
    u_ref[...] = u
    z_ref[...] = u.astype(BF)


def project_own(flags, own, wp, wc):
    return pl.pallas_call(
        project_own_kernel,
        name="project_own",
        out_shape=(
            jax.ShapeDtypeStruct((D, D), BF),
            jax.ShapeDtypeStruct((ROWS, D), BF),
            jax.ShapeDtypeStruct((ROWS, D), F32),
            jax.ShapeDtypeStruct((ROWS, 128), F32),
        ),
        in_specs=[SMEM, VMEM, HBM, HBM],
        out_specs=(VMEM,) * 4,
        scratch_shapes=[pltpu.SemaphoreType.DMA((3,))],
        compiler_params=pltpu.CompilerParams(vmem_limit_bytes=PROJECT_LIMIT * 1024 * 1024),
        cost_estimate=pl.CostEstimate(
            flops=2 * ROWS * D * D, bytes_accessed=2 * D * D + 8 * ROWS * D, transcendentals=0
        ),
    )(flags, own, wp, wc)


def project_other_kernel(recv, w_ref, z_own, z_ref, u_ref, rn_ref):
    z_ref[:ROWS] = z_own[...]
    u, rn_ref[...] = normalised(
        jnp.dot(recv[...], w_ref[...], preferred_element_type=F32)
    )
    u_ref[...] = u
    z_ref[ROWS:] = u.astype(BF)


def project_other(recv, w, z_own):
    return pl.pallas_call(
        project_other_kernel,
        name="project_other",
        out_shape=(
            jax.ShapeDtypeStruct((2 * ROWS, D), BF),
            jax.ShapeDtypeStruct((ROWS, D), F32),
            jax.ShapeDtypeStruct((ROWS, 128), F32),
        ),
        in_specs=[VMEM] * 3,
        out_specs=(VMEM,) * 3,
        compiler_params=PARAMS,
        cost_estimate=pl.CostEstimate(
            flops=2 * ROWS * D * D, bytes_accessed=2 * D * D + 8 * ROWS * D, transcendentals=0
        ),
    )(recv, w, z_own)


def turn_kernel(flags, own, recv, ft_ref, turned):
    mirror = flags[3]
    turned[:, :ROWS] = own[...].T
    turned[:, ROWS:] = recv[...].T
    for j in range(4):
        start = pl.multiple_of(jnp.where(mirror == 1, 3 - j, j) * CHIP, CHIP)
        ft_ref[j * CHIP : (j + 1) * CHIP] = turned[pl.ds(start, CHIP)]


def turn(flags, own, recv):
    return pl.pallas_call(
        turn_kernel,
        name="turn",
        out_shape=jax.ShapeDtypeStruct((D, 2 * ROWS), BF),
        in_specs=[SMEM, VMEM, VMEM],
        out_specs=VMEM,
        scratch_shapes=[pltpu.VMEM((D, 2 * ROWS), BF)],
        compiler_params=PARAMS,
        cost_estimate=pl.CostEstimate(
            flops=0, bytes_accessed=8 * ROWS * D, transcendentals=0
        ),
    )(flags, own, recv)


def choose_kernel(flags, two, cross, out_ref, sem):
    place = flags[1]

    @pl.when(place <= 1)
    def _():
        pltpu.make_async_copy(cross, out_ref, sem).start()

    @pl.when(place > 1)
    def _():
        pltpu.make_async_copy(two, out_ref, sem).start()

    pltpu.make_async_copy(two, out_ref, sem).wait()


def choose(flags, two, cross):
    return pl.pallas_call(
        choose_kernel,
        name="choose",
        out_shape=jax.ShapeDtypeStruct((2 * ROWS, D), BF),
        in_specs=[SMEM] + [ANY] * 2,
        out_specs=VMEM,
        scratch_shapes=[pltpu.SemaphoreType.DMA(())],
        compiler_params=PARAMS,
        cost_estimate=pl.CostEstimate(
            flops=0, bytes_accessed=8 * ROWS * D, transcendentals=0
        ),
    )(flags, two, cross)


def pairs_kernel(
    flags, scale, z_ref, u_own, u_other, rn_own, rn_other,
    here, one, two, three, cross, near_one, afar_one, early_mid, early_far,
    dx_left, dx_right, others, sems,
):
    del early_mid, early_far
    place = flags[1]

    def fetch(source, s):
        for b in range(2):
            pltpu.make_async_copy(
                source.at[pl.ds((1 - b) * ROWS, ROWS)],
                others.at[b, pl.ds(s * ROWS, ROWS)],
                sems.at[2 * s + b],
            ).start()

    fetch(here, 0)

    @pl.when(place > 0)
    def _():
        fetch(one, 1)
        fetch(three, 3)

    @pl.when(place == 0)
    def _():
        fetch(near_one, 1)
        fetch(afar_one, 3)

    @pl.when(place <= 1)
    def _():
        fetch(cross, 2)

    @pl.when(place > 1)
    def _():
        fetch(two, 2)

    t = scale[0]
    bias = scale[1]
    for s in range(4):
        for b in range(2):
            pltpu.make_async_copy(
                here.at[pl.ds(0, ROWS)],
                others.at[b, pl.ds(s * ROWS, ROWS)],
                sems.at[2 * s + b],
            ).wait()
    row = lax.broadcasted_iota(jnp.int32, (ROWS, 4 * ROWS), 0)
    col = lax.broadcasted_iota(jnp.int32, (ROWS, 4 * ROWS), 1)
    for b in range(2):
        mine = z_ref[b * ROWS : (b + 1) * ROWS]
        logits = t * lax.dot_general(
            mine, others[b], (((1,), (1,)), ((), ())), preferred_element_type=F32
        ) + bias
        prob = jax.nn.sigmoid(logits) - jnp.where(row == col, 1.0, 0.0)
        weight = (prob * (1.0 / ROWS)).astype(BF)
        dz = t * jnp.dot(weight, others[b], preferred_element_type=F32)
        u = (u_own, u_other)[b][...]
        rn = (rn_own, rn_other)[b][:, :1]
        inner = jnp.sum(u * dz, axis=-1, keepdims=True)
        dx = ((dz - u * inner) * rn).astype(BF)
        for cols, dx_ref in zip(HALVES, (dx_left, dx_right)):
            dx_ref[b * ROWS : (b + 1) * ROWS] = dx[:, cols]


def pairs(flags, scale, z, *rest):
    rows = 2 * ROWS
    return pl.pallas_call(
        pairs_kernel,
        name="pairs",
        out_shape=(
            jax.ShapeDtypeStruct((rows, LEFT), BF),
            jax.ShapeDtypeStruct((rows, D - LEFT), BF),
        ),
        in_specs=[SMEM, SMEM] + [VMEM] * 5 + [ANY] * 9,
        out_specs=(VMEM, VMEM),
        scratch_shapes=[
            pltpu.VMEM((2, 4 * ROWS, D), BF),
            pltpu.SemaphoreType.DMA((8,)),
        ],
        compiler_params=PARAMS,
        cost_estimate=pl.CostEstimate(
            flops=16 * rows * ROWS * D, bytes_accessed=14 * rows * D, transcendentals=rows * 512
        ),
    )(flags, scale, z, *rest)


def near_kernel(ft, feats_end, feats_mid, *refs):
    inner_ref, outer_ref = refs[6:]
    for cols, dx, dx_end, dx_mid in zip(HALVES, refs[:2], refs[2:4], refs[4:6]):
        dx_own = dx[...]
        dx_other = dx_mid[...]
        inner_ref[:, cols] = (
            jnp.dot(ft[CHIP : 2 * CHIP], dx_own, preferred_element_type=F32)
            + jnp.dot(feats_end[:CHIP], dx_end[...], preferred_element_type=F32)
            + jnp.dot(feats_mid[:CHIP], dx_other, preferred_element_type=F32)
        )
        outer_ref[:, cols] = jnp.dot(
            ft[:CHIP], dx_own, preferred_element_type=F32
        ) + jnp.dot(feats_mid[CHIP:], dx_other, preferred_element_type=F32)


def near(ft, feats_end, feats_mid, *dxs):
    return pl.pallas_call(
        near_kernel,
        name="near",
        out_shape=(
            jax.ShapeDtypeStruct((CHIP, D), F32),
            jax.ShapeDtypeStruct((CHIP, D), F32),
        ),
        in_specs=[VMEM] * 9,
        out_specs=(VMEM, VMEM),
        compiler_params=PARAMS,
        cost_estimate=pl.CostEstimate(
            flops=20 * CHIP * ROWS * D, bytes_accessed=14 * CHIP * D, transcendentals=0
        ),
    )(ft, feats_end, feats_mid, *dxs)


def far_kernel(half, flags, outer_ref, feats, dx, *refs):
    same, crossed, part = refs[-3:]
    c = flags[0]
    part[...] = outer_ref[:, HALVES[half]] + jnp.dot(
        feats[CHIP:], dx[...], preferred_element_type=F32
    )
    mine = pl.ds(pl.multiple_of(c * CORE, CORE), CORE)
    theirs = pl.ds(pl.multiple_of((1 - c) * CORE, CORE), CORE)
    same[...] = part[mine].astype(BF)
    crossed[...] = part[theirs].astype(BF)


def far(half, flags, outer, feats, dx, *after):
    cols = dx.shape[1]
    return pl.pallas_call(
        functools.partial(far_kernel, half),
        name="far",
        out_shape=(
            jax.ShapeDtypeStruct((CORE, cols), BF),
            jax.ShapeDtypeStruct((CORE, cols), BF),
            jax.ShapeDtypeStruct((CHIP, cols), F32),
        ),
        in_specs=[SMEM] + [VMEM] * 3 + [ANY] * len(after),
        out_specs=(VMEM,) * 3,
        compiler_params=PARAMS,
        cost_estimate=pl.CostEstimate(
            flops=4 * CHIP * ROWS * cols, bytes_accessed=14 * CHIP * cols, transcendentals=0
        ),
    )(flags, outer, feats, dx, *after)


def rest_kernel(
    flags, inner_ref, feats, dx_left, dx_right, part_left, part_right,
    keep, swap_left, swap_right, total,
):
    c = flags[0]
    mine = pl.ds(pl.multiple_of(c * CORE, CORE), CORE)
    theirs = pl.ds(pl.multiple_of((1 - c) * CORE, CORE), CORE)

    @pl.when(flags[4] == 1)
    def _():
        for cols, dx in zip(HALVES, (dx_left, dx_right)):
            total[:, cols] = inner_ref[:, cols] + jnp.dot(
                feats[:CHIP], dx[...], preferred_element_type=F32
            )
        keep[...] = total[mine]
        swap_left[...] = total[theirs, :LEFT].astype(BF)
        swap_right[...] = total[theirs, LEFT:].astype(BF)

    @pl.when(flags[4] == 0)
    def _():
        for cols, part, swap in zip(
            HALVES, (part_left, part_right), (swap_left, swap_right)
        ):
            keep[:, cols] = part[mine]
            swap[...] = part[theirs].astype(BF)


def rest(flags, *parts):
    return pl.pallas_call(
        rest_kernel,
        name="rest",
        out_shape=(
            jax.ShapeDtypeStruct((CORE, D), F32),
            jax.ShapeDtypeStruct((CORE, LEFT), BF),
            jax.ShapeDtypeStruct((CORE, D - LEFT), BF),
        ),
        in_specs=[SMEM] + [VMEM] * 6,
        out_specs=(VMEM,) * 3,
        scratch_shapes=[pltpu.VMEM((CHIP, D), F32)],
        compiler_params=PARAMS,
        cost_estimate=pl.CostEstimate(
            flops=4 * CHIP * ROWS * D, bytes_accessed=14 * CHIP * D, transcendentals=0
        ),
    )(flags, *parts)


def finish_kernel(
    flags, same_left, crossed_left, same_right, crossed_right, swap_left, swap_right, keep,
    image_ref, text_ref,
):
    def put(own_ref, other_ref):
        for cols, same, crossed, swap in (
            (HALVES[0], same_left, crossed_left, swap_left),
            (HALVES[1], same_right, crossed_right, swap_right),
        ):
            own_ref[0, :, cols] = keep[:, cols] + same[...].astype(F32)
            other_ref[0, :, cols] = swap[...].astype(F32) + crossed[...].astype(F32)

    @pl.when(flags[0] == 0)
    def _():
        put(image_ref, text_ref)

    @pl.when(flags[0] == 1)
    def _():
        put(text_ref, image_ref)


def finish(flags, *parts):
    shape = jax.ShapeDtypeStruct((1, CORE, D), F32)
    return pl.pallas_call(
        finish_kernel,
        name="finish",
        out_shape=(shape, shape),
        in_specs=[SMEM] + [VMEM] * 7,
        out_specs=(VMEM, VMEM),
        compiler_params=PARAMS,
        cost_estimate=pl.CostEstimate(
            flops=4 * CORE * D, bytes_accessed=18 * CORE * D, transcendentals=0
        ),
    )(flags, *parts)


def on_device(pictures, captions, picture_head, caption_head, sharpness, shift_term):
    c = lax.axis_index("c")
    y = lax.axis_index("y")
    zl = lax.axis_index("zl")
    yy = jnp.where(c == 0, y, 7 - y)
    flags = jnp.stack([c, yy, zl, zl >= 2, (zl == 1) | (zl == 2)]).astype(jnp.int32)
    scale = jnp.concatenate([sharpness, shift_term])

    received = send(jnp.where(c == 0, captions, pictures), other_core)
    own = jnp.where(c == 0, pictures, captions)
    head, z_own, u_own, rn_own = project_own(flags, own, picture_head, caption_head)
    z, u_other, rn_other = project_other(received, head, z_own)

    one = send(z, first_hop)
    cross = send(z, crossing)
    ft = turn(flags, own, received)
    ft_end = send(ft[CHIP : 2 * CHIP], inward)
    ft_mid = send(ft[2 * CHIP :], middle)
    ft_far = send(ft[2 * CHIP :], inward_far)
    one, ft_end = lax.optimization_barrier((one, ft_end))
    two = send(one, second_hop)
    near_one = send(cross, from_near)
    afar_one = send(cross, from_afar)
    two, ft_far = lax.optimization_barrier((two, ft_far))
    three = send(choose(flags, two, cross), third_hop)
    here = send(z, other_core)
    dxs = pairs(
        flags, scale, z, u_own, u_other, rn_own, rn_other, here, one, two, three,
        cross, near_one, afar_one, ft_mid, ft_far,
    )

    ends = [send(dx, inward) for dx in dxs]
    mids = [send(dx, middle) for dx in dxs]
    inner, outer = near(ft, ft_end, ft_mid, *dxs, *ends, *mids)
    right, inner = lax.optimization_barrier((ends[1], inner))
    fars = [send(ends[0], middle), send(right, middle)]
    same_left, crossed_left, part_left = far(0, flags, outer, ft_far, fars[0])
    same_left = send(same_left, outward)
    crossed_left = send(crossed_left, outward_cross)
    same_right, crossed_right, part_right = far(1, flags, outer, ft_far, fars[1], part_left)
    same_right = send(same_right, outward)
    crossed_right = send(crossed_right, outward_cross)
    keep, *swaps = rest(flags, inner, ft_far, *fars, part_left, part_right)
    swaps, same_left, crossed_left = lax.optimization_barrier(
        (swaps, same_left, crossed_left)
    )
    swaps = [send(swap, other_core) for swap in swaps]
    return finish(
        flags, same_left, crossed_left, same_right, crossed_right, *swaps, keep
    )


def solution(mesh):
    physical = Mesh(mesh.devices.reshape(SIZES), NAMES)
    rows = P(NAMES, None)
    grad = P(("x", "zh", "y"), ("zl", "c"), None)
    return jax.shard_map(
        on_device,
        mesh=physical,
        in_specs=(rows, rows, P(), P(), P(), P()),
        out_specs=(grad, grad),
        check_vma=False,
    )
```

```python
import functools

import jax
import jax.numpy as jnp
from jax import lax
from jax.experimental import pallas as pl
from jax.experimental.pallas import tpu as pltpu
from jax.sharding import Mesh, PartitionSpec as P

NAMES = ("x", "zh", "y", "zl", "c")
NX, NZH, NY, NZL, NC = SIZES = (8, 2, 8, 4, 2)
ROWS = 128
D = 1152
CHIP = 288
CORE = 144
LEFT = 512
HALVES = (slice(0, LEFT), slice(LEFT, D))
EPS = 1e-06
BF = jnp.bfloat16
F32 = jnp.float32
PROJECT_LIMIT = 49
VMEM = pl.BlockSpec(memory_space=pltpu.VMEM)
SMEM = pl.BlockSpec(memory_space=pltpu.SMEM)
ANY = pl.BlockSpec(memory_space=pl.ANY)
HBM = pl.BlockSpec(memory_space=pltpu.HBM)
PARAMS = pltpu.CompilerParams(vmem_limit_bytes=32 * 1024 * 1024)


def index_of(x, zh, y, zl, c):
    return (((x * NZH + zh) * NY + y) * NZL + zl) * NC + c


def pairs_of(rule):
    found = []
    for x in range(NX):
        for zh in range(NZH):
            for y in range(NY):
                for zl in range(NZL):
                    for c in range(NC):
                        target = rule(x, zh, y, zl, c)
                        if target is not None:
                            found.append((index_of(x, zh, y, zl, c), index_of(*target)))
    return found


def send(value, rule):
    return lax.ppermute(value, NAMES, pairs_of(rule))


def other_core(x, zh, y, zl, c):
    return (x, zh, y, zl, 1 - c)


def first_hop(x, zh, y, zl, c):
    if c == 1:
        return (x, zh, y + 1, zl, 0) if y < 7 else None
    return (x, zh, y - 1, zl, 1) if y > 0 else None


def second_hop(x, zh, y, zl, c):
    if not 1 <= y <= 6:
        return None
    return (x, zh, y + 1 if c == 0 else y - 1, zl, c)


def third_hop(x, zh, y, zl, c):
    if c == 0:
        return (x, zh, y + 1, zl, 0) if y < 7 else None
    return (x, zh, y - 1, zl, 1) if y > 0 else None


def above(x, zh, column):
    return (x, 1, column) if zh == 0 else ((x + 1) % NX, 0, column)


def below(x, zh, column):
    return (x, 0, column) if zh == 1 else ((x - 1) % NX, 1, column)


def first_crossing(x, zh, y, zl, c):
    if c == 1 and y >= 6:
        return (*above(x, zh, y - 6), zl, 0)
    if c == 0 and y <= 1:
        return (*below(x, zh, 6 + y), zl, 1)
    return None


def second_crossing(x, zh, y, zl, c):
    if c == 0 and y == 6:
        return (*above(x, zh, 0), zl, 0)
    if c == 1 and y == 1:
        return (*below(x, zh, 7), zl, 1)
    return None


def from_near(x, zh, y, zl, c):
    if c == 0 and y == 1:
        return (x, zh, 0, zl, 0)
    if c == 1 and y == 6:
        return (x, zh, 7, zl, 1)
    return None


def inward(x, zh, y, zl, c):
    return {0: (x, zh, y, 1, c), 3: (x, zh, y, 2, c)}.get(zl)


def middle(x, zh, y, zl, c):
    return {1: (x, zh, y, 2, c), 2: (x, zh, y, 1, c)}.get(zl)


def inward_far(x, zh, y, zl, c):
    return {0: (x, zh, y, 2, c), 3: (x, zh, y, 1, c)}.get(zl)


def outward(x, zh, y, zl, c):
    return {1: (x, zh, y, 0, c), 2: (x, zh, y, 3, c)}.get(zl)


def outward_cross(x, zh, y, zl, c):
    return {1: (x, zh, y, 0, 1 - c), 2: (x, zh, y, 3, 1 - c)}.get(zl)


def normalised(x):
    total = jnp.sum(x * x, axis=-1, keepdims=True)
    rn = 1.0 / jnp.sqrt(total + EPS)
    return x * rn, jnp.broadcast_to(rn, (ROWS, 128))


def project_own_kernel(flags, own, wp, wc, w_ref, z_ref, u_ref, rn_ref, sems):
    c = flags[0]
    parts = 3
    width = D // parts

    def fetch(head):
        for j in range(parts):
            cols = pl.ds(j * width, width)
            pltpu.make_async_copy(head.at[:, cols], w_ref.at[:, cols], sems.at[j]).start()

    @pl.when(c == 0)
    def _():
        fetch(wp)

    @pl.when(c == 1)
    def _():
        fetch(wc)

    for j in range(parts):
        cols = pl.ds(j * width, width)
        pltpu.make_async_copy(wp.at[:, cols], w_ref.at[:, cols], sems.at[j]).wait()
        u_ref[:, cols] = jnp.dot(own[...], w_ref[:, cols], preferred_element_type=F32)
    u, rn_ref[...] = normalised(u_ref[...])
    u_ref[...] = u
    z_ref[...] = u.astype(BF)


def project_own(flags, own, wp, wc):
    return pl.pallas_call(
        project_own_kernel,
        name="project_own",
        out_shape=(
            jax.ShapeDtypeStruct((D, D), BF),
            jax.ShapeDtypeStruct((ROWS, D), BF),
            jax.ShapeDtypeStruct((ROWS, D), F32),
            jax.ShapeDtypeStruct((ROWS, 128), F32),
        ),
        in_specs=[SMEM, VMEM, HBM, HBM],
        out_specs=(VMEM,) * 4,
        scratch_shapes=[pltpu.SemaphoreType.DMA((3,))],
        compiler_params=pltpu.CompilerParams(vmem_limit_bytes=PROJECT_LIMIT * 1024 * 1024),
        cost_estimate=pl.CostEstimate(
            flops=2 * ROWS * D * D, bytes_accessed=2 * D * D + 8 * ROWS * D, transcendentals=0
        ),
    )(flags, own, wp, wc)


def project_other_kernel(recv, w_ref, z_own, z_ref, u_ref, rn_ref):
    z_ref[:ROWS] = z_own[...]
    u, rn_ref[...] = normalised(
        jnp.dot(recv[...], w_ref[...], preferred_element_type=F32)
    )
    u_ref[...] = u
    z_ref[ROWS:] = u.astype(BF)


def project_other(recv, w, z_own):
    return pl.pallas_call(
        project_other_kernel,
        name="project_other",
        out_shape=(
            jax.ShapeDtypeStruct((2 * ROWS, D), BF),
            jax.ShapeDtypeStruct((ROWS, D), F32),
            jax.ShapeDtypeStruct((ROWS, 128), F32),
        ),
        in_specs=[VMEM] * 3,
        out_specs=(VMEM,) * 3,
        compiler_params=PARAMS,
        cost_estimate=pl.CostEstimate(
            flops=2 * ROWS * D * D, bytes_accessed=2 * D * D + 8 * ROWS * D, transcendentals=0
        ),
    )(recv, w, z_own)


def turn_kernel(flags, own, recv, ft_ref, turned):
    mirror = flags[3]
    turned[:, :ROWS] = own[...].T
    turned[:, ROWS:] = recv[...].T
    for j in range(4):
        start = pl.multiple_of(jnp.where(mirror == 1, 3 - j, j) * CHIP, CHIP)
        ft_ref[j * CHIP : (j + 1) * CHIP] = turned[pl.ds(start, CHIP)]


def turn(flags, own, recv):
    return pl.pallas_call(
        turn_kernel,
        name="turn",
        out_shape=jax.ShapeDtypeStruct((D, 2 * ROWS), BF),
        in_specs=[SMEM, VMEM, VMEM],
        out_specs=VMEM,
        scratch_shapes=[pltpu.VMEM((D, 2 * ROWS), BF)],
        compiler_params=PARAMS,
        cost_estimate=pl.CostEstimate(
            flops=0, bytes_accessed=8 * ROWS * D, transcendentals=0
        ),
    )(flags, own, recv)


def choose_kernel(flags, two, cross, out_ref, sem):
    place = flags[1]

    @pl.when(place <= 1)
    def _():
        pltpu.make_async_copy(cross, out_ref, sem).start()

    @pl.when(place > 1)
    def _():
        pltpu.make_async_copy(two, out_ref, sem).start()

    pltpu.make_async_copy(two, out_ref, sem).wait()


def choose(flags, two, cross):
    return pl.pallas_call(
        choose_kernel,
        name="choose",
        out_shape=jax.ShapeDtypeStruct((2 * ROWS, D), BF),
        in_specs=[SMEM] + [ANY] * 2,
        out_specs=VMEM,
        scratch_shapes=[pltpu.SemaphoreType.DMA(())],
        compiler_params=PARAMS,
        cost_estimate=pl.CostEstimate(
            flops=0, bytes_accessed=8 * ROWS * D, transcendentals=0
        ),
    )(flags, two, cross)


def pairs_kernel(
    flags, scale, z_ref, u_own, u_other, rn_own, rn_other,
    here, one, two, three, cross, near_one, cross_two, *refs
):
    dx_left, dx_right, others, sems = refs[-4:]
    place = flags[1]

    def fetch(source, s):
        for b in range(2):
            pltpu.make_async_copy(
                source.at[pl.ds((1 - b) * ROWS, ROWS)],
                others.at[b, pl.ds(s * ROWS, ROWS)],
                sems.at[2 * s + b],
            ).start()

    fetch(here, 0)

    @pl.when(place > 0)
    def _():
        fetch(one, 1)
        fetch(three, 3)

    @pl.when(place == 0)
    def _():
        fetch(near_one, 1)
        fetch(cross_two, 3)

    @pl.when(place <= 1)
    def _():
        fetch(cross, 2)

    @pl.when(place > 1)
    def _():
        fetch(two, 2)

    t = scale[0]
    bias = scale[1]
    for s in range(4):
        for b in range(2):
            pltpu.make_async_copy(
                here.at[pl.ds(0, ROWS)],
                others.at[b, pl.ds(s * ROWS, ROWS)],
                sems.at[2 * s + b],
            ).wait()
    row = lax.broadcasted_iota(jnp.int32, (ROWS, 4 * ROWS), 0)
    col = lax.broadcasted_iota(jnp.int32, (ROWS, 4 * ROWS), 1)
    for b in range(2):
        mine = z_ref[b * ROWS : (b + 1) * ROWS]
        logits = t * lax.dot_general(
            mine, others[b], (((1,), (1,)), ((), ())), preferred_element_type=F32
        ) + bias
        prob = jax.nn.sigmoid(logits) - jnp.where(row == col, 1.0, 0.0)
        weight = (prob * (1.0 / ROWS)).astype(BF)
        dz = t * jnp.dot(weight, others[b], preferred_element_type=F32)
        u = (u_own, u_other)[b][...]
        rn = (rn_own, rn_other)[b][:, :1]
        inner = jnp.sum(u * dz, axis=-1, keepdims=True)
        dx = ((dz - u * inner) * rn).astype(BF)
        for cols, dx_ref in zip(HALVES, (dx_left, dx_right)):
            dx_ref[b * ROWS : (b + 1) * ROWS] = dx[:, cols]


def pairs(flags, scale, z, *rest):
    rows = 2 * ROWS
    return pl.pallas_call(
        pairs_kernel,
        name="pairs",
        out_shape=(
            jax.ShapeDtypeStruct((rows, LEFT), BF),
            jax.ShapeDtypeStruct((rows, D - LEFT), BF),
        ),
        in_specs=[SMEM, SMEM] + [VMEM] * 5 + [ANY] * 10,
        out_specs=(VMEM, VMEM),
        scratch_shapes=[
            pltpu.VMEM((2, 4 * ROWS, D), BF),
            pltpu.SemaphoreType.DMA((8,)),
        ],
        compiler_params=PARAMS,
        cost_estimate=pl.CostEstimate(
            flops=16 * rows * ROWS * D, bytes_accessed=14 * rows * D, transcendentals=rows * 512
        ),
    )(flags, scale, z, *rest)


def near_kernel(ft, feats_end, feats_mid, *refs):
    inner_ref, outer_ref = refs[6:]
    for cols, dx, dx_end, dx_mid in zip(HALVES, refs[:2], refs[2:4], refs[4:6]):
        dx_own = dx[...]
        dx_other = dx_mid[...]
        inner_ref[:, cols] = (
            jnp.dot(ft[CHIP : 2 * CHIP], dx_own, preferred_element_type=F32)
            + jnp.dot(feats_end[:CHIP], dx_end[...], preferred_element_type=F32)
            + jnp.dot(feats_mid[:CHIP], dx_other, preferred_element_type=F32)
        )
        outer_ref[:, cols] = jnp.dot(
            ft[:CHIP], dx_own, preferred_element_type=F32
        ) + jnp.dot(feats_mid[CHIP:], dx_other, preferred_element_type=F32)


def near(ft, feats_end, feats_mid, *dxs):
    return pl.pallas_call(
        near_kernel,
        name="near",
        out_shape=(
            jax.ShapeDtypeStruct((CHIP, D), F32),
            jax.ShapeDtypeStruct((CHIP, D), F32),
        ),
        in_specs=[VMEM] * 9,
        out_specs=(VMEM, VMEM),
        compiler_params=PARAMS,
        cost_estimate=pl.CostEstimate(
            flops=20 * CHIP * ROWS * D, bytes_accessed=14 * CHIP * D, transcendentals=0
        ),
    )(ft, feats_end, feats_mid, *dxs)


def far_kernel(half, flags, outer_ref, feats, dx, *refs):
    same, crossed, part = refs[-3:]
    c = flags[0]
    part[...] = outer_ref[:, HALVES[half]] + jnp.dot(
        feats[CHIP:], dx[...], preferred_element_type=F32
    )
    mine = pl.ds(pl.multiple_of(c * CORE, CORE), CORE)
    theirs = pl.ds(pl.multiple_of((1 - c) * CORE, CORE), CORE)
    same[...] = part[mine].astype(BF)
    crossed[...] = part[theirs].astype(BF)


def far(half, flags, outer, feats, dx, *after):
    cols = dx.shape[1]
    return pl.pallas_call(
        functools.partial(far_kernel, half),
        name="far",
        out_shape=(
            jax.ShapeDtypeStruct((CORE, cols), BF),
            jax.ShapeDtypeStruct((CORE, cols), BF),
            jax.ShapeDtypeStruct((CHIP, cols), F32),
        ),
        in_specs=[SMEM] + [VMEM] * 3 + [ANY] * len(after),
        out_specs=(VMEM,) * 3,
        compiler_params=PARAMS,
        cost_estimate=pl.CostEstimate(
            flops=4 * CHIP * ROWS * cols, bytes_accessed=14 * CHIP * cols, transcendentals=0
        ),
    )(flags, outer, feats, dx, *after)


def rest_kernel(
    flags, inner_ref, feats, dx_left, dx_right, part_left, part_right,
    keep, swap_left, swap_right, total,
):
    c = flags[0]
    mine = pl.ds(pl.multiple_of(c * CORE, CORE), CORE)
    theirs = pl.ds(pl.multiple_of((1 - c) * CORE, CORE), CORE)

    @pl.when(flags[4] == 1)
    def _():
        for cols, dx in zip(HALVES, (dx_left, dx_right)):
            total[:, cols] = inner_ref[:, cols] + jnp.dot(
                feats[:CHIP], dx[...], preferred_element_type=F32
            )
        keep[...] = total[mine]
        swap_left[...] = total[theirs, :LEFT].astype(BF)
        swap_right[...] = total[theirs, LEFT:].astype(BF)

    @pl.when(flags[4] == 0)
    def _():
        for cols, part, swap in zip(
            HALVES, (part_left, part_right), (swap_left, swap_right)
        ):
            keep[:, cols] = part[mine]
            swap[...] = part[theirs].astype(BF)


def rest(flags, *parts):
    return pl.pallas_call(
        rest_kernel,
        name="rest",
        out_shape=(
            jax.ShapeDtypeStruct((CORE, D), F32),
            jax.ShapeDtypeStruct((CORE, LEFT), BF),
            jax.ShapeDtypeStruct((CORE, D - LEFT), BF),
        ),
        in_specs=[SMEM] + [VMEM] * 6,
        out_specs=(VMEM,) * 3,
        scratch_shapes=[pltpu.VMEM((CHIP, D), F32)],
        compiler_params=PARAMS,
        cost_estimate=pl.CostEstimate(
            flops=4 * CHIP * ROWS * D, bytes_accessed=14 * CHIP * D, transcendentals=0
        ),
    )(flags, *parts)


def finish_kernel(
    flags, same_left, crossed_left, same_right, crossed_right, swap_left, swap_right, keep,
    image_ref, text_ref,
):
    def put(own_ref, other_ref):
        for cols, same, crossed, swap in (
            (HALVES[0], same_left, crossed_left, swap_left),
            (HALVES[1], same_right, crossed_right, swap_right),
        ):
            own_ref[0, :, cols] = keep[:, cols] + same[...].astype(F32)
            other_ref[0, :, cols] = swap[...].astype(F32) + crossed[...].astype(F32)

    @pl.when(flags[0] == 0)
    def _():
        put(image_ref, text_ref)

    @pl.when(flags[0] == 1)
    def _():
        put(text_ref, image_ref)


def finish(flags, *parts):
    shape = jax.ShapeDtypeStruct((1, CORE, D), F32)
    return pl.pallas_call(
        finish_kernel,
        name="finish",
        out_shape=(shape, shape),
        in_specs=[SMEM] + [VMEM] * 7,
        out_specs=(VMEM, VMEM),
        compiler_params=PARAMS,
        cost_estimate=pl.CostEstimate(
            flops=4 * CORE * D, bytes_accessed=18 * CORE * D, transcendentals=0
        ),
    )(flags, *parts)


def on_device(pictures, captions, picture_head, caption_head, sharpness, shift_term):
    c = lax.axis_index("c")
    y = lax.axis_index("y")
    zl = lax.axis_index("zl")
    yy = jnp.where(c == 0, y, 7 - y)
    flags = jnp.stack([c, yy, zl, zl >= 2, (zl == 1) | (zl == 2)]).astype(jnp.int32)
    scale = jnp.concatenate([sharpness, shift_term])

    received = send(jnp.where(c == 0, captions, pictures), other_core)
    own = jnp.where(c == 0, pictures, captions)
    head, z_own, u_own, rn_own = project_own(flags, own, picture_head, caption_head)
    z, u_other, rn_other = project_other(received, head, z_own)

    one = send(z, first_hop)
    cross = send(z, first_crossing)
    ft = turn(flags, own, received)
    one, ft = lax.optimization_barrier((one, ft))
    ft_end = send(ft[CHIP : 2 * CHIP], inward)
    ft_mid = send(ft[2 * CHIP :], middle)
    ft_far = send(ft[2 * CHIP :], inward_far)
    two = send(one, second_hop)
    cross_two = send(one, second_crossing)
    near_one = send(cross, from_near)
    two, ft_far = lax.optimization_barrier((two, ft_far))
    three = send(choose(flags, two, cross), third_hop)
    here = send(z, other_core)
    dxs = pairs(
        flags, scale, z, u_own, u_other, rn_own, rn_other, here, one, two, three,
        cross, near_one, cross_two, ft_mid, ft_far, ft_end,
    )

    ends = [send(dx, inward) for dx in dxs]
    mids = [send(dx, middle) for dx in dxs]
    inner, outer = near(ft, ft_end, ft_mid, *dxs, *ends, *mids)
    right, inner = lax.optimization_barrier((ends[1], inner))
    fars = [send(ends[0], middle), send(right, middle)]
    same_left, crossed_left, part_left = far(0, flags, outer, ft_far, fars[0])
    same_left = send(same_left, outward)
    crossed_left = send(crossed_left, outward_cross)
    same_right, crossed_right, part_right = far(1, flags, outer, ft_far, fars[1], part_left)
    same_right = send(same_right, outward)
    crossed_right = send(crossed_right, outward_cross)
    keep, *swaps = rest(flags, inner, ft_far, *fars, part_left, part_right)
    swaps, same_left, crossed_left = lax.optimization_barrier(
        (swaps, same_left, crossed_left)
    )
    swaps = [send(swap, other_core) for swap in swaps]
    return finish(
        flags, same_left, crossed_left, same_right, crossed_right, *swaps, keep
    )


def solution(mesh):
    physical = Mesh(mesh.devices.reshape(SIZES), NAMES)
    rows = P(NAMES, None)
    grad = P(("x", "zh", "y"), ("zl", "c"), None)
    return jax.shard_map(
        on_device,
        mesh=physical,
        in_specs=(rows, rows, P(), P(), P(), P()),
        out_specs=(grad, grad),
        check_vma=False,
    )
```

```python
import functools

import jax
import jax.numpy as jnp
from jax import lax
from jax.experimental import pallas as pl
from jax.experimental.pallas import tpu as pltpu
from jax.sharding import Mesh, PartitionSpec as P

NAMES = ("x", "zh", "y", "zl", "c")
NX, NZH, NY, NZL, NC = SIZES = (8, 2, 8, 4, 2)
ROWS = 128
D = 1152
CHIP = 288
CORE = 144
LEFT = 512
HALVES = (slice(0, LEFT), slice(LEFT, D))
EPS = 1e-06
BF = jnp.bfloat16
F32 = jnp.float32
PROJECT_LIMIT = 49
VMEM = pl.BlockSpec(memory_space=pltpu.VMEM)
SMEM = pl.BlockSpec(memory_space=pltpu.SMEM)
ANY = pl.BlockSpec(memory_space=pl.ANY)
HBM = pl.BlockSpec(memory_space=pltpu.HBM)
PARAMS = pltpu.CompilerParams(vmem_limit_bytes=32 * 1024 * 1024)


def index_of(x, zh, y, zl, c):
    return (((x * NZH + zh) * NY + y) * NZL + zl) * NC + c


def pairs_of(rule):
    found = []
    for x in range(NX):
        for zh in range(NZH):
            for y in range(NY):
                for zl in range(NZL):
                    for c in range(NC):
                        target = rule(x, zh, y, zl, c)
                        if target is not None:
                            found.append((index_of(x, zh, y, zl, c), index_of(*target)))
    return found


def send(value, rule):
    return lax.ppermute(value, NAMES, pairs_of(rule))


def other_core(x, zh, y, zl, c):
    return (x, zh, y, zl, 1 - c)


def first_hop(x, zh, y, zl, c):
    if c == 1:
        return (x, zh, y + 1, zl, 0) if y < 7 else None
    return (x, zh, y - 1, zl, 1) if y > 0 else None


def second_hop(x, zh, y, zl, c):
    if not 1 <= y <= 6:
        return None
    return (x, zh, y + 1 if c == 0 else y - 1, zl, c)


def third_hop(x, zh, y, zl, c):
    if c == 0:
        return (x, zh, y + 1, zl, 0) if y < 7 else None
    return (x, zh, y - 1, zl, 1) if y > 0 else None


def above(x, zh, column):
    return (x, 1, column) if zh == 0 else ((x + 1) % NX, 0, column)


def below(x, zh, column):
    return (x, 0, column) if zh == 1 else ((x - 1) % NX, 1, column)


def first_crossing(x, zh, y, zl, c):
    if c == 1 and y >= 6:
        return (*above(x, zh, y - 6), zl, 0)
    if c == 0 and y <= 1:
        return (*below(x, zh, 6 + y), zl, 1)
    return None


def second_crossing(x, zh, y, zl, c):
    if c == 0 and y == 6:
        return (*above(x, zh, 0), zl, 0)
    if c == 1 and y == 1:
        return (*below(x, zh, 7), zl, 1)
    return None


def from_near(x, zh, y, zl, c):
    if c == 0 and y == 1:
        return (x, zh, 0, zl, 0)
    if c == 1 and y == 6:
        return (x, zh, 7, zl, 1)
    return None


def inward(x, zh, y, zl, c):
    return {0: (x, zh, y, 1, c), 3: (x, zh, y, 2, c)}.get(zl)


def middle(x, zh, y, zl, c):
    return {1: (x, zh, y, 2, c), 2: (x, zh, y, 1, c)}.get(zl)


def inward_far(x, zh, y, zl, c):
    return {0: (x, zh, y, 2, c), 3: (x, zh, y, 1, c)}.get(zl)


def outward(x, zh, y, zl, c):
    return {1: (x, zh, y, 0, c), 2: (x, zh, y, 3, c)}.get(zl)


def outward_cross(x, zh, y, zl, c):
    return {1: (x, zh, y, 0, 1 - c), 2: (x, zh, y, 3, 1 - c)}.get(zl)


def normalised(x):
    total = jnp.sum(x * x, axis=-1, keepdims=True)
    rn = 1.0 / jnp.sqrt(total + EPS)
    return x * rn, jnp.broadcast_to(rn, (ROWS, 128))


def project_own_kernel(flags, own, wp, wc, w_ref, z_ref, u_ref, rn_ref, sems):
    c = flags[0]
    parts = 3
    width = D // parts

    def fetch(head):
        for j in range(parts):
            cols = pl.ds(j * width, width)
            pltpu.make_async_copy(head.at[:, cols], w_ref.at[:, cols], sems.at[j]).start()

    @pl.when(c == 0)
    def _():
        fetch(wp)

    @pl.when(c == 1)
    def _():
        fetch(wc)

    for j in range(parts):
        cols = pl.ds(j * width, width)
        pltpu.make_async_copy(wp.at[:, cols], w_ref.at[:, cols], sems.at[j]).wait()
        u_ref[:, cols] = jnp.dot(own[...], w_ref[:, cols], preferred_element_type=F32)
    u, rn_ref[...] = normalised(u_ref[...])
    u_ref[...] = u
    z_ref[...] = u.astype(BF)


def project_own(flags, own, wp, wc):
    return pl.pallas_call(
        project_own_kernel,
        name="project_own",
        out_shape=(
            jax.ShapeDtypeStruct((D, D), BF),
            jax.ShapeDtypeStruct((ROWS, D), BF),
            jax.ShapeDtypeStruct((ROWS, D), F32),
            jax.ShapeDtypeStruct((ROWS, 128), F32),
        ),
        in_specs=[SMEM, VMEM, HBM, HBM],
        out_specs=(VMEM,) * 4,
        scratch_shapes=[pltpu.SemaphoreType.DMA((3,))],
        compiler_params=pltpu.CompilerParams(vmem_limit_bytes=PROJECT_LIMIT * 1024 * 1024),
        cost_estimate=pl.CostEstimate(
            flops=2 * ROWS * D * D, bytes_accessed=2 * D * D + 8 * ROWS * D, transcendentals=0
        ),
    )(flags, own, wp, wc)


def project_other_kernel(recv, w_ref, z_own, z_ref, u_ref, rn_ref):
    z_ref[:ROWS] = z_own[...]
    u, rn_ref[...] = normalised(
        jnp.dot(recv[...], w_ref[...], preferred_element_type=F32)
    )
    u_ref[...] = u
    z_ref[ROWS:] = u.astype(BF)


def project_other(recv, w, z_own):
    return pl.pallas_call(
        project_other_kernel,
        name="project_other",
        out_shape=(
            jax.ShapeDtypeStruct((2 * ROWS, D), BF),
            jax.ShapeDtypeStruct((ROWS, D), F32),
            jax.ShapeDtypeStruct((ROWS, 128), F32),
        ),
        in_specs=[VMEM] * 3,
        out_specs=(VMEM,) * 3,
        compiler_params=PARAMS,
        cost_estimate=pl.CostEstimate(
            flops=2 * ROWS * D * D, bytes_accessed=2 * D * D + 8 * ROWS * D, transcendentals=0
        ),
    )(recv, w, z_own)


def turn_kernel(flags, own, recv, ft_ref, turned):
    mirror = flags[3]
    turned[:, :ROWS] = own[...].T
    turned[:, ROWS:] = recv[...].T
    for j in range(4):
        start = pl.multiple_of(jnp.where(mirror == 1, 3 - j, j) * CHIP, CHIP)
        ft_ref[j * CHIP : (j + 1) * CHIP] = turned[pl.ds(start, CHIP)]


def turn(flags, own, recv):
    return pl.pallas_call(
        turn_kernel,
        name="turn",
        out_shape=jax.ShapeDtypeStruct((D, 2 * ROWS), BF),
        in_specs=[SMEM, VMEM, VMEM],
        out_specs=VMEM,
        scratch_shapes=[pltpu.VMEM((D, 2 * ROWS), BF)],
        compiler_params=PARAMS,
        cost_estimate=pl.CostEstimate(
            flops=0, bytes_accessed=8 * ROWS * D, transcendentals=0
        ),
    )(flags, own, recv)


def choose_kernel(flags, two, cross, out_ref, sem):
    place = flags[1]

    @pl.when(place <= 1)
    def _():
        pltpu.make_async_copy(cross, out_ref, sem).start()

    @pl.when(place > 1)
    def _():
        pltpu.make_async_copy(two, out_ref, sem).start()

    pltpu.make_async_copy(two, out_ref, sem).wait()


def choose(flags, two, cross):
    return pl.pallas_call(
        choose_kernel,
        name="choose",
        out_shape=jax.ShapeDtypeStruct((2 * ROWS, D), BF),
        in_specs=[SMEM] + [ANY] * 2,
        out_specs=VMEM,
        scratch_shapes=[pltpu.SemaphoreType.DMA(())],
        compiler_params=PARAMS,
        cost_estimate=pl.CostEstimate(
            flops=0, bytes_accessed=8 * ROWS * D, transcendentals=0
        ),
    )(flags, two, cross)


def pairs_kernel(
    flags, scale, z_ref, u_own, u_other, rn_own, rn_other,
    here, one, two, three, cross, near_one, cross_two, *refs
):
    dx_left, dx_right, others, sems = refs[-4:]
    place = flags[1]

    def fetch(source, s):
        for b in range(2):
            pltpu.make_async_copy(
                source.at[pl.ds((1 - b) * ROWS, ROWS)],
                others.at[b, pl.ds(s * ROWS, ROWS)],
                sems.at[2 * s + b],
            ).start()

    fetch(here, 0)

    @pl.when(place > 0)
    def _():
        fetch(one, 1)
        fetch(three, 3)

    @pl.when(place == 0)
    def _():
        fetch(near_one, 1)
        fetch(cross_two, 3)

    @pl.when(place <= 1)
    def _():
        fetch(cross, 2)

    @pl.when(place > 1)
    def _():
        fetch(two, 2)

    t = scale[0]
    bias = scale[1]
    for s in range(4):
        for b in range(2):
            pltpu.make_async_copy(
                here.at[pl.ds(0, ROWS)],
                others.at[b, pl.ds(s * ROWS, ROWS)],
                sems.at[2 * s + b],
            ).wait()
    row = lax.broadcasted_iota(jnp.int32, (ROWS, 4 * ROWS), 0)
    col = lax.broadcasted_iota(jnp.int32, (ROWS, 4 * ROWS), 1)
    for b in range(2):
        mine = z_ref[b * ROWS : (b + 1) * ROWS]
        logits = t * lax.dot_general(
            mine, others[b], (((1,), (1,)), ((), ())), preferred_element_type=F32
        ) + bias
        prob = jax.nn.sigmoid(logits) - jnp.where(row == col, 1.0, 0.0)
        weight = (prob * (1.0 / ROWS)).astype(BF)
        dz = t * jnp.dot(weight, others[b], preferred_element_type=F32)
        u = (u_own, u_other)[b][...]
        rn = (rn_own, rn_other)[b][:, :1]
        inner = jnp.sum(u * dz, axis=-1, keepdims=True)
        dx = ((dz - u * inner) * rn).astype(BF)
        for cols, dx_ref in zip(HALVES, (dx_left, dx_right)):
            dx_ref[b * ROWS : (b + 1) * ROWS] = dx[:, cols]


def pairs(flags, scale, z, *rest):
    rows = 2 * ROWS
    return pl.pallas_call(
        pairs_kernel,
        name="pairs",
        out_shape=(
            jax.ShapeDtypeStruct((rows, LEFT), BF),
            jax.ShapeDtypeStruct((rows, D - LEFT), BF),
        ),
        in_specs=[SMEM, SMEM] + [VMEM] * 5 + [ANY] * 10,
        out_specs=(VMEM, VMEM),
        scratch_shapes=[
            pltpu.VMEM((2, 4 * ROWS, D), BF),
            pltpu.SemaphoreType.DMA((8,)),
        ],
        compiler_params=PARAMS,
        cost_estimate=pl.CostEstimate(
            flops=16 * rows * ROWS * D, bytes_accessed=14 * rows * D, transcendentals=rows * 512
        ),
    )(flags, scale, z, *rest)


def near_kernel(ft, feats_end, feats_mid, *refs):
    inner_ref, outer_ref = refs[6:]
    for cols, dx, dx_end, dx_mid in zip(HALVES, refs[:2], refs[2:4], refs[4:6]):
        dx_own = dx[...]
        dx_other = dx_mid[...]
        inner_ref[:, cols] = (
            jnp.dot(ft[CHIP : 2 * CHIP], dx_own, preferred_element_type=F32)
            + jnp.dot(feats_end[:CHIP], dx_end[...], preferred_element_type=F32)
            + jnp.dot(feats_mid[:CHIP], dx_other, preferred_element_type=F32)
        )
        outer_ref[:, cols] = jnp.dot(
            ft[:CHIP], dx_own, preferred_element_type=F32
        ) + jnp.dot(feats_mid[CHIP:], dx_other, preferred_element_type=F32)


def near(ft, feats_end, feats_mid, *dxs):
    return pl.pallas_call(
        near_kernel,
        name="near",
        out_shape=(
            jax.ShapeDtypeStruct((CHIP, D), F32),
            jax.ShapeDtypeStruct((CHIP, D), F32),
        ),
        in_specs=[VMEM] * 9,
        out_specs=(VMEM, VMEM),
        compiler_params=PARAMS,
        cost_estimate=pl.CostEstimate(
            flops=20 * CHIP * ROWS * D, bytes_accessed=14 * CHIP * D, transcendentals=0
        ),
    )(ft, feats_end, feats_mid, *dxs)


def far_kernel(half, flags, outer_ref, feats, dx, *refs):
    same, crossed, part = refs[-3:]
    c = flags[0]
    part[...] = outer_ref[:, HALVES[half]] + jnp.dot(
        feats[CHIP:], dx[...], preferred_element_type=F32
    )
    mine = pl.ds(pl.multiple_of(c * CORE, CORE), CORE)
    theirs = pl.ds(pl.multiple_of((1 - c) * CORE, CORE), CORE)
    same[...] = part[mine].astype(BF)
    crossed[...] = part[theirs].astype(BF)


def far(half, flags, outer, feats, dx, *after):
    cols = dx.shape[1]
    return pl.pallas_call(
        functools.partial(far_kernel, half),
        name="far",
        out_shape=(
            jax.ShapeDtypeStruct((CORE, cols), BF),
            jax.ShapeDtypeStruct((CORE, cols), BF),
            jax.ShapeDtypeStruct((CHIP, cols), F32),
        ),
        in_specs=[SMEM] + [VMEM] * 3 + [ANY] * len(after),
        out_specs=(VMEM,) * 3,
        compiler_params=PARAMS,
        cost_estimate=pl.CostEstimate(
            flops=4 * CHIP * ROWS * cols, bytes_accessed=14 * CHIP * cols, transcendentals=0
        ),
    )(flags, outer, feats, dx, *after)


def rest_kernel(
    flags, inner_ref, feats, dx_left, dx_right, part_left, part_right,
    keep, swap_left, swap_right, total,
):
    c = flags[0]
    mine = pl.ds(pl.multiple_of(c * CORE, CORE), CORE)
    theirs = pl.ds(pl.multiple_of((1 - c) * CORE, CORE), CORE)

    @pl.when(flags[4] == 1)
    def _():
        for cols, dx in zip(HALVES, (dx_left, dx_right)):
            total[:, cols] = inner_ref[:, cols] + jnp.dot(
                feats[:CHIP], dx[...], preferred_element_type=F32
            )
        keep[...] = total[mine]
        swap_left[...] = total[theirs, :LEFT].astype(BF)
        swap_right[...] = total[theirs, LEFT:].astype(BF)

    @pl.when(flags[4] == 0)
    def _():
        for cols, part, swap in zip(
            HALVES, (part_left, part_right), (swap_left, swap_right)
        ):
            keep[:, cols] = part[mine]
            swap[...] = part[theirs].astype(BF)


def rest(flags, *parts):
    return pl.pallas_call(
        rest_kernel,
        name="rest",
        out_shape=(
            jax.ShapeDtypeStruct((CORE, D), F32),
            jax.ShapeDtypeStruct((CORE, LEFT), BF),
            jax.ShapeDtypeStruct((CORE, D - LEFT), BF),
        ),
        in_specs=[SMEM] + [VMEM] * 6,
        out_specs=(VMEM,) * 3,
        scratch_shapes=[pltpu.VMEM((CHIP, D), F32)],
        compiler_params=PARAMS,
        cost_estimate=pl.CostEstimate(
            flops=4 * CHIP * ROWS * D, bytes_accessed=14 * CHIP * D, transcendentals=0
        ),
    )(flags, *parts)


def finish_kernel(
    flags, same_left, crossed_left, same_right, crossed_right, swap_left, swap_right, keep,
    image_ref, text_ref,
):
    def put(own_ref, other_ref):
        for cols, same, crossed, swap in (
            (HALVES[0], same_left, crossed_left, swap_left),
            (HALVES[1], same_right, crossed_right, swap_right),
        ):
            own_ref[0, :, cols] = keep[:, cols] + same[...].astype(F32)
            other_ref[0, :, cols] = swap[...].astype(F32) + crossed[...].astype(F32)

    @pl.when(flags[0] == 0)
    def _():
        put(image_ref, text_ref)

    @pl.when(flags[0] == 1)
    def _():
        put(text_ref, image_ref)


def finish(flags, *parts):
    shape = jax.ShapeDtypeStruct((1, CORE, D), F32)
    return pl.pallas_call(
        finish_kernel,
        name="finish",
        out_shape=(shape, shape),
        in_specs=[SMEM] + [VMEM] * 7,
        out_specs=(VMEM, VMEM),
        compiler_params=PARAMS,
        cost_estimate=pl.CostEstimate(
            flops=4 * CORE * D, bytes_accessed=18 * CORE * D, transcendentals=0
        ),
    )(flags, *parts)


def on_device(pictures, captions, picture_head, caption_head, sharpness, shift_term):
    c = lax.axis_index("c")
    y = lax.axis_index("y")
    zl = lax.axis_index("zl")
    yy = jnp.where(c == 0, y, 7 - y)
    flags = jnp.stack([c, yy, zl, zl >= 2, (zl == 1) | (zl == 2)]).astype(jnp.int32)
    scale = jnp.concatenate([sharpness, shift_term])

    received = send(jnp.where(c == 0, captions, pictures), other_core)
    own = jnp.where(c == 0, pictures, captions)
    head, z_own, u_own, rn_own = project_own(flags, own, picture_head, caption_head)
    z, u_other, rn_other = project_other(received, head, z_own)

    one = send(z, first_hop)
    cross = send(z, first_crossing)
    ft = turn(flags, own, received)
    one, ft = lax.optimization_barrier((one, ft))
    ft_end = send(ft[CHIP : 2 * CHIP], inward)
    ft_mid = send(ft[2 * CHIP :], middle)
    ft_far = send(ft[2 * CHIP :], inward_far)
    two = send(one, second_hop)
    cross_two = send(one, second_crossing)
    near_one = send(cross, from_near)
    two, ft_mid = lax.optimization_barrier((two, ft_mid))
    three = send(choose(flags, two, cross), third_hop)
    here = send(z, other_core)
    dxs = pairs(
        flags, scale, z, u_own, u_other, rn_own, rn_other, here, one, two, three,
        cross, near_one, cross_two, ft_far, ft_mid, ft_end,
    )

    ends = [send(dx, inward) for dx in dxs]
    mids = [send(dx, middle) for dx in dxs]
    inner, outer = near(ft, ft_end, ft_mid, *dxs, *ends, *mids)
    right, inner = lax.optimization_barrier((ends[1], inner))
    fars = [send(ends[0], middle), send(right, middle)]
    same_left, crossed_left, part_left = far(0, flags, outer, ft_far, fars[0])
    same_left = send(same_left, outward)
    crossed_left = send(crossed_left, outward_cross)
    same_right, crossed_right, part_right = far(1, flags, outer, ft_far, fars[1], part_left)
    same_right = send(same_right, outward)
    crossed_right = send(crossed_right, outward_cross)
    keep, *swaps = rest(flags, inner, ft_far, *fars, part_left, part_right)
    swaps, same_left, crossed_left = lax.optimization_barrier(
        (swaps, same_left, crossed_left)
    )
    swaps = [send(swap, other_core) for swap in swaps]
    return finish(
        flags, same_left, crossed_left, same_right, crossed_right, *swaps, keep
    )


def solution(mesh):
    physical = Mesh(mesh.devices.reshape(SIZES), NAMES)
    rows = P(NAMES, None)
    grad = P(("x", "zh", "y"), ("zl", "c"), None)
    return jax.shard_map(
        on_device,
        mesh=physical,
        in_specs=(rows, rows, P(), P(), P(), P()),
        out_specs=(grad, grad),
        check_vma=False,
    )
```

```python
import functools

import jax
import jax.numpy as jnp
from jax import lax
from jax.experimental import pallas as pl
from jax.experimental.pallas import tpu as pltpu
from jax.sharding import Mesh, PartitionSpec as P

NAMES = ("x", "zh", "y", "zl", "c")
NX, NZH, NY, NZL, NC = SIZES = (8, 2, 8, 4, 2)
ROWS = 128
D = 1152
CHIP = 288
CORE = 144
LEFT = 512
HALVES = (slice(0, LEFT), slice(LEFT, D))
EPS = 1e-06
BF = jnp.bfloat16
F32 = jnp.float32
PROJECT_LIMIT = 49
VMEM = pl.BlockSpec(memory_space=pltpu.VMEM)
SMEM = pl.BlockSpec(memory_space=pltpu.SMEM)
ANY = pl.BlockSpec(memory_space=pl.ANY)
HBM = pl.BlockSpec(memory_space=pltpu.HBM)
PARAMS = pltpu.CompilerParams(vmem_limit_bytes=32 * 1024 * 1024)


def index_of(x, zh, y, zl, c):
    return (((x * NZH + zh) * NY + y) * NZL + zl) * NC + c


def pairs_of(rule):
    found = []
    for x in range(NX):
        for zh in range(NZH):
            for y in range(NY):
                for zl in range(NZL):
                    for c in range(NC):
                        target = rule(x, zh, y, zl, c)
                        if target is not None:
                            found.append((index_of(x, zh, y, zl, c), index_of(*target)))
    return found


def send(value, rule):
    return lax.ppermute(value, NAMES, pairs_of(rule))


def other_core(x, zh, y, zl, c):
    return (x, zh, y, zl, 1 - c)


def first_hop(x, zh, y, zl, c):
    if c == 1:
        return (x, zh, y + 1, zl, 0) if y < 7 else None
    return (x, zh, y - 1, zl, 1) if y > 0 else None


def second_hop(x, zh, y, zl, c):
    if not 1 <= y <= 6:
        return None
    return (x, zh, y + 1 if c == 0 else y - 1, zl, c)


def third_hop(x, zh, y, zl, c):
    if c == 0:
        return (x, zh, y + 1, zl, 0) if y < 7 else None
    return (x, zh, y - 1, zl, 1) if y > 0 else None


def above(x, zh, column):
    return (x, 1, column) if zh == 0 else ((x + 1) % NX, 0, column)


def below(x, zh, column):
    return (x, 0, column) if zh == 1 else ((x - 1) % NX, 1, column)


def first_crossing(x, zh, y, zl, c):
    if c == 1 and y >= 6:
        return (*above(x, zh, y - 6), zl, 0)
    if c == 0 and y <= 1:
        return (*below(x, zh, 6 + y), zl, 1)
    return None


def second_crossing(x, zh, y, zl, c):
    if c == 0 and y == 6:
        return (*above(x, zh, 0), zl, 0)
    if c == 1 and y == 1:
        return (*below(x, zh, 7), zl, 1)
    return None


def from_near(x, zh, y, zl, c):
    if c == 0 and y == 1:
        return (x, zh, 0, zl, 0)
    if c == 1 and y == 6:
        return (x, zh, 7, zl, 1)
    return None


def inward(x, zh, y, zl, c):
    return {0: (x, zh, y, 1, c), 3: (x, zh, y, 2, c)}.get(zl)


def middle(x, zh, y, zl, c):
    return {1: (x, zh, y, 2, c), 2: (x, zh, y, 1, c)}.get(zl)


def inward_far(x, zh, y, zl, c):
    return {0: (x, zh, y, 2, c), 3: (x, zh, y, 1, c)}.get(zl)


def outward(x, zh, y, zl, c):
    return {1: (x, zh, y, 0, c), 2: (x, zh, y, 3, c)}.get(zl)


def outward_cross(x, zh, y, zl, c):
    return {1: (x, zh, y, 0, 1 - c), 2: (x, zh, y, 3, 1 - c)}.get(zl)


def normalised(x):
    total = jnp.sum(x * x, axis=-1, keepdims=True)
    rn = 1.0 / jnp.sqrt(total + EPS)
    return x * rn, jnp.broadcast_to(rn, (ROWS, 128))


def project_own_kernel(flags, own, wp, wc, w_ref, z_ref, u_ref, rn_ref, sems):
    c = flags[0]
    parts = 3
    width = D // parts

    def fetch(head):
        for j in range(parts):
            cols = pl.ds(j * width, width)
            pltpu.make_async_copy(head.at[:, cols], w_ref.at[:, cols], sems.at[j]).start()

    @pl.when(c == 0)
    def _():
        fetch(wp)

    @pl.when(c == 1)
    def _():
        fetch(wc)

    for j in range(parts):
        cols = pl.ds(j * width, width)
        pltpu.make_async_copy(wp.at[:, cols], w_ref.at[:, cols], sems.at[j]).wait()
        u_ref[:, cols] = jnp.dot(own[...], w_ref[:, cols], preferred_element_type=F32)
    u, rn_ref[...] = normalised(u_ref[...])
    u_ref[...] = u
    z_ref[...] = u.astype(BF)


def project_own(flags, own, wp, wc):
    return pl.pallas_call(
        project_own_kernel,
        name="project_own",
        out_shape=(
            jax.ShapeDtypeStruct((D, D), BF),
            jax.ShapeDtypeStruct((ROWS, D), BF),
            jax.ShapeDtypeStruct((ROWS, D), F32),
            jax.ShapeDtypeStruct((ROWS, 128), F32),
        ),
        in_specs=[SMEM, VMEM, HBM, HBM],
        out_specs=(VMEM,) * 4,
        scratch_shapes=[pltpu.SemaphoreType.DMA((3,))],
        compiler_params=pltpu.CompilerParams(vmem_limit_bytes=PROJECT_LIMIT * 1024 * 1024),
        cost_estimate=pl.CostEstimate(
            flops=2 * ROWS * D * D, bytes_accessed=2 * D * D + 8 * ROWS * D, transcendentals=0
        ),
    )(flags, own, wp, wc)


def project_other_kernel(recv, w_ref, z_own, z_ref, u_ref, rn_ref):
    z_ref[:ROWS] = z_own[...]
    u, rn_ref[...] = normalised(
        jnp.dot(recv[...], w_ref[...], preferred_element_type=F32)
    )
    u_ref[...] = u
    z_ref[ROWS:] = u.astype(BF)


def project_other(recv, w, z_own):
    return pl.pallas_call(
        project_other_kernel,
        name="project_other",
        out_shape=(
            jax.ShapeDtypeStruct((2 * ROWS, D), BF),
            jax.ShapeDtypeStruct((ROWS, D), F32),
            jax.ShapeDtypeStruct((ROWS, 128), F32),
        ),
        in_specs=[VMEM] * 3,
        out_specs=(VMEM,) * 3,
        compiler_params=PARAMS,
        cost_estimate=pl.CostEstimate(
            flops=2 * ROWS * D * D, bytes_accessed=2 * D * D + 8 * ROWS * D, transcendentals=0
        ),
    )(recv, w, z_own)


def turn_kernel(flags, own, recv, ft_ref, turned):
    mirror = flags[3]
    turned[:, :ROWS] = own[...].T
    turned[:, ROWS:] = recv[...].T
    for j in range(4):
        start = pl.multiple_of(jnp.where(mirror == 1, 3 - j, j) * CHIP, CHIP)
        ft_ref[j * CHIP : (j + 1) * CHIP] = turned[pl.ds(start, CHIP)]


def turn(flags, own, recv):
    return pl.pallas_call(
        turn_kernel,
        name="turn",
        out_shape=jax.ShapeDtypeStruct((D, 2 * ROWS), BF),
        in_specs=[SMEM, VMEM, VMEM],
        out_specs=VMEM,
        scratch_shapes=[pltpu.VMEM((D, 2 * ROWS), BF)],
        compiler_params=PARAMS,
        cost_estimate=pl.CostEstimate(
            flops=0, bytes_accessed=8 * ROWS * D, transcendentals=0
        ),
    )(flags, own, recv)


def choose_kernel(flags, two, cross, out_ref, sem):
    place = flags[1]

    @pl.when(place <= 1)
    def _():
        pltpu.make_async_copy(cross, out_ref, sem).start()

    @pl.when(place > 1)
    def _():
        pltpu.make_async_copy(two, out_ref, sem).start()

    pltpu.make_async_copy(two, out_ref, sem).wait()


def choose(flags, two, cross):
    return pl.pallas_call(
        choose_kernel,
        name="choose",
        out_shape=jax.ShapeDtypeStruct((2 * ROWS, D), BF),
        in_specs=[SMEM] + [ANY] * 2,
        out_specs=VMEM,
        scratch_shapes=[pltpu.SemaphoreType.DMA(())],
        compiler_params=PARAMS,
        cost_estimate=pl.CostEstimate(
            flops=0, bytes_accessed=8 * ROWS * D, transcendentals=0
        ),
    )(flags, two, cross)


def pairs_kernel(
    flags, scale, z_ref, u_own, u_other, rn_own, rn_other,
    here, one, two, three, cross, near_one, cross_two, *refs
):
    dx_left, dx_right, others, sems = refs[-4:]
    place = flags[1]

    def fetch(source, s):
        for b in range(2):
            pltpu.make_async_copy(
                source.at[pl.ds((1 - b) * ROWS, ROWS)],
                others.at[b, pl.ds(s * ROWS, ROWS)],
                sems.at[2 * s + b],
            ).start()

    fetch(here, 0)

    @pl.when(place > 0)
    def _():
        fetch(one, 1)
        fetch(three, 3)

    @pl.when(place == 0)
    def _():
        fetch(near_one, 1)
        fetch(cross_two, 3)

    @pl.when(place <= 1)
    def _():
        fetch(cross, 2)

    @pl.when(place > 1)
    def _():
        fetch(two, 2)

    t = scale[0]
    bias = scale[1]
    for s in range(4):
        for b in range(2):
            pltpu.make_async_copy(
                here.at[pl.ds(0, ROWS)],
                others.at[b, pl.ds(s * ROWS, ROWS)],
                sems.at[2 * s + b],
            ).wait()
    row = lax.broadcasted_iota(jnp.int32, (ROWS, 4 * ROWS), 0)
    col = lax.broadcasted_iota(jnp.int32, (ROWS, 4 * ROWS), 1)
    for b in range(2):
        mine = z_ref[b * ROWS : (b + 1) * ROWS]
        logits = t * lax.dot_general(
            mine, others[b], (((1,), (1,)), ((), ())), preferred_element_type=F32
        ) + bias
        prob = jax.nn.sigmoid(logits) - jnp.where(row == col, 1.0, 0.0)
        weight = (prob * (1.0 / ROWS)).astype(BF)
        dz = t * jnp.dot(weight, others[b], preferred_element_type=F32)
        u = (u_own, u_other)[b][...]
        rn = (rn_own, rn_other)[b][:, :1]
        inner = jnp.sum(u * dz, axis=-1, keepdims=True)
        dx = ((dz - u * inner) * rn).astype(BF)
        for cols, dx_ref in zip(HALVES, (dx_left, dx_right)):
            dx_ref[b * ROWS : (b + 1) * ROWS] = dx[:, cols]


def pairs(flags, scale, z, *rest):
    rows = 2 * ROWS
    return pl.pallas_call(
        pairs_kernel,
        name="pairs",
        out_shape=(
            jax.ShapeDtypeStruct((rows, LEFT), BF),
            jax.ShapeDtypeStruct((rows, D - LEFT), BF),
        ),
        in_specs=[SMEM, SMEM] + [VMEM] * 5 + [ANY] * 10,
        out_specs=(VMEM, VMEM),
        scratch_shapes=[
            pltpu.VMEM((2, 4 * ROWS, D), BF),
            pltpu.SemaphoreType.DMA((8,)),
        ],
        compiler_params=PARAMS,
        cost_estimate=pl.CostEstimate(
            flops=16 * rows * ROWS * D, bytes_accessed=14 * rows * D, transcendentals=rows * 512
        ),
    )(flags, scale, z, *rest)


def near_kernel(ft, feats_end, feats_mid, *refs):
    inner_ref, outer_ref = refs[6:]
    for cols, dx, dx_end, dx_mid in zip(HALVES, refs[:2], refs[2:4], refs[4:6]):
        dx_own = dx[...]
        dx_other = dx_mid[...]
        inner_ref[:, cols] = (
            jnp.dot(ft[CHIP : 2 * CHIP], dx_own, preferred_element_type=F32)
            + jnp.dot(feats_end[:CHIP], dx_end[...], preferred_element_type=F32)
            + jnp.dot(feats_mid[:CHIP], dx_other, preferred_element_type=F32)
        )
        outer_ref[:, cols] = jnp.dot(
            ft[:CHIP], dx_own, preferred_element_type=F32
        ) + jnp.dot(feats_mid[CHIP:], dx_other, preferred_element_type=F32)


def near(ft, feats_end, feats_mid, *dxs):
    return pl.pallas_call(
        near_kernel,
        name="near",
        out_shape=(
            jax.ShapeDtypeStruct((CHIP, D), F32),
            jax.ShapeDtypeStruct((CHIP, D), F32),
        ),
        in_specs=[VMEM] * 9,
        out_specs=(VMEM, VMEM),
        compiler_params=PARAMS,
        cost_estimate=pl.CostEstimate(
            flops=20 * CHIP * ROWS * D, bytes_accessed=14 * CHIP * D, transcendentals=0
        ),
    )(ft, feats_end, feats_mid, *dxs)


def far_kernel(half, flags, outer_ref, feats, dx, *refs):
    same, crossed, part = refs[-3:]
    c = flags[0]
    part[...] = outer_ref[:, HALVES[half]] + jnp.dot(
        feats[CHIP:], dx[...], preferred_element_type=F32
    )
    mine = pl.ds(pl.multiple_of(c * CORE, CORE), CORE)
    theirs = pl.ds(pl.multiple_of((1 - c) * CORE, CORE), CORE)
    same[...] = part[mine].astype(BF)
    crossed[...] = part[theirs].astype(BF)


def far(half, flags, outer, feats, dx, *after):
    cols = dx.shape[1]
    return pl.pallas_call(
        functools.partial(far_kernel, half),
        name="far",
        out_shape=(
            jax.ShapeDtypeStruct((CORE, cols), BF),
            jax.ShapeDtypeStruct((CORE, cols), BF),
            jax.ShapeDtypeStruct((CHIP, cols), F32),
        ),
        in_specs=[SMEM] + [VMEM] * 3 + [ANY] * len(after),
        out_specs=(VMEM,) * 3,
        compiler_params=PARAMS,
        cost_estimate=pl.CostEstimate(
            flops=4 * CHIP * ROWS * cols, bytes_accessed=14 * CHIP * cols, transcendentals=0
        ),
    )(flags, outer, feats, dx, *after)


def rest_kernel(
    flags, inner_ref, feats, dx_left, dx_right, part_left, part_right,
    keep, swap_left, swap_right, total,
):
    c = flags[0]
    mine = pl.ds(pl.multiple_of(c * CORE, CORE), CORE)
    theirs = pl.ds(pl.multiple_of((1 - c) * CORE, CORE), CORE)

    @pl.when(flags[4] == 1)
    def _():
        for cols, dx in zip(HALVES, (dx_left, dx_right)):
            total[:, cols] = inner_ref[:, cols] + jnp.dot(
                feats[:CHIP], dx[...], preferred_element_type=F32
            )
        keep[...] = total[mine]
        swap_left[...] = total[theirs, :LEFT].astype(BF)
        swap_right[...] = total[theirs, LEFT:].astype(BF)

    @pl.when(flags[4] == 0)
    def _():
        for cols, part, swap in zip(
            HALVES, (part_left, part_right), (swap_left, swap_right)
        ):
            keep[:, cols] = part[mine]
            swap[...] = part[theirs].astype(BF)


def rest(flags, *parts):
    return pl.pallas_call(
        rest_kernel,
        name="rest",
        out_shape=(
            jax.ShapeDtypeStruct((CORE, D), F32),
            jax.ShapeDtypeStruct((CORE, LEFT), BF),
            jax.ShapeDtypeStruct((CORE, D - LEFT), BF),
        ),
        in_specs=[SMEM] + [VMEM] * 6,
        out_specs=(VMEM,) * 3,
        scratch_shapes=[pltpu.VMEM((CHIP, D), F32)],
        compiler_params=PARAMS,
        cost_estimate=pl.CostEstimate(
            flops=4 * CHIP * ROWS * D, bytes_accessed=14 * CHIP * D, transcendentals=0
        ),
    )(flags, *parts)


def finish_kernel(
    flags, same_left, crossed_left, same_right, crossed_right, swap_left, swap_right, keep,
    image_ref, text_ref,
):
    def put(own_ref, other_ref):
        for cols, same, crossed, swap in (
            (HALVES[0], same_left, crossed_left, swap_left),
            (HALVES[1], same_right, crossed_right, swap_right),
        ):
            own_ref[0, :, cols] = keep[:, cols] + same[...].astype(F32)
            other_ref[0, :, cols] = swap[...].astype(F32) + crossed[...].astype(F32)

    @pl.when(flags[0] == 0)
    def _():
        put(image_ref, text_ref)

    @pl.when(flags[0] == 1)
    def _():
        put(text_ref, image_ref)


def finish(flags, *parts):
    shape = jax.ShapeDtypeStruct((1, CORE, D), F32)
    return pl.pallas_call(
        finish_kernel,
        name="finish",
        out_shape=(shape, shape),
        in_specs=[SMEM] + [VMEM] * 7,
        out_specs=(VMEM, VMEM),
        compiler_params=PARAMS,
        cost_estimate=pl.CostEstimate(
            flops=4 * CORE * D, bytes_accessed=18 * CORE * D, transcendentals=0
        ),
    )(flags, *parts)


def on_device(pictures, captions, picture_head, caption_head, sharpness, shift_term):
    c = lax.axis_index("c")
    y = lax.axis_index("y")
    zl = lax.axis_index("zl")
    yy = jnp.where(c == 0, y, 7 - y)
    flags = jnp.stack([c, yy, zl, zl >= 2, (zl == 1) | (zl == 2)]).astype(jnp.int32)
    scale = jnp.concatenate([sharpness, shift_term])

    received = send(jnp.where(c == 0, captions, pictures), other_core)
    own = jnp.where(c == 0, pictures, captions)
    head, z_own, u_own, rn_own = project_own(flags, own, picture_head, caption_head)
    z, u_other, rn_other = project_other(received, head, z_own)

    one = send(z, first_hop)
    cross = send(z, first_crossing)
    ft = turn(flags, own, received)
    one, ft = lax.optimization_barrier((one, ft))
    ft_end = send(ft[CHIP : 2 * CHIP], inward)
    ft_mid = send(ft[2 * CHIP :], middle)
    ft_far = send(ft[2 * CHIP :], inward_far)
    two = send(one, second_hop)
    cross_two = send(one, second_crossing)
    near_one = send(cross, from_near)
    three = send(choose(flags, two, cross), third_hop)
    here = send(z, other_core)
    dxs = pairs(
        flags, scale, z, u_own, u_other, rn_own, rn_other, here, one, two, three,
        cross, near_one, cross_two, ft_far, ft_mid, ft_end,
    )

    ends = [send(dx, inward) for dx in dxs]
    mids = [send(dx, middle) for dx in dxs]
    inner, outer = near(ft, ft_end, ft_mid, *dxs, *ends, *mids)
    right, inner = lax.optimization_barrier((ends[1], inner))
    fars = [send(ends[0], middle), send(right, middle)]
    same_left, crossed_left, part_left = far(0, flags, outer, ft_far, fars[0])
    same_left = send(same_left, outward)
    crossed_left = send(crossed_left, outward_cross)
    same_right, crossed_right, part_right = far(1, flags, outer, ft_far, fars[1], part_left)
    same_right = send(same_right, outward)
    crossed_right = send(crossed_right, outward_cross)
    keep, *swaps = rest(flags, inner, ft_far, *fars, part_left, part_right)
    swaps, same_left, crossed_left = lax.optimization_barrier(
        (swaps, same_left, crossed_left)
    )
    swaps = [send(swap, other_core) for swap in swaps]
    return finish(
        flags, same_left, crossed_left, same_right, crossed_right, *swaps, keep
    )


def solution(mesh):
    physical = Mesh(mesh.devices.reshape(SIZES), NAMES)
    rows = P(NAMES, None)
    grad = P(("x", "zh", "y"), ("zl", "c"), None)
    return jax.shard_map(
        on_device,
        mesh=physical,
        in_specs=(rows, rows, P(), P(), P(), P()),
        out_specs=(grad, grad),
        check_vma=False,
    )
```

```python
import functools

import jax
import jax.numpy as jnp
from jax import lax
from jax.experimental import pallas as pl
from jax.experimental.pallas import tpu as pltpu
from jax.sharding import Mesh, PartitionSpec as P

NAMES = ("x", "zh", "y", "zl", "c")
NX, NZH, NY, NZL, NC = SIZES = (8, 2, 8, 4, 2)
ROWS = 128
D = 1152
CHIP = 288
CORE = 144
LEFT = 512
HALVES = (slice(0, LEFT), slice(LEFT, D))
EPS = 1e-06
BF = jnp.bfloat16
F32 = jnp.float32
PROJECT_LIMIT = 49
VMEM = pl.BlockSpec(memory_space=pltpu.VMEM)
SMEM = pl.BlockSpec(memory_space=pltpu.SMEM)
ANY = pl.BlockSpec(memory_space=pl.ANY)
HBM = pl.BlockSpec(memory_space=pltpu.HBM)
PARAMS = pltpu.CompilerParams(vmem_limit_bytes=32 * 1024 * 1024)


def index_of(x, zh, y, zl, c):
    return (((x * NZH + zh) * NY + y) * NZL + zl) * NC + c


def pairs_of(rule):
    found = []
    for x in range(NX):
        for zh in range(NZH):
            for y in range(NY):
                for zl in range(NZL):
                    for c in range(NC):
                        target = rule(x, zh, y, zl, c)
                        if target is not None:
                            found.append((index_of(x, zh, y, zl, c), index_of(*target)))
    return found


def send(value, rule):
    return lax.ppermute(value, NAMES, pairs_of(rule))


def other_core(x, zh, y, zl, c):
    return (x, zh, y, zl, 1 - c)


def first_hop(x, zh, y, zl, c):
    if c == 1:
        return (x, zh, y + 1, zl, 0) if y < 7 else None
    return (x, zh, y - 1, zl, 1) if y > 0 else None


def second_hop(x, zh, y, zl, c):
    if not 1 <= y <= 6:
        return None
    return (x, zh, y + 1 if c == 0 else y - 1, zl, c)


def third_hop(x, zh, y, zl, c):
    if c == 0:
        return (x, zh, y + 1, zl, 0) if y < 7 else None
    return (x, zh, y - 1, zl, 1) if y > 0 else None


def above(x, zh, column):
    return (x, 1, column) if zh == 0 else ((x + 1) % NX, 0, column)


def below(x, zh, column):
    return (x, 0, column) if zh == 1 else ((x - 1) % NX, 1, column)


def first_crossing(x, zh, y, zl, c):
    if c == 1 and y >= 6:
        return (*above(x, zh, y - 6), zl, 0)
    if c == 0 and y <= 1:
        return (*below(x, zh, 6 + y), zl, 1)
    return None


def second_crossing(x, zh, y, zl, c):
    if c == 0 and y == 6:
        return (*above(x, zh, 0), zl, 0)
    if c == 1 and y == 1:
        return (*below(x, zh, 7), zl, 1)
    return None


def from_near(x, zh, y, zl, c):
    if c == 0 and y == 1:
        return (x, zh, 0, zl, 0)
    if c == 1 and y == 6:
        return (x, zh, 7, zl, 1)
    return None


def inward(x, zh, y, zl, c):
    return {0: (x, zh, y, 1, c), 3: (x, zh, y, 2, c)}.get(zl)


def middle(x, zh, y, zl, c):
    return {1: (x, zh, y, 2, c), 2: (x, zh, y, 1, c)}.get(zl)


def inward_far(x, zh, y, zl, c):
    return {0: (x, zh, y, 2, c), 3: (x, zh, y, 1, c)}.get(zl)


def outward(x, zh, y, zl, c):
    return {1: (x, zh, y, 0, c), 2: (x, zh, y, 3, c)}.get(zl)


def outward_cross(x, zh, y, zl, c):
    return {1: (x, zh, y, 0, 1 - c), 2: (x, zh, y, 3, 1 - c)}.get(zl)


def normalised(x):
    total = jnp.sum(x * x, axis=-1, keepdims=True)
    rn = 1.0 / jnp.sqrt(total + EPS)
    return x * rn, jnp.broadcast_to(rn, (ROWS, 128))


def project_own_kernel(flags, own, wp, wc, w_ref, z_ref, u_ref, rn_ref, sems):
    c = flags[0]
    parts = 3
    width = D // parts

    def fetch(head):
        for j in range(parts):
            cols = pl.ds(j * width, width)
            pltpu.make_async_copy(head.at[:, cols], w_ref.at[:, cols], sems.at[j]).start()

    @pl.when(c == 0)
    def _():
        fetch(wp)

    @pl.when(c == 1)
    def _():
        fetch(wc)

    for j in range(parts):
        cols = pl.ds(j * width, width)
        pltpu.make_async_copy(wp.at[:, cols], w_ref.at[:, cols], sems.at[j]).wait()
        u_ref[:, cols] = jnp.dot(own[...], w_ref[:, cols], preferred_element_type=F32)
    u, rn_ref[...] = normalised(u_ref[...])
    u_ref[...] = u
    z_ref[...] = u.astype(BF)


def project_own(flags, own, wp, wc):
    return pl.pallas_call(
        project_own_kernel,
        name="project_own",
        out_shape=(
            jax.ShapeDtypeStruct((D, D), BF),
            jax.ShapeDtypeStruct((ROWS, D), BF),
            jax.ShapeDtypeStruct((ROWS, D), F32),
            jax.ShapeDtypeStruct((ROWS, 128), F32),
        ),
        in_specs=[SMEM, VMEM, HBM, HBM],
        out_specs=(VMEM,) * 4,
        scratch_shapes=[pltpu.SemaphoreType.DMA((3,))],
        compiler_params=pltpu.CompilerParams(vmem_limit_bytes=PROJECT_LIMIT * 1024 * 1024),
        cost_estimate=pl.CostEstimate(
            flops=2 * ROWS * D * D, bytes_accessed=2 * D * D + 8 * ROWS * D, transcendentals=0
        ),
    )(flags, own, wp, wc)


def project_other_kernel(recv, w_ref, z_own, z_ref, u_ref, rn_ref):
    z_ref[:ROWS] = z_own[...]
    u, rn_ref[...] = normalised(
        jnp.dot(recv[...], w_ref[...], preferred_element_type=F32)
    )
    u_ref[...] = u
    z_ref[ROWS:] = u.astype(BF)


def project_other(recv, w, z_own):
    return pl.pallas_call(
        project_other_kernel,
        name="project_other",
        out_shape=(
            jax.ShapeDtypeStruct((2 * ROWS, D), BF),
            jax.ShapeDtypeStruct((ROWS, D), F32),
            jax.ShapeDtypeStruct((ROWS, 128), F32),
        ),
        in_specs=[VMEM] * 3,
        out_specs=(VMEM,) * 3,
        compiler_params=PARAMS,
        cost_estimate=pl.CostEstimate(
            flops=2 * ROWS * D * D, bytes_accessed=2 * D * D + 8 * ROWS * D, transcendentals=0
        ),
    )(recv, w, z_own)


def turn_kernel(flags, own, recv, ft_ref, turned):
    mirror = flags[3]
    turned[:, :ROWS] = own[...].T
    turned[:, ROWS:] = recv[...].T
    for j in range(4):
        start = pl.multiple_of(jnp.where(mirror == 1, 3 - j, j) * CHIP, CHIP)
        ft_ref[j * CHIP : (j + 1) * CHIP] = turned[pl.ds(start, CHIP)]


def turn(flags, own, recv):
    return pl.pallas_call(
        turn_kernel,
        name="turn",
        out_shape=jax.ShapeDtypeStruct((D, 2 * ROWS), BF),
        in_specs=[SMEM, VMEM, VMEM],
        out_specs=VMEM,
        scratch_shapes=[pltpu.VMEM((D, 2 * ROWS), BF)],
        compiler_params=PARAMS,
        cost_estimate=pl.CostEstimate(
            flops=0, bytes_accessed=8 * ROWS * D, transcendentals=0
        ),
    )(flags, own, recv)


def choose_kernel(flags, two, cross, out_ref, sem):
    place = flags[1]

    @pl.when(place <= 1)
    def _():
        pltpu.make_async_copy(cross, out_ref, sem).start()

    @pl.when(place > 1)
    def _():
        pltpu.make_async_copy(two, out_ref, sem).start()

    pltpu.make_async_copy(two, out_ref, sem).wait()


def choose(flags, two, cross):
    return pl.pallas_call(
        choose_kernel,
        name="choose",
        out_shape=jax.ShapeDtypeStruct((2 * ROWS, D), BF),
        in_specs=[SMEM] + [ANY] * 2,
        out_specs=VMEM,
        scratch_shapes=[pltpu.SemaphoreType.DMA(())],
        compiler_params=PARAMS,
        cost_estimate=pl.CostEstimate(
            flops=0, bytes_accessed=8 * ROWS * D, transcendentals=0
        ),
    )(flags, two, cross)


def pairs_kernel(
    flags, scale, z_ref, u_own, u_other, rn_own, rn_other,
    here, one, two, three, cross, near_one, cross_two, *refs
):
    dx_left, dx_right, others, sems = refs[-4:]
    place = flags[1]

    def fetch(source, s):
        for b in range(2):
            pltpu.make_async_copy(
                source.at[pl.ds((1 - b) * ROWS, ROWS)],
                others.at[b, pl.ds(s * ROWS, ROWS)],
                sems.at[2 * s + b],
            ).start()

    fetch(here, 0)

    @pl.when(place > 0)
    def _():
        fetch(one, 1)
        fetch(three, 3)

    @pl.when(place == 0)
    def _():
        fetch(near_one, 1)
        fetch(cross_two, 3)

    @pl.when(place <= 1)
    def _():
        fetch(cross, 2)

    @pl.when(place > 1)
    def _():
        fetch(two, 2)

    t = scale[0]
    bias = scale[1]
    for s in range(4):
        for b in range(2):
            pltpu.make_async_copy(
                here.at[pl.ds(0, ROWS)],
                others.at[b, pl.ds(s * ROWS, ROWS)],
                sems.at[2 * s + b],
            ).wait()
    row = lax.broadcasted_iota(jnp.int32, (ROWS, 4 * ROWS), 0)
    col = lax.broadcasted_iota(jnp.int32, (ROWS, 4 * ROWS), 1)
    for b in range(2):
        mine = z_ref[b * ROWS : (b + 1) * ROWS]
        logits = t * lax.dot_general(
            mine, others[b], (((1,), (1,)), ((), ())), preferred_element_type=F32
        ) + bias
        prob = jax.nn.sigmoid(logits) - jnp.where(row == col, 1.0, 0.0)
        weight = (prob * (1.0 / ROWS)).astype(BF)
        dz = t * jnp.dot(weight, others[b], preferred_element_type=F32)
        u = (u_own, u_other)[b][...]
        rn = (rn_own, rn_other)[b][:, :1]
        inner = jnp.sum(u * dz, axis=-1, keepdims=True)
        dx = ((dz - u * inner) * rn).astype(BF)
        for cols, dx_ref in zip(HALVES, (dx_left, dx_right)):
            dx_ref[b * ROWS : (b + 1) * ROWS] = dx[:, cols]


def pairs(flags, scale, z, *rest):
    rows = 2 * ROWS
    return pl.pallas_call(
        pairs_kernel,
        name="pairs",
        out_shape=(
            jax.ShapeDtypeStruct((rows, LEFT), BF),
            jax.ShapeDtypeStruct((rows, D - LEFT), BF),
        ),
        in_specs=[SMEM, SMEM] + [VMEM] * 5 + [ANY] * 10,
        out_specs=(VMEM, VMEM),
        scratch_shapes=[
            pltpu.VMEM((2, 4 * ROWS, D), BF),
            pltpu.SemaphoreType.DMA((8,)),
        ],
        compiler_params=PARAMS,
        cost_estimate=pl.CostEstimate(
            flops=16 * rows * ROWS * D, bytes_accessed=14 * rows * D, transcendentals=rows * 512
        ),
    )(flags, scale, z, *rest)


def near_kernel(ft, feats_end, feats_mid, *refs):
    inner_ref, outer_ref = refs[6:]
    for cols, dx, dx_end, dx_mid in zip(HALVES, refs[:2], refs[2:4], refs[4:6]):
        dx_own = dx[...]
        dx_other = dx_mid[...]
        inner_ref[:, cols] = (
            jnp.dot(ft[CHIP : 2 * CHIP], dx_own, preferred_element_type=F32)
            + jnp.dot(feats_end[:CHIP], dx_end[...], preferred_element_type=F32)
            + jnp.dot(feats_mid[:CHIP], dx_other, preferred_element_type=F32)
        )
        outer_ref[:, cols] = jnp.dot(
            ft[:CHIP], dx_own, preferred_element_type=F32
        ) + jnp.dot(feats_mid[CHIP:], dx_other, preferred_element_type=F32)


def near(ft, feats_end, feats_mid, *dxs):
    return pl.pallas_call(
        near_kernel,
        name="near",
        out_shape=(
            jax.ShapeDtypeStruct((CHIP, D), F32),
            jax.ShapeDtypeStruct((CHIP, D), F32),
        ),
        in_specs=[VMEM] * 9,
        out_specs=(VMEM, VMEM),
        compiler_params=PARAMS,
        cost_estimate=pl.CostEstimate(
            flops=20 * CHIP * ROWS * D, bytes_accessed=14 * CHIP * D, transcendentals=0
        ),
    )(ft, feats_end, feats_mid, *dxs)


def far_kernel(half, flags, outer_ref, feats, dx, *refs):
    same, crossed, part = refs[-3:]
    c = flags[0]
    part[...] = outer_ref[:, HALVES[half]] + jnp.dot(
        feats[CHIP:], dx[...], preferred_element_type=F32
    )
    mine = pl.ds(pl.multiple_of(c * CORE, CORE), CORE)
    theirs = pl.ds(pl.multiple_of((1 - c) * CORE, CORE), CORE)
    same[...] = part[mine].astype(BF)
    crossed[...] = part[theirs].astype(BF)


def far(half, flags, outer, feats, dx, *after):
    cols = dx.shape[1]
    return pl.pallas_call(
        functools.partial(far_kernel, half),
        name="far",
        out_shape=(
            jax.ShapeDtypeStruct((CORE, cols), BF),
            jax.ShapeDtypeStruct((CORE, cols), BF),
            jax.ShapeDtypeStruct((CHIP, cols), F32),
        ),
        in_specs=[SMEM] + [VMEM] * 3 + [ANY] * len(after),
        out_specs=(VMEM,) * 3,
        compiler_params=PARAMS,
        cost_estimate=pl.CostEstimate(
            flops=4 * CHIP * ROWS * cols, bytes_accessed=14 * CHIP * cols, transcendentals=0
        ),
    )(flags, outer, feats, dx, *after)


def rest_kernel(
    flags, inner_ref, feats, dx_left, dx_right, part_left, part_right,
    keep, swap_left, swap_right, total,
):
    c = flags[0]
    mine = pl.ds(pl.multiple_of(c * CORE, CORE), CORE)
    theirs = pl.ds(pl.multiple_of((1 - c) * CORE, CORE), CORE)

    @pl.when(flags[4] == 1)
    def _():
        for cols, dx in zip(HALVES, (dx_left, dx_right)):
            total[:, cols] = inner_ref[:, cols] + jnp.dot(
                feats[:CHIP], dx[...], preferred_element_type=F32
            )
        keep[...] = total[mine]
        swap_left[...] = total[theirs, :LEFT].astype(BF)
        swap_right[...] = total[theirs, LEFT:].astype(BF)

    @pl.when(flags[4] == 0)
    def _():
        for cols, part, swap in zip(
            HALVES, (part_left, part_right), (swap_left, swap_right)
        ):
            keep[:, cols] = part[mine]
            swap[...] = part[theirs].astype(BF)


def rest(flags, *parts):
    return pl.pallas_call(
        rest_kernel,
        name="rest",
        out_shape=(
            jax.ShapeDtypeStruct((CORE, D), F32),
            jax.ShapeDtypeStruct((CORE, LEFT), BF),
            jax.ShapeDtypeStruct((CORE, D - LEFT), BF),
        ),
        in_specs=[SMEM] + [VMEM] * 6,
        out_specs=(VMEM,) * 3,
        scratch_shapes=[pltpu.VMEM((CHIP, D), F32)],
        compiler_params=PARAMS,
        cost_estimate=pl.CostEstimate(
            flops=4 * CHIP * ROWS * D, bytes_accessed=14 * CHIP * D, transcendentals=0
        ),
    )(flags, *parts)


def finish_kernel(
    flags, same_left, crossed_left, same_right, crossed_right, swap_left, swap_right, keep,
    image_ref, text_ref,
):
    def put(own_ref, other_ref):
        for cols, same, crossed, swap in (
            (HALVES[0], same_left, crossed_left, swap_left),
            (HALVES[1], same_right, crossed_right, swap_right),
        ):
            own_ref[0, :, cols] = keep[:, cols] + same[...].astype(F32)
            other_ref[0, :, cols] = swap[...].astype(F32) + crossed[...].astype(F32)

    @pl.when(flags[0] == 0)
    def _():
        put(image_ref, text_ref)

    @pl.when(flags[0] == 1)
    def _():
        put(text_ref, image_ref)


def finish(flags, *parts):
    shape = jax.ShapeDtypeStruct((1, CORE, D), F32)
    return pl.pallas_call(
        finish_kernel,
        name="finish",
        out_shape=(shape, shape),
        in_specs=[SMEM] + [VMEM] * 7,
        out_specs=(VMEM, VMEM),
        compiler_params=PARAMS,
        cost_estimate=pl.CostEstimate(
            flops=4 * CORE * D, bytes_accessed=18 * CORE * D, transcendentals=0
        ),
    )(flags, *parts)


def on_device(pictures, captions, picture_head, caption_head, sharpness, shift_term):
    c = lax.axis_index("c")
    y = lax.axis_index("y")
    zl = lax.axis_index("zl")
    yy = jnp.where(c == 0, y, 7 - y)
    flags = jnp.stack([c, yy, zl, zl >= 2, (zl == 1) | (zl == 2)]).astype(jnp.int32)
    scale = jnp.concatenate([sharpness, shift_term])

    received = send(jnp.where(c == 0, captions, pictures), other_core)
    own = jnp.where(c == 0, pictures, captions)
    head, z_own, u_own, rn_own = project_own(flags, own, picture_head, caption_head)
    z, u_other, rn_other = project_other(received, head, z_own)

    one = send(z, first_hop)
    cross = send(z, first_crossing)
    ft = turn(flags, own, received)
    one, ft = lax.optimization_barrier((one, ft))
    ft_end = send(ft[CHIP : 2 * CHIP], inward)
    ft_mid = send(ft[2 * CHIP :], middle)
    ft_far = send(ft[2 * CHIP :], inward_far)
    two = send(one, second_hop)
    cross_two = send(one, second_crossing)
    near_one = send(cross, from_near)
    two, ft_end = lax.optimization_barrier((two, ft_end))
    three = send(choose(flags, two, cross), third_hop)
    here = send(z, other_core)
    dxs = pairs(
        flags, scale, z, u_own, u_other, rn_own, rn_other, here, one, two, three,
        cross, near_one, cross_two, ft_far, ft_mid, ft_end,
    )

    ends = [send(dx, inward) for dx in dxs]
    mids = [send(dx, middle) for dx in dxs]
    inner, outer = near(ft, ft_end, ft_mid, *dxs, *ends, *mids)
    right, inner = lax.optimization_barrier((ends[1], inner))
    fars = [send(ends[0], middle), send(right, middle)]
    same_left, crossed_left, part_left = far(0, flags, outer, ft_far, fars[0])
    same_left = send(same_left, outward)
    crossed_left = send(crossed_left, outward_cross)
    same_right, crossed_right, part_right = far(1, flags, outer, ft_far, fars[1], part_left)
    same_right = send(same_right, outward)
    crossed_right = send(crossed_right, outward_cross)
    keep, *swaps = rest(flags, inner, ft_far, *fars, part_left, part_right)
    swaps, same_left, crossed_left = lax.optimization_barrier(
        (swaps, same_left, crossed_left)
    )
    swaps = [send(swap, other_core) for swap in swaps]
    return finish(
        flags, same_left, crossed_left, same_right, crossed_right, *swaps, keep
    )


def solution(mesh):
    physical = Mesh(mesh.devices.reshape(SIZES), NAMES)
    rows = P(NAMES, None)
    grad = P(("x", "zh", "y"), ("zl", "c"), None)
    return jax.shard_map(
        on_device,
        mesh=physical,
        in_specs=(rows, rows, P(), P(), P(), P()),
        out_specs=(grad, grad),
        check_vma=False,
    )
```
